32 devices in a mesh: len: 8 (over y, x, core), mem: 4 (over z).
Axes of the slice: x: 2, y: 2, z: 4, core: 2. Of those that a mesh axis runs over, the one named last changes fastest.
Arguments:
- phase_left: float32 [32, 1048576], P('mem', 'len'), may hold values from -3.140625 to 3.140625
- phase_right: float32 [32, 1048576], P('mem', 'len'), may hold values from -3.140625 to 3.140625
- roughness: float32 [32], P('mem'), may hold values from 0.1 to 10
- waviness: float32 [32], P('mem'), may hold values from 1.5 to 2.5
- coherence: float32 [32], P('mem'), may hold values from 32 to 512
Outputs:
- profile: float32 [2, 32, 1048576], P(None, 'mem', 'len')
- r_factor: float32 [32, 32], replicated
The draws below stay inside these ranges and needn't reach their ends.
All inputs are finite; a program needn't handle non-finite values.
Results may differ from the reference program's by a relative error of at most 0.0003.
Values sent between devices are 32-bit elements; how exact they have to be, the bound alone decides.
No kernel may reach another device: no remote copies, remote signals or barrier semaphores. Data moves between devices by JAX's collectives and lax.ppermute only.
A program may use at most 128 MiB of HBM per device.

```python
import math
import jax
import jax.numpy as jnp
from jax import lax

OUTER = 1024
INNER = 1024
MEMBERS = 32
ANCHOR = 64
POINTS = 1048576


def block_levels(key, shape, split, low, top_value):
    factor_of, own = 1.0, jax.random.fold_in(key, 6)
    for position, blocks in split:
        draws = jnp.exp(jax.random.uniform(jax.random.fold_in(own, position), (blocks,), jnp.float32, low / len(split), top_value / len(split)))
        factor_of = factor_of * jnp.repeat(draws, shape[position] // blocks).reshape([-1 if axis == position else 1 for axis in range(len(shape))])
    return factor_of


def setup_inputs(seed: int = 0) -> dict:
    splits = jax.random.split(jax.random.key(seed), 6)
    return {
        "phase_left": jnp.clip(jax.random.uniform(splits[0], (MEMBERS, POINTS), jnp.float32, -3.140625, 3.140625), -3.140625, 3.140625),
        "phase_right": jnp.clip(jax.random.uniform(splits[1], (MEMBERS, POINTS), jnp.float32, -3.140625, 3.140625), -3.140625, 3.140625),
        "roughness": jnp.clip(jnp.exp(math.log(10.0) - 4.6051702 * jax.random.uniform(splits[2], (MEMBERS,), jnp.float32) ** block_levels(splits[2], (MEMBERS,), ((0, 4),), -0.2, 0.2)), 0.1, 10.0),
        "waviness": jnp.clip(1.5 + 1.0 * jax.random.uniform(splits[3], (MEMBERS,), jnp.float32) ** block_levels(splits[3], (MEMBERS,), ((0, 4),), -0.2, 0.2), 1.5, 2.5),
        "coherence": jnp.clip(jnp.exp(math.log(512.0) - 2.7725887 * jax.random.uniform(splits[4], (MEMBERS,), jnp.float32) ** block_levels(splits[4], (MEMBERS,), ((0, 4),), -0.2, 0.2)), 32.0, 512.0),
    }


def spectra_of(phase_left, phase_right, roughness, waviness, coherence, freq):
    amplitude = jnp.sqrt(2.0 * roughness * (waviness - 1.0) / ANCHOR)[:, None] * ((freq + ANCHOR) / ANCHOR) ** (-0.5 * waviness[:, None])
    freq_ratio = freq / coherence[:, None]
    coherent = 1.0 / (1.0 + freq_ratio * freq_ratio)
    incoherent = freq_ratio * jnp.sqrt(2.0 + freq_ratio * freq_ratio) * coherent
    cos_left = jnp.cos(phase_left)
    sin_left = jnp.sin(phase_left)
    cos_right = jnp.cos(phase_right)
    sin_right = jnp.sin(phase_right)
    real_part = jnp.stack([amplitude * cos_left, amplitude * (coherent * cos_left + incoherent * cos_right)])
    imag_part = jnp.stack([amplitude * sin_left, amplitude * (coherent * sin_left + incoherent * sin_right)])
    return (real_part, imag_part)

def reference(phase_left, phase_right, roughness, waviness, coherence):
    point_count = OUTER * INNER
    freq = jnp.arange(point_count, dtype=jnp.float32)[None, :]
    real_part, imag_part = spectra_of(phase_left, phase_right, roughness, waviness, coherence, freq)
    spectrum = lax.complex(real_part, imag_part)
    profile = jnp.real(jnp.fft.ifft(spectrum, axis=-1)) * point_count
    profile = profile.astype(real_part.dtype)
    snapshot = jnp.transpose(profile, (0, 2, 1)).reshape(2 * point_count, MEMBERS) / jnp.sqrt(jnp.float32(2 * point_count))
    upper = jnp.linalg.qr(snapshot, mode='r')
    r_factor = upper * jnp.sign(jnp.diagonal(upper))[:, None]
    return (profile, r_factor)
```

```python
import functools
import math

import jax
import jax.numpy as jnp
import numpy as np
from jax import lax
from jax.experimental import pallas as pl
from jax.experimental.pallas import tpu as pltpu
from jax.sharding import PartitionSpec as P

OUTER = 1024
INNER = 1024
ANCHOR = 64
RADIX = 4
QUARTER = 256
LANES = 128
STEP = 16
WIDE = 256
BLOCK_ROWS = 16
IN_PARTS = 2
OUT_PARTS = 2
VMEM_LIMIT = 48 * 1024 * 1024
SIN_HALF = (0.49999999785787, -0.02083332246218, 2.604078316692e-4, -1.547581723527e-6, 5.088214043e-9)
COS_HALF = (
    0.99999999977982,
    -0.12499999839235,
    2.604164763023e-3,
    -2.170056380508e-5,
    9.67192778775e-8,
    -2.5440497557e-10,
)


highest = lax.Precision.HIGHEST


def merged(shard, axis, combine):
    everything = lax.all_gather(shard, axis)
    leading = everything[0]

    def step(k, so_far):
        return combine(so_far, everything[k])

    return lax.fori_loop(1, lax.axis_size(axis), step, leading)


def dft_tables(length):
    index = lax.iota(jnp.int32, length)
    product = index[:, None] * index[None, :] % length
    phase_angle = product.astype(jnp.float32) * (2.0 * math.pi / length)
    return (jnp.cos(phase_angle), jnp.sin(phase_angle))


def spectra_of(phase_left, phase_right, roughness, waviness, coherence, freq):
    amplitude = jnp.sqrt(2.0 * roughness * (waviness - 1.0) / ANCHOR)[:, None] * (
        (freq + ANCHOR) / ANCHOR
    ) ** (-0.5 * waviness[:, None])
    freq_ratio = freq / coherence[:, None]
    coherent = 1.0 / (1.0 + freq_ratio * freq_ratio)
    incoherent = freq_ratio * jnp.sqrt(2.0 + freq_ratio * freq_ratio) * coherent
    cos_left = jnp.cos(phase_left)
    sin_left = jnp.sin(phase_left)
    cos_right = jnp.cos(phase_right)
    sin_right = jnp.sin(phase_right)
    real_part = jnp.stack(
        [amplitude * cos_left, amplitude * (coherent * cos_left + incoherent * cos_right)]
    )
    imag_part = jnp.stack(
        [amplitude * sin_left, amplitude * (coherent * sin_left + incoherent * sin_right)]
    )
    return (real_part, imag_part)


def upper_of(gram_matrix):
    return jnp.linalg.cholesky(gram_matrix).T


def combine_factors(upper_a, upper_b):
    gram_matrix = jnp.dot(upper_a.T, upper_a, precision=highest) + jnp.dot(
        upper_b.T, upper_b, precision=highest
    )
    return upper_of(gram_matrix)


def gram_of(snapshot):
    return jnp.einsum("tmr,tnr->mn", snapshot, snapshot, precision=highest)


def per_device_spread(phase_left, phase_right, roughness, waviness, coherence):
    shards = lax.axis_size("len")
    my_index = lax.axis_index("len")
    local_members, local_len = phase_left.shape
    columns = 2 * local_members
    outer_block = OUTER // shards
    inner_block = INNER // shards

    def to_rows(part):
        shaped = part.reshape(2, local_members, inner_block, OUTER)
        return jnp.transpose(shaped, (2, 3, 0, 1)).reshape(
            inner_block, shards, outer_block * columns
        )

    inner_cos, inner_sin = dft_tables(INNER)
    freq = (my_index * local_len + lax.iota(jnp.int32, local_len)).astype(jnp.float32)[None, :]
    real_part, imag_part = spectra_of(phase_left, phase_right, roughness, waviness, coherence, freq)
    pieces = (
        lax.all_to_all(to_rows(real_part), "len", split_axis=1, concat_axis=0, tiled=True),
        lax.all_to_all(to_rows(imag_part), "len", split_axis=1, concat_axis=0, tiled=True),
    )
    real_in = pieces[0].reshape(INNER, -1)
    imag_in = pieces[1].reshape(INNER, -1)
    real_out = jnp.dot(inner_cos, real_in, precision=highest) - jnp.dot(
        inner_sin, imag_in, precision=highest
    )
    imag_out = jnp.dot(inner_cos, imag_in, precision=highest) + jnp.dot(
        inner_sin, real_in, precision=highest
    )
    row_index = lax.iota(jnp.int32, INNER)[:, None]
    outer_index = (my_index * outer_block + lax.iota(jnp.int32, outer_block))[None, :]
    twist = (row_index * outer_index % (OUTER * INNER)).astype(jnp.float32) * (
        2.0 * math.pi / (OUTER * INNER)
    )
    twist_cos = jnp.repeat(jnp.cos(twist), columns, axis=1)
    twist_sin = jnp.repeat(jnp.sin(twist), columns, axis=1)
    rot_real = (real_out * twist_cos - imag_out * twist_sin).reshape(
        shards, inner_block, outer_block * columns
    )
    rot_imag = (real_out * twist_sin + imag_out * twist_cos).reshape(
        shards, inner_block, outer_block * columns
    )
    outer_cos, outer_sin = dft_tables(OUTER)
    outer_cos = outer_cos.reshape(OUTER, shards, outer_block)
    outer_sin = outer_sin.reshape(OUTER, shards, outer_block)
    pieces = (
        lax.all_to_all(rot_real, "len", split_axis=0, concat_axis=0, tiled=True),
        lax.all_to_all(rot_imag, "len", split_axis=0, concat_axis=0, tiled=True),
    )
    item_count = pieces[0].shape[1]
    real_in = pieces[0].reshape(shards, item_count, outer_block, columns)
    imag_in = pieces[1].reshape(shards, item_count, outer_block, columns)
    first = jnp.einsum("jqa,qiac->cij", outer_cos, real_in, precision=highest)
    second = jnp.einsum("jqa,qiac->cij", outer_sin, imag_in, precision=highest)
    profile_block = first - second
    outgoing = jnp.transpose(
        profile_block.reshape(columns, inner_block, shards, outer_block), (2, 0, 1, 3)
    ).reshape(shards, -1)
    arrived = lax.all_to_all(outgoing, "len", split_axis=0, concat_axis=0, tiled=True)
    profile = jnp.transpose(
        arrived.reshape(shards, columns, inner_block, outer_block), (1, 3, 0, 2)
    ).reshape(2, local_members, local_len)
    scale = 1.0 / math.sqrt(2.0 * OUTER * INNER)
    snapshot = profile_block.reshape(2, local_members, inner_block * OUTER) * scale
    gathered = lax.all_gather(snapshot, "mem", axis=1, tiled=True)
    gram_local = gram_of(gathered)
    r_factor = merged(upper_of(gram_local), "len", combine_factors)
    return (profile, r_factor)


def host_cis(product, period):
    angle = product % period * (2.0 * np.pi / period)
    return np.cos(angle), np.sin(angle)


def split_host(table):
    coarse = table.astype(np.float32).astype(jnp.bfloat16)
    fine = (table - coarse.astype(np.float64)).astype(np.float32).astype(jnp.bfloat16)
    return np.stack([coarse, fine])


def outer_matrices():
    c, e, b = np.arange(QUARTER), np.arange(RADIX), np.arange(QUARTER)
    cos_part, sin_part = host_cis((RADIX * c[None, :, None] + e[:, None, None]) * b[None, None, :], OUTER)
    upper = np.concatenate([cos_part, -sin_part], axis=2)
    lower = np.concatenate([sin_part, cos_part], axis=2)
    return split_host(np.concatenate([upper, lower], axis=1))


def inner_matrices():
    c, e, b = np.arange(QUARTER), np.arange(RADIX), np.arange(QUARTER)
    cos_part, sin_part = host_cis((RADIX * c[None, :, None] + e[:, None, None]) * b[None, None, :], INNER)
    return split_host(np.concatenate([cos_part, -sin_part], axis=2))


def twist_tables():
    j1 = RADIX * np.arange(QUARTER)[None, :, None] + np.arange(RADIX)[:, None, None]
    cos_part, sin_part = host_cis(j1 * np.arange(INNER)[None, None, :], OUTER * INNER)
    return np.stack([cos_part, sin_part]).astype(np.float32)


def sin_cos(angle):
    square = angle * angle

    def series(coefficients):
        total = jnp.float32(coefficients[-1])
        for coefficient in coefficients[-2::-1]:
            total = total * square + jnp.float32(coefficient)
        return total

    half_sin = angle * series(SIN_HALF)
    half_cos = series(COS_HALF)
    twice = half_sin + half_sin
    return twice * half_cos, 1.0 - twice * half_sin


def line_spectra(left, right, freq, scale, exponent, inverse_coherence):
    amplitude = scale * jnp.exp2(exponent * jnp.log2((freq + ANCHOR) * (1.0 / ANCHOR)))
    freq_ratio = freq * inverse_coherence
    ratio_square = freq_ratio * freq_ratio
    coherent = 1.0 / (1.0 + ratio_square)
    incoherent = freq_ratio * jnp.sqrt(2.0 + ratio_square) * coherent
    sin_left, cos_left = sin_cos(left)
    sin_right, cos_right = sin_cos(right)
    independent = amplitude * incoherent
    first = (amplitude * cos_left, amplitude * sin_left)
    second = (
        coherent * first[0] + independent * cos_right,
        coherent * first[1] + independent * sin_right,
    )
    return first, second


def radix_four(parts):
    (r0, i0), (r1, i1), (r2, i2), (r3, i3) = parts
    even_sum, even_gap = (r0 + r2, i0 + i2), (r0 - r2, i0 - i2)
    odd_sum, odd_gap = (r1 + r3, i1 + i3), (r1 - r3, i1 - i3)
    return (
        (even_sum[0] + odd_sum[0], even_sum[1] + odd_sum[1]),
        (even_gap[0] - odd_gap[1], even_gap[1] + odd_gap[0]),
        (even_sum[0] - odd_sum[0], even_sum[1] - odd_sum[1]),
        (even_gap[0] + odd_gap[1], even_gap[1] - odd_gap[0]),
    )


def store_split(coarse_ref, fine_ref, where, value):
    coarse = value.astype(jnp.bfloat16)
    coarse_ref[where] = coarse
    fine_ref[where] = (value - coarse.astype(jnp.float32)).astype(jnp.bfloat16)


def triple_dot(matrix_ref, e, coarse, fine, dims):
    def product(a, b):
        return lax.dot_general(a, b, (dims, ((), ())), preferred_element_type=jnp.float32)

    return product(matrix_ref[0, e], coarse) + (
        product(matrix_ref[0, e], fine) + product(matrix_ref[1, e], coarse)
    )


def outer_kernel(base, params_ref, phase_ref, matrix_ref, twist_ref, out_ref, coarse_ref, fine_ref):
    scale, exponent, inverse_coherence = params_ref[0], params_ref[1], params_ref[2]
    rows = phase_ref.shape[3]
    first_lane = base + pl.program_id(0) * LANES
    lane = lax.broadcasted_iota(jnp.int32, (STEP, LANES), 1) + first_lane
    row = lax.broadcasted_iota(jnp.int32, (STEP, LANES), 0)
    place = row * INNER + lane

    def some_rows(step, carry):
        b = step * STEP
        tracks = []
        for a in range(RADIX):
            k1 = a * QUARTER + b
            source, inside = k1 // rows, pl.multiple_of(k1 % rows, STEP)
            freq = (place + k1 * INNER).astype(jnp.float32)
            left = phase_ref[source, 0, 0, pl.ds(inside, STEP), :]
            right = phase_ref[source, 1, 0, pl.ds(inside, STEP), :]
            tracks.append(line_spectra(left, right, freq, scale, exponent, inverse_coherence))
        for t in range(2):
            mixed = radix_four([track[t] for track in tracks])
            for e in range(RADIX):
                for ri in range(2):
                    at = pl.ds(pl.multiple_of(ri * QUARTER + b, STEP), STEP)
                    store_split(coarse_ref, fine_ref, (e, at, pl.ds(t * LANES, LANES)), mixed[e][ri])
        return carry

    lax.fori_loop(0, QUARTER // STEP, some_rows, 0)
    for e in range(RADIX):
        mid = triple_dot(matrix_ref, e, coarse_ref[e], fine_ref[e], ((1,), (0,)))
        cos_part, sin_part = twist_ref[0, e], twist_ref[1, e]
        for t in range(2):
            real = mid[:QUARTER, t * LANES : (t + 1) * LANES]
            imag = mid[QUARTER:, t * LANES : (t + 1) * LANES]
            out_ref[t, 0, pl.ds(e, QUARTER, stride=RADIX), :] = real * cos_part - imag * sin_part
            out_ref[t, 1, pl.ds(e, QUARTER, stride=RADIX), :] = real * sin_part + imag * cos_part


def inner_kernel(*refs):
    mid_refs, (matrix_ref, out_ref, coarse_ref, fine_ref) = refs[:-4], refs[-4:]
    wide, columns = mid_refs[0].shape[2:]
    shards, _, _, rows, _ = out_ref.shape

    def some_rows(step, carry):
        at = pl.multiple_of(step * STEP, STEP)
        for t in range(2):
            for half in range(0, QUARTER, 128):
                parts = [
                    tuple(
                        mid_refs[(a * QUARTER + half) // columns][
                            t, ri, pl.ds(at, STEP), pl.ds((a * QUARTER + half) % columns, 128)
                        ]
                        for ri in range(2)
                    )
                    for a in range(RADIX)
                ]
                mixed = radix_four(parts)
                for e in range(RADIX):
                    for ri in range(2):
                        where = (
                            e,
                            pl.ds(pl.multiple_of(t * wide + at, STEP), STEP),
                            pl.ds(ri * QUARTER + half, 128),
                        )
                        store_split(coarse_ref, fine_ref, where, mixed[e][ri])
        return carry

    lax.fori_loop(0, wide // STEP, some_rows, 0)
    some = rows // RADIX
    for e in range(RADIX):
        value = triple_dot(matrix_ref, e, coarse_ref[e], fine_ref[e], ((1,), (1,)))
        for t in range(2):
            for f in range(shards):
                for tile in range(wide // LANES):
                    lanes = t * wide + tile * LANES
                    out_ref[f, t, tile, pl.ds(e, some, stride=RADIX), :] = value[
                        f * some : (f + 1) * some, lanes : lanes + LANES
                    ]


def part_kernel(left_ref, right_ref, *out_refs):
    members, _, tiles, rows, _ = out_refs[0].shape
    flat_refs = [ref.reshape(members * 2 * tiles * rows, LANES) for ref in out_refs]
    for t, ref in enumerate((left_ref, right_ref)):
        for r in range(rows):
            for part, flat_ref in enumerate(flat_refs):
                for tile in range(tiles):
                    at = r * INNER + (part * tiles + tile) * LANES
                    start = (t * tiles + tile) * rows + r
                    flat_ref[pl.ds(start, members, stride=2 * tiles * rows), :] = ref[:, at : at + LANES]


def join_kernel(*refs):
    out_ref = refs[-1]
    members, _, tiles, rows, _ = refs[0].shape
    flat_refs = [ref.reshape(members * 2 * tiles * rows, LANES) for ref in refs[:-1]]
    for t in range(2):
        for r in range(rows):
            for part, flat_ref in enumerate(flat_refs):
                for tile in range(tiles):
                    at = r * INNER + (part * tiles + tile) * LANES
                    start = (t * tiles + tile) * rows + r
                    out_ref[t, :, at : at + LANES] = flat_ref[
                        pl.ds(start, members, stride=2 * tiles * rows), :
                    ]


def limits():
    return pltpu.CompilerParams(vmem_limit_bytes=VMEM_LIMIT)


def part_call(phase_left, phase_right, parts):
    members, length = phase_left.shape
    rows = length // INNER
    tiles = INNER // parts // LANES
    return pl.pallas_call(
        part_kernel,
        grid=(rows // BLOCK_ROWS,),
        in_specs=[pl.BlockSpec((members, BLOCK_ROWS * INNER), lambda g: (0, g))] * 2,
        out_specs=[pl.BlockSpec((members, 2, tiles, BLOCK_ROWS, LANES), lambda g: (0, 0, 0, g, 0))] * parts,
        out_shape=[jax.ShapeDtypeStruct((members, 2, tiles, rows, LANES), jnp.float32)] * parts,
        compiler_params=limits(),
        cost_estimate=pl.CostEstimate(flops=0, bytes_accessed=16 * members * length, transcendentals=0),
    )(phase_left, phase_right)


def join_call(pieces):
    members, _, tiles, rows, _ = pieces[0].shape
    return pl.pallas_call(
        join_kernel,
        grid=(rows // BLOCK_ROWS,),
        in_specs=[pl.BlockSpec((members, 2, tiles, BLOCK_ROWS, LANES), lambda g: (0, 0, 0, g, 0))]
        * len(pieces),
        out_specs=pl.BlockSpec((2, members, BLOCK_ROWS * INNER), lambda g: (0, 0, g)),
        out_shape=jax.ShapeDtypeStruct((2, members, rows * INNER), jnp.float32),
        compiler_params=limits(),
        cost_estimate=pl.CostEstimate(flops=0, bytes_accessed=16 * members * rows * INNER, transcendentals=0),
    )(*pieces)


def outer_call(params, phases, matrices, twists, part):
    sources, _, tiles, rows, _ = phases.shape
    columns = tiles * LANES
    return pl.pallas_call(
        functools.partial(outer_kernel, part * columns),
        grid=(columns // LANES,),
        in_specs=[
            pl.BlockSpec(memory_space=pltpu.SMEM),
            pl.BlockSpec((sources, 2, 1, rows, LANES), lambda g: (0, 0, g, 0, 0)),
            pl.BlockSpec(matrices.shape, lambda g: (0, 0, 0, 0)),
            pl.BlockSpec(
                (2, RADIX, QUARTER, LANES), lambda g: (0, 0, 0, part * (columns // LANES) + g)
            ),
        ],
        out_specs=pl.BlockSpec((2, 2, OUTER, LANES), lambda g: (0, 0, 0, g)),
        out_shape=jax.ShapeDtypeStruct((2, 2, OUTER, columns), jnp.float32),
        scratch_shapes=[pltpu.VMEM((RADIX, 2 * QUARTER, 2 * LANES), jnp.bfloat16)] * 2,
        compiler_params=limits(),
        cost_estimate=pl.CostEstimate(
            flops=48 * OUTER * QUARTER * columns, bytes_accessed=32 * OUTER * columns, transcendentals=0
        ),
    )(params, phases, matrices, twists)


def inner_call(mids, matrices, shards, part, parts):
    wide = WIDE
    rows = INNER // shards
    columns = OUTER // parts
    blocks = columns // wide

    return pl.pallas_call(
        inner_kernel,
        grid=(blocks,),
        in_specs=[
            pl.BlockSpec((2, 2, wide, mid.shape[-1]), lambda g: (0, 0, part * blocks + g, 0)) for mid in mids
        ]
        + [pl.BlockSpec(matrices.shape, lambda g: (0, 0, 0, 0))],
        out_specs=pl.BlockSpec((shards, 2, wide // LANES, rows, LANES), lambda g: (0, 0, g, 0, 0)),
        out_shape=jax.ShapeDtypeStruct((shards, 2, columns // LANES, rows, LANES), jnp.float32),
        scratch_shapes=[pltpu.VMEM((RADIX, 2 * wide, 2 * QUARTER), jnp.bfloat16)] * 2,
        compiler_params=limits(),
        cost_estimate=pl.CostEstimate(
            flops=24 * OUTER * QUARTER * columns, bytes_accessed=24 * OUTER * columns, transcendentals=0
        ),
    )(*mids, matrices)


def per_device_whole(phase_left, phase_right, roughness, waviness, coherence):
    local_members, local_len = phase_left.shape
    shards = lax.axis_size("len")
    my_index = lax.axis_index("len")
    points = OUTER * INNER

    def own(values):
        return lax.dynamic_index_in_dim(values, my_index, 0, keepdims=False)

    def swap(piece):
        return lax.all_to_all(piece, "len", split_axis=0, concat_axis=0, tiled=True)

    params = jnp.stack(
        [
            own(jnp.sqrt(2.0 * roughness * (waviness - 1.0) / ANCHOR)),
            own(-0.5 * waviness),
            own(1.0 / coherence),
        ]
    )
    outer_tables = jnp.asarray(outer_matrices())
    inner_tables = jnp.asarray(inner_matrices())
    twists = jnp.asarray(twist_tables())
    mids = [
        outer_call(params, swap(piece), outer_tables, twists, part)
        for part, piece in enumerate(part_call(phase_left, phase_right, IN_PARTS))
    ]
    pieces = [swap(inner_call(mids, inner_tables, shards, part, OUT_PARTS)) for part in range(OUT_PARTS)]
    profile = join_call(pieces)
    groups = lax.axis_size("mem")
    stretch = local_len // groups
    stretches = jnp.stack([profile[:, :, q * stretch : (q + 1) * stretch] for q in range(groups)])
    together = lax.all_to_all(stretches, "mem", split_axis=0, concat_axis=0, tiled=True)
    gram_matrix = sum(
        gram_of(together[:, t].reshape(1, groups * local_members, stretch)) for t in range(2)
    )
    gram_matrix = lax.psum(gram_matrix, ("len", "mem")) * (0.5 / points)
    return (profile, upper_of(gram_matrix))


def per_device(phase_left, phase_right, roughness, waviness, coherence):
    whole_members = phase_left.shape[0] == lax.axis_size("len")
    form = per_device_whole if whole_members else per_device_spread
    return form(phase_left, phase_right, roughness, waviness, coherence)


def solution(mesh):
    placed = (P("mem", "len"), P("mem", "len"), P("mem"), P("mem"), P("mem"))
    return jax.shard_map(
        per_device,
        mesh=mesh,
        in_specs=placed,
        out_specs=(P(None, "mem", "len"), P()),
        check_vma=False,
    )
```

```python
import functools
import math

import jax
import jax.numpy as jnp
import numpy as np
from jax import lax
from jax.experimental import pallas as pl
from jax.experimental.pallas import tpu as pltpu
from jax.sharding import PartitionSpec as P

OUTER = 1024
INNER = 1024
ANCHOR = 64
RADIX = 4
QUARTER = 256
LANES = 128
STEP = 16
WIDE = 256
BLOCK_ROWS = 16
IN_PARTS = 2
MIRROR_BLOCK = 2048
VMEM_LIMIT = 48 * 1024 * 1024
SIN_HALF = (0.49999999785787, -0.02083332246218, 2.604078316692e-4, -1.547581723527e-6, 5.088214043e-9)
COS_HALF = (
    0.99999999977982,
    -0.12499999839235,
    2.604164763023e-3,
    -2.170056380508e-5,
    9.67192778775e-8,
    -2.5440497557e-10,
)


highest = lax.Precision.HIGHEST


def merged(shard, axis, combine):
    everything = lax.all_gather(shard, axis)
    leading = everything[0]

    def step(k, so_far):
        return combine(so_far, everything[k])

    return lax.fori_loop(1, lax.axis_size(axis), step, leading)


def dft_tables(length):
    index = lax.iota(jnp.int32, length)
    product = index[:, None] * index[None, :] % length
    phase_angle = product.astype(jnp.float32) * (2.0 * math.pi / length)
    return (jnp.cos(phase_angle), jnp.sin(phase_angle))


def spectra_of(phase_left, phase_right, roughness, waviness, coherence, freq):
    amplitude = jnp.sqrt(2.0 * roughness * (waviness - 1.0) / ANCHOR)[:, None] * (
        (freq + ANCHOR) / ANCHOR
    ) ** (-0.5 * waviness[:, None])
    freq_ratio = freq / coherence[:, None]
    coherent = 1.0 / (1.0 + freq_ratio * freq_ratio)
    incoherent = freq_ratio * jnp.sqrt(2.0 + freq_ratio * freq_ratio) * coherent
    cos_left = jnp.cos(phase_left)
    sin_left = jnp.sin(phase_left)
    cos_right = jnp.cos(phase_right)
    sin_right = jnp.sin(phase_right)
    real_part = jnp.stack(
        [amplitude * cos_left, amplitude * (coherent * cos_left + incoherent * cos_right)]
    )
    imag_part = jnp.stack(
        [amplitude * sin_left, amplitude * (coherent * sin_left + incoherent * sin_right)]
    )
    return (real_part, imag_part)


def upper_of(gram_matrix):
    return jnp.linalg.cholesky(gram_matrix).T


def combine_factors(upper_a, upper_b):
    gram_matrix = jnp.dot(upper_a.T, upper_a, precision=highest) + jnp.dot(
        upper_b.T, upper_b, precision=highest
    )
    return upper_of(gram_matrix)


def gram_of(snapshot):
    return jnp.einsum("tmr,tnr->mn", snapshot, snapshot, precision=highest)


def per_device_spread(phase_left, phase_right, roughness, waviness, coherence):
    shards = lax.axis_size("len")
    my_index = lax.axis_index("len")
    local_members, local_len = phase_left.shape
    columns = 2 * local_members
    outer_block = OUTER // shards
    inner_block = INNER // shards

    def to_rows(part):
        shaped = part.reshape(2, local_members, inner_block, OUTER)
        return jnp.transpose(shaped, (2, 3, 0, 1)).reshape(
            inner_block, shards, outer_block * columns
        )

    inner_cos, inner_sin = dft_tables(INNER)
    freq = (my_index * local_len + lax.iota(jnp.int32, local_len)).astype(jnp.float32)[None, :]
    real_part, imag_part = spectra_of(phase_left, phase_right, roughness, waviness, coherence, freq)
    pieces = (
        lax.all_to_all(to_rows(real_part), "len", split_axis=1, concat_axis=0, tiled=True),
        lax.all_to_all(to_rows(imag_part), "len", split_axis=1, concat_axis=0, tiled=True),
    )
    real_in = pieces[0].reshape(INNER, -1)
    imag_in = pieces[1].reshape(INNER, -1)
    real_out = jnp.dot(inner_cos, real_in, precision=highest) - jnp.dot(
        inner_sin, imag_in, precision=highest
    )
    imag_out = jnp.dot(inner_cos, imag_in, precision=highest) + jnp.dot(
        inner_sin, real_in, precision=highest
    )
    row_index = lax.iota(jnp.int32, INNER)[:, None]
    outer_index = (my_index * outer_block + lax.iota(jnp.int32, outer_block))[None, :]
    twist = (row_index * outer_index % (OUTER * INNER)).astype(jnp.float32) * (
        2.0 * math.pi / (OUTER * INNER)
    )
    twist_cos = jnp.repeat(jnp.cos(twist), columns, axis=1)
    twist_sin = jnp.repeat(jnp.sin(twist), columns, axis=1)
    rot_real = (real_out * twist_cos - imag_out * twist_sin).reshape(
        shards, inner_block, outer_block * columns
    )
    rot_imag = (real_out * twist_sin + imag_out * twist_cos).reshape(
        shards, inner_block, outer_block * columns
    )
    outer_cos, outer_sin = dft_tables(OUTER)
    outer_cos = outer_cos.reshape(OUTER, shards, outer_block)
    outer_sin = outer_sin.reshape(OUTER, shards, outer_block)
    pieces = (
        lax.all_to_all(rot_real, "len", split_axis=0, concat_axis=0, tiled=True),
        lax.all_to_all(rot_imag, "len", split_axis=0, concat_axis=0, tiled=True),
    )
    item_count = pieces[0].shape[1]
    real_in = pieces[0].reshape(shards, item_count, outer_block, columns)
    imag_in = pieces[1].reshape(shards, item_count, outer_block, columns)
    first = jnp.einsum("jqa,qiac->cij", outer_cos, real_in, precision=highest)
    second = jnp.einsum("jqa,qiac->cij", outer_sin, imag_in, precision=highest)
    profile_block = first - second
    outgoing = jnp.transpose(
        profile_block.reshape(columns, inner_block, shards, outer_block), (2, 0, 1, 3)
    ).reshape(shards, -1)
    arrived = lax.all_to_all(outgoing, "len", split_axis=0, concat_axis=0, tiled=True)
    profile = jnp.transpose(
        arrived.reshape(shards, columns, inner_block, outer_block), (1, 3, 0, 2)
    ).reshape(2, local_members, local_len)
    scale = 1.0 / math.sqrt(2.0 * OUTER * INNER)
    snapshot = profile_block.reshape(2, local_members, inner_block * OUTER) * scale
    gathered = lax.all_gather(snapshot, "mem", axis=1, tiled=True)
    gram_local = gram_of(gathered)
    r_factor = merged(upper_of(gram_local), "len", combine_factors)
    return (profile, r_factor)


def host_cis(product, period):
    angle = product % period * (2.0 * np.pi / period)
    return np.cos(angle), np.sin(angle)


def split_host(table):
    coarse = table.astype(np.float32).astype(jnp.bfloat16)
    fine = (table - coarse.astype(np.float64)).astype(np.float32).astype(jnp.bfloat16)
    return np.stack([coarse, fine])


def outer_matrices():
    c, e, b = np.arange(QUARTER), np.arange(RADIX), np.arange(QUARTER)
    cos_part, sin_part = host_cis((RADIX * c[None, :, None] + e[:, None, None]) * b[None, None, :], OUTER)
    upper = np.concatenate([cos_part, -sin_part], axis=2)
    lower = np.concatenate([sin_part, cos_part], axis=2)
    return split_host(np.concatenate([upper, lower], axis=1))


def inner_matrices():
    c, e, b = np.arange(QUARTER), np.arange(RADIX), np.arange(QUARTER)
    cos_part, sin_part = host_cis((RADIX * c[None, :, None] + e[:, None, None]) * b[None, None, :], INNER)
    return split_host(np.concatenate([cos_part, -sin_part], axis=2))


def twist_tables():
    j1 = RADIX * np.arange(QUARTER)[None, :, None] + np.arange(RADIX)[:, None, None]
    cos_part, sin_part = host_cis(j1 * np.arange(INNER)[None, None, :], OUTER * INNER)
    return np.stack([cos_part, sin_part]).astype(np.float32)


def sin_cos(angle):
    square = angle * angle

    def series(coefficients):
        total = jnp.float32(coefficients[-1])
        for coefficient in coefficients[-2::-1]:
            total = total * square + jnp.float32(coefficient)
        return total

    half_sin = angle * series(SIN_HALF)
    half_cos = series(COS_HALF)
    twice = half_sin + half_sin
    return twice * half_cos, 1.0 - twice * half_sin


def line_spectra(left, right, freq, scale, exponent, inverse_coherence):
    amplitude = scale * jnp.exp2(exponent * jnp.log2((freq + ANCHOR) * (1.0 / ANCHOR)))
    freq_ratio = freq * inverse_coherence
    ratio_square = freq_ratio * freq_ratio
    coherent = 1.0 / (1.0 + ratio_square)
    incoherent = freq_ratio * jnp.sqrt(2.0 + ratio_square) * coherent
    sin_left, cos_left = sin_cos(left)
    sin_right, cos_right = sin_cos(right)
    independent = amplitude * incoherent
    first = (amplitude * cos_left, amplitude * sin_left)
    second = (
        coherent * first[0] + independent * cos_right,
        coherent * first[1] + independent * sin_right,
    )
    return first, second


def radix_four(parts):
    (r0, i0), (r1, i1), (r2, i2), (r3, i3) = parts
    even_sum, even_gap = (r0 + r2, i0 + i2), (r0 - r2, i0 - i2)
    odd_sum, odd_gap = (r1 + r3, i1 + i3), (r1 - r3, i1 - i3)
    return (
        (even_sum[0] + odd_sum[0], even_sum[1] + odd_sum[1]),
        (even_gap[0] - odd_gap[1], even_gap[1] + odd_gap[0]),
        (even_sum[0] - odd_sum[0], even_sum[1] - odd_sum[1]),
        (even_gap[0] + odd_gap[1], even_gap[1] - odd_gap[0]),
    )


def store_split(coarse_ref, fine_ref, where, value):
    coarse = value.astype(jnp.bfloat16)
    coarse_ref[where] = coarse
    fine_ref[where] = (value - coarse.astype(jnp.float32)).astype(jnp.bfloat16)


def triple_dot(matrix_ref, e, coarse, fine, dims):
    def product(a, b):
        return lax.dot_general(a, b, (dims, ((), ())), preferred_element_type=jnp.float32)

    return product(matrix_ref[0, e], coarse) + (
        product(matrix_ref[0, e], fine) + product(matrix_ref[1, e], coarse)
    )


def outer_kernel(base, params_ref, phase_ref, matrix_ref, twist_ref, out_ref, coarse_ref, fine_ref):
    scale, exponent, inverse_coherence = params_ref[0], params_ref[1], params_ref[2]
    rows = phase_ref.shape[3]
    first_lane = base + pl.program_id(0) * LANES
    lane = lax.broadcasted_iota(jnp.int32, (STEP, LANES), 1) + first_lane
    row = lax.broadcasted_iota(jnp.int32, (STEP, LANES), 0)
    place = row * INNER + lane

    def some_rows(step, carry):
        b = step * STEP
        tracks = []
        for a in range(RADIX):
            k1 = a * QUARTER + b
            source, inside = k1 // rows, pl.multiple_of(k1 % rows, STEP)
            freq = (place + k1 * INNER).astype(jnp.float32)
            left = phase_ref[source, 0, 0, pl.ds(inside, STEP), :]
            right = phase_ref[source, 1, 0, pl.ds(inside, STEP), :]
            tracks.append(line_spectra(left, right, freq, scale, exponent, inverse_coherence))
        for t in range(2):
            mixed = radix_four([track[t] for track in tracks])
            for e in range(RADIX):
                for ri in range(2):
                    at = pl.ds(pl.multiple_of(ri * QUARTER + b, STEP), STEP)
                    store_split(coarse_ref, fine_ref, (e, at, pl.ds(t * LANES, LANES)), mixed[e][ri])
        return carry

    lax.fori_loop(0, QUARTER // STEP, some_rows, 0)
    for e in range(RADIX):
        mid = triple_dot(matrix_ref, e, coarse_ref[e], fine_ref[e], ((1,), (0,)))
        cos_part, sin_part = twist_ref[0, e], twist_ref[1, e]
        for t in range(2):
            real = mid[:QUARTER, t * LANES : (t + 1) * LANES]
            imag = mid[QUARTER:, t * LANES : (t + 1) * LANES]
            out_ref[t, 0, pl.ds(e, QUARTER, stride=RADIX), :] = real * cos_part - imag * sin_part
            out_ref[t, 1, pl.ds(e, QUARTER, stride=RADIX), :] = real * sin_part + imag * cos_part


def inner_kernel(*refs):
    mid_refs, (matrix_ref, out_ref, coarse_ref, fine_ref) = refs[:-4], refs[-4:]
    wide, columns = mid_refs[0].shape[2:]
    shards, _, rows, _ = out_ref.shape

    def some_rows(step, carry):
        at = pl.multiple_of(step * STEP, STEP)
        for half in range(0, QUARTER, LANES):
            parts = [
                tuple(
                    mid_refs[(a * QUARTER + half) // columns][
                        0, ri, pl.ds(at, STEP), pl.ds((a * QUARTER + half) % columns, LANES)
                    ]
                    for ri in range(2)
                )
                for a in range(RADIX)
            ]
            mixed = radix_four(parts)
            for e in range(RADIX):
                for ri in range(2):
                    where = (e, pl.ds(at, STEP), pl.ds(ri * QUARTER + half, LANES))
                    store_split(coarse_ref, fine_ref, where, mixed[e][ri])
        return carry

    lax.fori_loop(0, wide // STEP, some_rows, 0)
    some = rows // RADIX
    for e in range(RADIX):
        value = triple_dot(matrix_ref, e, coarse_ref[e], fine_ref[e], ((1,), (1,)))
        for f in range(shards):
            for tile in range(wide // LANES):
                out_ref[f, tile, pl.ds(e, some, stride=RADIX), :] = value[
                    f * some : (f + 1) * some, tile * LANES : (tile + 1) * LANES
                ]


def part_kernel(part, left_ref, right_ref, out_ref):
    members, _, tiles, rows, _ = out_ref.shape
    flat_ref = out_ref.reshape(members * 2 * tiles * rows, LANES)
    for t, ref in enumerate((left_ref, right_ref)):
        for r in range(rows):
            for tile in range(tiles):
                at = r * INNER + (part * tiles + tile) * LANES
                start = (t * tiles + tile) * rows + r
                flat_ref[pl.ds(start, members, stride=2 * tiles * rows), :] = ref[:, at : at + LANES]


def join_kernel(*refs):
    in_ref, out_ref = refs[0], refs[-1]
    members, tiles, rows, _ = in_ref.shape
    flat_ref = in_ref.reshape(members * tiles * rows, LANES)
    for r in range(rows):
        for tile in range(tiles):
            at = r * INNER + tile * LANES
            out_ref[0, :, at : at + LANES] = flat_ref[pl.ds(tile * rows + r, members, stride=tiles * rows), :]


def mirror_kernel(base_ref, params_ref, *refs):
    slots = (len(refs) - 2) // 2
    own_refs, far_refs, (out_ref, last_ref) = refs[:slots], refs[slots : 2 * slots], refs[2 * slots :]
    _, members, block = own_refs[0].shape
    tiles = block // LANES
    first = pl.program_id(0) * block
    shape = (2 * members, LANES)
    lane = lax.broadcasted_iota(jnp.int32, shape, 1)
    mirror = (LANES - lane) % LANES

    @pl.when(pl.program_id(0) == 0)
    def _():
        last_ref[...] = jnp.zeros_like(last_ref)

    def one_tile(tile, carry):
        at = pl.ds(pl.multiple_of(tile * LANES, LANES), LANES)
        far_at = pl.ds(pl.multiple_of((tiles - 1 - tile) * LANES, LANES), LANES)
        offset = first + tile * LANES + lane
        freq = (base_ref[0] + offset).astype(jnp.float32)
        far_freq = (OUTER * INNER - base_ref[0] - offset).astype(jnp.float32)
        inner = offset > 0
        for pair in range(slots // 2):
            rows = slice(2 * members * pair, 2 * members * (pair + 1))
            own, far = [], []
            for t in range(2):
                own.append(
                    jnp.concatenate([own_refs[2 * pair][t, :, at], own_refs[2 * pair + 1][t, :, at]], axis=0)
                )
                ahead = jnp.concatenate(
                    [far_refs[2 * pair][t, :, far_at], far_refs[2 * pair + 1][t, :, far_at]], axis=0
                )
                turned = jnp.take_along_axis(ahead, mirror, axis=1, mode="promise_in_bounds")
                far.append(jnp.where(lane == 0, last_ref[pair, t], turned))
                last_ref[pair, t] = turned
            scale, exponent, inverse_coherence = (params_ref[n, rows, :] for n in range(3))
            near_lines = line_spectra(*own, freq, scale, exponent, inverse_coherence)
            far_lines = line_spectra(*far, far_freq, scale, exponent, inverse_coherence)
            for t in range(2):
                real = near_lines[t][0] + far_lines[t][0]
                imag = near_lines[t][1] - far_lines[t][1]
                out_ref[t, 0, rows, at] = jnp.where(inner, real, 0.0)
                out_ref[t, 1, rows, at] = jnp.where(inner, imag, 0.0)
        return carry

    lax.fori_loop(0, tiles, one_tile, 0)


def limits():
    return pltpu.CompilerParams(vmem_limit_bytes=VMEM_LIMIT)


def part_call(phase_left, phase_right, part, parts):
    members, length = phase_left.shape
    rows = length // INNER
    tiles = INNER // parts // LANES
    return pl.pallas_call(
        functools.partial(part_kernel, part),
        grid=(rows // BLOCK_ROWS,),
        in_specs=[pl.BlockSpec((members, BLOCK_ROWS * INNER), lambda g: (0, g))] * 2,
        out_specs=pl.BlockSpec((members, 2, tiles, BLOCK_ROWS, LANES), lambda g: (0, 0, 0, g, 0)),
        out_shape=jax.ShapeDtypeStruct((members, 2, tiles, rows, LANES), jnp.float32),
        compiler_params=limits(),
        cost_estimate=pl.CostEstimate(flops=0, bytes_accessed=16 * members * length, transcendentals=0),
    )(phase_left, phase_right)


def join_call(piece, track, so_far):
    members, tiles, rows, _ = piece.shape
    operands = (piece,) if so_far is None else (piece, so_far)
    return pl.pallas_call(
        join_kernel,
        grid=(rows // BLOCK_ROWS,),
        in_specs=[
            pl.BlockSpec((members, tiles, BLOCK_ROWS, LANES), lambda g: (0, 0, g, 0)),
            pl.BlockSpec(memory_space=pl.ANY),
        ][: len(operands)],
        out_specs=pl.BlockSpec((1, members, BLOCK_ROWS * INNER), lambda g: (track, 0, g)),
        out_shape=jax.ShapeDtypeStruct((2, members, rows * INNER), jnp.float32),
        input_output_aliases={} if so_far is None else {1: 0},
        compiler_params=limits(),
        cost_estimate=pl.CostEstimate(flops=0, bytes_accessed=8 * members * rows * INNER, transcendentals=0),
    )(*operands)


def mirror_call(base, params, own, far):
    _, members, width = own[0].shape
    slots = len(own)
    block = min(width, MIRROR_BLOCK)
    blocks = width // block
    return pl.pallas_call(
        mirror_kernel,
        grid=(blocks,),
        in_specs=[pl.BlockSpec(memory_space=pltpu.SMEM), pl.BlockSpec(params.shape, lambda g: (0, 0, 0))]
        + [pl.BlockSpec((2, members, block), lambda g: (0, 0, g))] * slots
        + [pl.BlockSpec((2, members, block), lambda g: (0, 0, blocks - 1 - g))] * slots,
        out_specs=pl.BlockSpec((2, 2, slots * members, block), lambda g: (0, 0, 0, g)),
        out_shape=jax.ShapeDtypeStruct((2, 2, slots * members, width), jnp.float32),
        scratch_shapes=[pltpu.VMEM((slots // 2, 2, 2 * members, LANES), jnp.float32)],
        compiler_params=limits(),
        cost_estimate=pl.CostEstimate(
            flops=400 * slots * members * width, bytes_accessed=32 * slots * members * width, transcendentals=0
        ),
    )(base, params, *own, *far)


def outer_call(params, phases, matrices, twists, part):
    sources, _, tiles, rows, _ = phases.shape
    columns = tiles * LANES
    return pl.pallas_call(
        functools.partial(outer_kernel, part * columns),
        grid=(columns // LANES,),
        in_specs=[
            pl.BlockSpec(memory_space=pltpu.SMEM),
            pl.BlockSpec((sources, 2, 1, rows, LANES), lambda g: (0, 0, g, 0, 0)),
            pl.BlockSpec(matrices.shape, lambda g: (0, 0, 0, 0)),
            pl.BlockSpec(
                (2, RADIX, QUARTER, LANES), lambda g: (0, 0, 0, part * (columns // LANES) + g)
            ),
        ],
        out_specs=pl.BlockSpec((2, 2, OUTER, LANES), lambda g: (0, 0, 0, g)),
        out_shape=jax.ShapeDtypeStruct((2, 2, OUTER, columns), jnp.float32),
        scratch_shapes=[pltpu.VMEM((RADIX, 2 * QUARTER, 2 * LANES), jnp.bfloat16)] * 2,
        compiler_params=limits(),
        cost_estimate=pl.CostEstimate(
            flops=48 * OUTER * QUARTER * columns, bytes_accessed=32 * OUTER * columns, transcendentals=0
        ),
    )(params, phases, matrices, twists)


def inner_call(mids, matrices, shards, track):
    rows = INNER // shards
    return pl.pallas_call(
        inner_kernel,
        grid=(OUTER // WIDE,),
        in_specs=[pl.BlockSpec((1, 2, WIDE, mid.shape[-1]), lambda g: (track, 0, g, 0)) for mid in mids]
        + [pl.BlockSpec(matrices.shape, lambda g: (0, 0, 0, 0))],
        out_specs=pl.BlockSpec((shards, WIDE // LANES, rows, LANES), lambda g: (0, g, 0, 0)),
        out_shape=jax.ShapeDtypeStruct((shards, OUTER // LANES, rows, LANES), jnp.float32),
        scratch_shapes=[pltpu.VMEM((RADIX, WIDE, 2 * QUARTER), jnp.bfloat16)] * 2,
        compiler_params=limits(),
        cost_estimate=pl.CostEstimate(
            flops=12 * OUTER * QUARTER * INNER, bytes_accessed=12 * OUTER * INNER, transcendentals=0
        ),
    )(*mids, matrices)


def line_params(roughness, waviness, coherence):
    return jnp.stack(
        [jnp.sqrt(2.0 * roughness * (waviness - 1.0) / ANCHOR), -0.5 * waviness, 1.0 / coherence]
    )


def exchange_lines(phase_left, phase_right):
    shards, groups = lax.axis_size("len"), lax.axis_size("mem")
    my_group = lax.axis_index("mem")
    half = phase_left.shape[1] // 2
    width = half // groups

    def lines(start):
        return jnp.stack(
            [lax.dynamic_slice_in_dim(phase, start, width, 1) for phase in (phase_left, phase_right)]
        )

    def to_group(piece, slot):
        return lax.ppermute(piece, "mem", [(z, z ^ slot) for z in range(groups)]) if slot else piece

    far = [
        to_group(lines(half + (groups - 1 - (my_group ^ slot)) * width), slot) for slot in range(groups)
    ]
    own = [to_group(lines((my_group ^ slot) * width), slot) for slot in range(groups)]
    far = [lax.ppermute(piece, "len", [(d, shards - 1 - d) for d in range(shards)]) for piece in far]
    return own, far


def edge_lines(phase_left, phase_right, params):
    shards, groups = lax.axis_size("len"), lax.axis_size("mem")
    members, local_len = phase_left.shape
    edges = 2 * groups
    width = local_len // edges
    columns = [phase[:, n * width : n * width + 1] for phase in (phase_left, phase_right) for n in range(edges)]
    everything = lax.all_gather(jnp.concatenate(columns + [params.T], axis=1), ("len", "mem"))
    everything = everything.reshape(shards, groups, members, 2 * edges + 3)
    all_params = everything[0, :, :, 2 * edges :]
    phases = [
        jnp.transpose(everything[..., n * edges : (n + 1) * edges], (1, 2, 0, 3)).reshape(
            groups * members, shards * edges
        )
        for n in range(2)
    ]
    return phases, all_params, width


def edge_gram(phases, all_params, width):
    freq = (width * lax.iota(jnp.int32, phases[0].shape[1])).astype(jnp.float32)[None, :]
    flat = all_params.reshape(-1, 3)
    lines = line_spectra(*phases, freq, *(flat[:, n : n + 1] for n in range(3)))

    def mirrored(value):
        return jnp.roll(jnp.flip(value, axis=1), 1, axis=1)

    both = jnp.stack(
        [line[0] + mirrored(line[0]) for line in lines] + [line[1] - mirrored(line[1]) for line in lines]
    )
    return gram_of(both)


def gram_by_lines(phase_left, phase_right, roughness, waviness, coherence):
    shards, groups = lax.axis_size("len"), lax.axis_size("mem")
    my_index, my_group = lax.axis_index("len"), lax.axis_index("mem")
    members, local_len = phase_left.shape
    own, far = exchange_lines(phase_left, phase_right)
    phases, all_params, width = edge_lines(
        phase_left, phase_right, line_params(roughness, waviness, coherence)
    )
    slot_params = jnp.concatenate(
        [lax.dynamic_index_in_dim(all_params, my_group ^ slot, 0, keepdims=False) for slot in range(groups)]
    )
    slot_params = jnp.broadcast_to(slot_params.T[:, :, None], (3, groups * members, LANES))
    base = (my_index * local_len + my_group * width).astype(jnp.int32).reshape(1)
    sums = mirror_call(base, slot_params, own, far)
    slot_gram = sum(gram_of(sums[t]) for t in range(2))
    row = lax.broadcasted_iota(jnp.int32, slot_gram.shape, 0)
    column = lax.broadcasted_iota(jnp.int32, slot_gram.shape, 1)
    to_slot = (row % members == column % members) & ((row // members) ^ my_group == column // members)
    to_slot = to_slot.astype(jnp.float32)
    own_gram = jnp.dot(jnp.dot(to_slot, slot_gram, precision=highest), to_slot.T, precision=highest)
    inner_gram = jnp.sum(lax.all_gather(own_gram, ("len", "mem")), axis=0)
    return 0.25 * inner_gram + 0.125 * edge_gram(phases, all_params, width)


def per_device_whole(phase_left, phase_right, roughness, waviness, coherence):
    shards = lax.axis_size("len")
    my_index = lax.axis_index("len")

    def swap(piece):
        return lax.all_to_all(piece, "len", split_axis=0, concat_axis=0, tiled=True)

    params = lax.dynamic_index_in_dim(
        line_params(roughness, waviness, coherence), my_index, 1, keepdims=False
    )
    outer_tables = jnp.asarray(outer_matrices())
    inner_tables = jnp.asarray(inner_matrices())
    twists = jnp.asarray(twist_tables())
    gram_matrix = gram_by_lines(phase_left, phase_right, roughness, waviness, coherence)
    mids = []
    for part in range(IN_PARTS):
        piece = swap(part_call(phase_left, phase_right, part, IN_PARTS))
        mids.append(outer_call(params, piece, outer_tables, twists, part))
    profile = None
    for track in range(2):
        profile = join_call(swap(inner_call(mids, inner_tables, shards, track)), track, profile)
    return (profile, upper_of(gram_matrix))


def per_device(phase_left, phase_right, roughness, waviness, coherence):
    whole_members = phase_left.shape[0] == lax.axis_size("len") and lax.axis_size("mem") in (2, 4)
    form = per_device_whole if whole_members else per_device_spread
    return form(phase_left, phase_right, roughness, waviness, coherence)


def solution(mesh):
    placed = (P("mem", "len"), P("mem", "len"), P("mem"), P("mem"), P("mem"))
    return jax.shard_map(
        per_device,
        mesh=mesh,
        in_specs=placed,
        out_specs=(P(None, "mem", "len"), P()),
        check_vma=False,
    )
```

```python
import functools
import math

import jax
import jax.numpy as jnp
import numpy as np
from jax import lax
from jax.experimental import pallas as pl
from jax.experimental.pallas import tpu as pltpu
from jax.sharding import PartitionSpec as P

OUTER = 1024
INNER = 1024
ANCHOR = 64
RADIX = 4
QUARTER = 256
LANES = 128
STEP = 16
WIDE = 256
BLOCK_ROWS = 16
OUTER_TILES = 2
OUT_PARTS = 2
VMEM_LIMIT = 48 * 1024 * 1024
SIN_HALF = (0.49999999785787, -0.02083332246218, 2.604078316692e-4, -1.547581723527e-6, 5.088214043e-9)
COS_HALF = (
    0.99999999977982,
    -0.12499999839235,
    2.604164763023e-3,
    -2.170056380508e-5,
    9.67192778775e-8,
    -2.5440497557e-10,
)


highest = lax.Precision.HIGHEST


def merged(shard, axis, combine):
    everything = lax.all_gather(shard, axis)
    leading = everything[0]

    def step(k, so_far):
        return combine(so_far, everything[k])

    return lax.fori_loop(1, lax.axis_size(axis), step, leading)


def dft_tables(length):
    index = lax.iota(jnp.int32, length)
    product = index[:, None] * index[None, :] % length
    phase_angle = product.astype(jnp.float32) * (2.0 * math.pi / length)
    return (jnp.cos(phase_angle), jnp.sin(phase_angle))


def spectra_of(phase_left, phase_right, roughness, waviness, coherence, freq):
    amplitude = jnp.sqrt(2.0 * roughness * (waviness - 1.0) / ANCHOR)[:, None] * (
        (freq + ANCHOR) / ANCHOR
    ) ** (-0.5 * waviness[:, None])
    freq_ratio = freq / coherence[:, None]
    coherent = 1.0 / (1.0 + freq_ratio * freq_ratio)
    incoherent = freq_ratio * jnp.sqrt(2.0 + freq_ratio * freq_ratio) * coherent
    cos_left = jnp.cos(phase_left)
    sin_left = jnp.sin(phase_left)
    cos_right = jnp.cos(phase_right)
    sin_right = jnp.sin(phase_right)
    real_part = jnp.stack(
        [amplitude * cos_left, amplitude * (coherent * cos_left + incoherent * cos_right)]
    )
    imag_part = jnp.stack(
        [amplitude * sin_left, amplitude * (coherent * sin_left + incoherent * sin_right)]
    )
    return (real_part, imag_part)


def upper_of(gram_matrix):
    return jnp.linalg.cholesky(gram_matrix).T


def combine_factors(upper_a, upper_b):
    gram_matrix = jnp.dot(upper_a.T, upper_a, precision=highest) + jnp.dot(
        upper_b.T, upper_b, precision=highest
    )
    return upper_of(gram_matrix)


def gram_of(snapshot):
    return jnp.einsum("tmr,tnr->mn", snapshot, snapshot, precision=highest)


def per_device_spread(phase_left, phase_right, roughness, waviness, coherence):
    shards = lax.axis_size("len")
    my_index = lax.axis_index("len")
    local_members, local_len = phase_left.shape
    columns = 2 * local_members
    outer_block = OUTER // shards
    inner_block = INNER // shards

    def to_rows(part):
        shaped = part.reshape(2, local_members, inner_block, OUTER)
        return jnp.transpose(shaped, (2, 3, 0, 1)).reshape(
            inner_block, shards, outer_block * columns
        )

    inner_cos, inner_sin = dft_tables(INNER)
    freq = (my_index * local_len + lax.iota(jnp.int32, local_len)).astype(jnp.float32)[None, :]
    real_part, imag_part = spectra_of(phase_left, phase_right, roughness, waviness, coherence, freq)
    pieces = (
        lax.all_to_all(to_rows(real_part), "len", split_axis=1, concat_axis=0, tiled=True),
        lax.all_to_all(to_rows(imag_part), "len", split_axis=1, concat_axis=0, tiled=True),
    )
    real_in = pieces[0].reshape(INNER, -1)
    imag_in = pieces[1].reshape(INNER, -1)
    real_out = jnp.dot(inner_cos, real_in, precision=highest) - jnp.dot(
        inner_sin, imag_in, precision=highest
    )
    imag_out = jnp.dot(inner_cos, imag_in, precision=highest) + jnp.dot(
        inner_sin, real_in, precision=highest
    )
    row_index = lax.iota(jnp.int32, INNER)[:, None]
    outer_index = (my_index * outer_block + lax.iota(jnp.int32, outer_block))[None, :]
    twist = (row_index * outer_index % (OUTER * INNER)).astype(jnp.float32) * (
        2.0 * math.pi / (OUTER * INNER)
    )
    twist_cos = jnp.repeat(jnp.cos(twist), columns, axis=1)
    twist_sin = jnp.repeat(jnp.sin(twist), columns, axis=1)
    rot_real = (real_out * twist_cos - imag_out * twist_sin).reshape(
        shards, inner_block, outer_block * columns
    )
    rot_imag = (real_out * twist_sin + imag_out * twist_cos).reshape(
        shards, inner_block, outer_block * columns
    )
    outer_cos, outer_sin = dft_tables(OUTER)
    outer_cos = outer_cos.reshape(OUTER, shards, outer_block)
    outer_sin = outer_sin.reshape(OUTER, shards, outer_block)
    pieces = (
        lax.all_to_all(rot_real, "len", split_axis=0, concat_axis=0, tiled=True),
        lax.all_to_all(rot_imag, "len", split_axis=0, concat_axis=0, tiled=True),
    )
    item_count = pieces[0].shape[1]
    real_in = pieces[0].reshape(shards, item_count, outer_block, columns)
    imag_in = pieces[1].reshape(shards, item_count, outer_block, columns)
    first = jnp.einsum("jqa,qiac->cij", outer_cos, real_in, precision=highest)
    second = jnp.einsum("jqa,qiac->cij", outer_sin, imag_in, precision=highest)
    profile_block = first - second
    outgoing = jnp.transpose(
        profile_block.reshape(columns, inner_block, shards, outer_block), (2, 0, 1, 3)
    ).reshape(shards, -1)
    arrived = lax.all_to_all(outgoing, "len", split_axis=0, concat_axis=0, tiled=True)
    profile = jnp.transpose(
        arrived.reshape(shards, columns, inner_block, outer_block), (1, 3, 0, 2)
    ).reshape(2, local_members, local_len)
    scale = 1.0 / math.sqrt(2.0 * OUTER * INNER)
    snapshot = profile_block.reshape(2, local_members, inner_block * OUTER) * scale
    gathered = lax.all_gather(snapshot, "mem", axis=1, tiled=True)
    gram_local = gram_of(gathered)
    r_factor = merged(upper_of(gram_local), "len", combine_factors)
    return (profile, r_factor)


def host_cis(product, period):
    angle = product % period * (2.0 * np.pi / period)
    return np.cos(angle), np.sin(angle)


def split_host(table):
    coarse = table.astype(np.float32).astype(jnp.bfloat16)
    fine = (table - coarse.astype(np.float64)).astype(np.float32).astype(jnp.bfloat16)
    return np.stack([coarse, fine])


def outer_matrices():
    c, e, b = np.arange(QUARTER), np.arange(RADIX), np.arange(QUARTER)
    cos_part, sin_part = host_cis((RADIX * c[None, :, None] + e[:, None, None]) * b[None, None, :], OUTER)
    upper = np.concatenate([cos_part, -sin_part], axis=2)
    lower = np.concatenate([sin_part, cos_part], axis=2)
    return split_host(np.concatenate([upper, lower], axis=1))


def inner_matrices():
    c, e, b = np.arange(QUARTER), np.arange(RADIX), np.arange(QUARTER)
    cos_part, sin_part = host_cis((RADIX * c[None, :, None] + e[:, None, None]) * b[None, None, :], INNER)
    return split_host(np.concatenate([cos_part, -sin_part], axis=2))


def twist_tables():
    j1 = RADIX * np.arange(QUARTER)[None, :, None] + np.arange(RADIX)[:, None, None]
    cos_part, sin_part = host_cis(j1 * np.arange(INNER)[None, None, :], OUTER * INNER)
    return np.stack([cos_part, sin_part]).astype(np.float32)


def sin_cos(angle):
    square = angle * angle

    def series(coefficients):
        total = jnp.float32(coefficients[-1])
        for coefficient in coefficients[-2::-1]:
            total = total * square + jnp.float32(coefficient)
        return total

    half_sin = angle * series(SIN_HALF)
    half_cos = series(COS_HALF)
    twice = half_sin + half_sin
    return twice * half_cos, 1.0 - twice * half_sin


def left_lines(left, freq, scale, exponent):
    amplitude = scale * jnp.exp2(exponent * jnp.log2((freq + ANCHOR) * (1.0 / ANCHOR)))
    sin_left, cos_left = sin_cos(left)
    return amplitude * cos_left, amplitude * sin_left


def line_spectra(left, right, freq, scale, exponent, inverse_coherence):
    amplitude = scale * jnp.exp2(exponent * jnp.log2((freq + ANCHOR) * (1.0 / ANCHOR)))
    freq_ratio = freq * inverse_coherence
    ratio_square = freq_ratio * freq_ratio
    coherent = 1.0 / (1.0 + ratio_square)
    incoherent = freq_ratio * jnp.sqrt(2.0 + ratio_square) * coherent
    sin_left, cos_left = sin_cos(left)
    sin_right, cos_right = sin_cos(right)
    independent = amplitude * incoherent
    first = (amplitude * cos_left, amplitude * sin_left)
    second = (
        coherent * first[0] + independent * cos_right,
        coherent * first[1] + independent * sin_right,
    )
    return first, second


def radix_four(parts):
    (r0, i0), (r1, i1), (r2, i2), (r3, i3) = parts
    even_sum, even_gap = (r0 + r2, i0 + i2), (r0 - r2, i0 - i2)
    odd_sum, odd_gap = (r1 + r3, i1 + i3), (r1 - r3, i1 - i3)
    return (
        (even_sum[0] + odd_sum[0], even_sum[1] + odd_sum[1]),
        (even_gap[0] - odd_gap[1], even_gap[1] + odd_gap[0]),
        (even_sum[0] - odd_sum[0], even_sum[1] - odd_sum[1]),
        (even_gap[0] + odd_gap[1], even_gap[1] - odd_gap[0]),
    )


def store_split(coarse_ref, fine_ref, where, value):
    coarse = value.astype(jnp.bfloat16)
    coarse_ref[where] = coarse
    fine_ref[where] = (value - coarse.astype(jnp.float32)).astype(jnp.bfloat16)


def triple_dot(matrix_ref, e, coarse, fine, dims):
    def product(a, b):
        return lax.dot_general(a, b, (dims, ((), ())), preferred_element_type=jnp.float32)

    return product(matrix_ref[0, e], coarse) + (
        product(matrix_ref[0, e], fine) + product(matrix_ref[1, e], coarse)
    )


def outer_kernel(track, params_ref, *refs):
    phase_refs, (matrix_ref, twist_ref, out_ref, coarse_ref, fine_ref) = refs[:-5], refs[-5:]
    scale, exponent, inverse_coherence = params_ref[0], params_ref[1], params_ref[2]
    _, tiles, rows, _ = phase_refs[0].shape
    lane = lax.broadcasted_iota(jnp.int32, (STEP, LANES), 1) + pl.program_id(0) * tiles * LANES
    row = lax.broadcasted_iota(jnp.int32, (STEP, LANES), 0)
    place = row * INNER + lane

    def some_rows(step, carry):
        b = step * STEP
        for tile in range(tiles):
            lines = []
            for a in range(RADIX):
                k1 = a * QUARTER + b
                source, inside = k1 // rows, pl.multiple_of(k1 % rows, STEP)
                freq = (place + (k1 * INNER + tile * LANES)).astype(jnp.float32)
                phases = [ref[source, tile, pl.ds(inside, STEP), :] for ref in phase_refs]
                if track == 0:
                    lines.append(left_lines(*phases, freq, scale, exponent))
                else:
                    lines.append(line_spectra(*phases, freq, scale, exponent, inverse_coherence)[1])
            mixed = radix_four(lines)
            for e in range(RADIX):
                for ri in range(2):
                    at = pl.ds(pl.multiple_of(ri * QUARTER + b, STEP), STEP)
                    where = (e, at, pl.ds(tile * LANES, LANES))
                    store_split(coarse_ref, fine_ref, where, mixed[e][ri])
        return carry

    lax.fori_loop(0, QUARTER // STEP, some_rows, 0)
    for e in range(RADIX):
        mid = triple_dot(matrix_ref, e, coarse_ref[e], fine_ref[e], ((1,), (0,)))
        for tile in range(tiles):
            lanes = slice(tile * LANES, (tile + 1) * LANES)
            cos_part, sin_part = twist_ref[0, e, :, lanes], twist_ref[1, e, :, lanes]
            real, imag = mid[:QUARTER, lanes], mid[QUARTER:, lanes]
            out_ref[tile, 0, pl.ds(e, QUARTER, stride=RADIX), :] = real * cos_part - imag * sin_part
            out_ref[tile, 1, pl.ds(e, QUARTER, stride=RADIX), :] = real * sin_part + imag * cos_part


def inner_kernel(mid_ref, matrix_ref, *refs):
    out_refs, (coarse_ref, fine_ref) = refs[:-2], refs[-2:]
    wide = mid_ref.shape[2]
    shards, _, rows, _ = out_refs[0].shape

    def some_rows(step, carry):
        at = pl.multiple_of(step * STEP, STEP)
        for half in range(0, QUARTER, LANES):
            parts = [
                tuple(mid_ref[(a * QUARTER + half) // LANES, ri, pl.ds(at, STEP), :] for ri in range(2))
                for a in range(RADIX)
            ]
            mixed = radix_four(parts)
            for e in range(RADIX):
                for ri in range(2):
                    where = (e, pl.ds(at, STEP), pl.ds(ri * QUARTER + half, LANES))
                    store_split(coarse_ref, fine_ref, where, mixed[e][ri])
        return carry

    lax.fori_loop(0, wide // STEP, some_rows, 0)
    some = rows // RADIX
    for e in range(RADIX):
        value = triple_dot(matrix_ref, e, coarse_ref[e], fine_ref[e], ((1,), (1,)))
        for f in range(shards):
            for part, out_ref in enumerate(out_refs):
                at = (f * len(out_refs) + part) * some
                for tile in range(wide // LANES):
                    out_ref[f, tile, pl.ds(e, some, stride=RADIX), :] = value[
                        at : at + some, tile * LANES : (tile + 1) * LANES
                    ]


def part_kernel(in_ref, out_ref):
    members, tiles, rows, _ = out_ref.shape
    flat_ref = out_ref.reshape(members * tiles * rows, LANES)
    for r in range(rows):
        for tile in range(tiles):
            at = (r * tiles + tile) * LANES
            flat_ref[pl.ds(tile * rows + r, members, stride=tiles * rows), :] = in_ref[:, at : at + LANES]


def join_kernel(*refs):
    in_ref, out_ref, copy_ref = refs[0], refs[-2], refs[-1]
    members, tiles, rows, _ = in_ref.shape
    flat_ref = in_ref.reshape(members * tiles * rows, LANES)
    for r in range(rows):
        for tile in range(tiles):
            at = (r * tiles + tile) * LANES
            value = flat_ref[pl.ds(tile * rows + r, members, stride=tiles * rows), :]
            out_ref[0, :, at : at + LANES] = value
            copy_ref[0, :, at : at + LANES] = value


def limits():
    return pltpu.CompilerParams(vmem_limit_bytes=VMEM_LIMIT)


def part_call(phase):
    members, length = phase.shape
    rows = length // INNER
    tiles = INNER // LANES
    return pl.pallas_call(
        part_kernel,
        grid=(rows // BLOCK_ROWS,),
        in_specs=[pl.BlockSpec((members, BLOCK_ROWS * INNER), lambda g: (0, g))],
        out_specs=pl.BlockSpec((members, tiles, BLOCK_ROWS, LANES), lambda g: (0, 0, g, 0)),
        out_shape=jax.ShapeDtypeStruct((members, tiles, rows, LANES), jnp.float32),
        compiler_params=limits(),
        cost_estimate=pl.CostEstimate(flops=0, bytes_accessed=8 * members * length, transcendentals=0),
    )(phase)


def join_call(piece, place, places, groups, so_far):
    members, tiles, rows, _ = piece.shape
    stretch = rows * INNER
    steps = rows // BLOCK_ROWS
    track, within = place // (places // 2), place % (places // 2)
    operands = (piece,) if so_far is None else (piece, so_far)
    each = steps // groups
    return pl.pallas_call(
        join_kernel,
        grid=(steps,),
        in_specs=[
            pl.BlockSpec((members, tiles, BLOCK_ROWS, LANES), lambda g: (0, 0, g, 0)),
            pl.BlockSpec(memory_space=pl.ANY),
        ][: len(operands)],
        out_specs=[
            pl.BlockSpec((1, members, BLOCK_ROWS * INNER), lambda g: (track, 0, within * steps + g)),
            pl.BlockSpec((1, members, BLOCK_ROWS * INNER), lambda g: (g // each, 0, g % each)),
        ],
        out_shape=[
            jax.ShapeDtypeStruct((2, members, stretch * places // 2), jnp.float32),
            jax.ShapeDtypeStruct((groups, members, stretch // groups), jnp.float32),
        ],
        input_output_aliases={} if so_far is None else {1: 0},
        compiler_params=limits(),
        cost_estimate=pl.CostEstimate(flops=0, bytes_accessed=12 * members * stretch, transcendentals=0),
    )(*operands)


def outer_call(params, phases, matrices, twists, track):
    sources, tiles, rows, _ = phases[0].shape
    some = OUTER_TILES
    return pl.pallas_call(
        functools.partial(outer_kernel, track),
        grid=(tiles // some,),
        in_specs=[pl.BlockSpec(memory_space=pltpu.SMEM)]
        + [pl.BlockSpec((sources, some, rows, LANES), lambda g: (0, g, 0, 0))] * len(phases)
        + [
            pl.BlockSpec(matrices.shape, lambda g: (0, 0, 0, 0)),
            pl.BlockSpec((2, RADIX, QUARTER, some * LANES), lambda g: (0, 0, 0, g)),
        ],
        out_specs=pl.BlockSpec((some, 2, OUTER, LANES), lambda g: (g, 0, 0, 0)),
        out_shape=jax.ShapeDtypeStruct((tiles, 2, OUTER, LANES), jnp.float32),
        scratch_shapes=[pltpu.VMEM((RADIX, 2 * QUARTER, some * LANES), jnp.bfloat16)] * 2,
        compiler_params=limits(),
        cost_estimate=pl.CostEstimate(
            flops=24 * OUTER * QUARTER * INNER, bytes_accessed=20 * OUTER * INNER, transcendentals=0
        ),
    )(params, *phases, matrices, twists)


def inner_call(mid, matrices, shards, parts):
    rows = INNER // shards // parts
    tiles = OUTER // LANES
    return pl.pallas_call(
        inner_kernel,
        grid=(OUTER // WIDE,),
        in_specs=[
            pl.BlockSpec((INNER // LANES, 2, WIDE, LANES), lambda g: (0, 0, g, 0)),
            pl.BlockSpec(matrices.shape, lambda g: (0, 0, 0, 0)),
        ],
        out_specs=[pl.BlockSpec((shards, WIDE // LANES, rows, LANES), lambda g: (0, g, 0, 0))] * parts,
        out_shape=[jax.ShapeDtypeStruct((shards, tiles, rows, LANES), jnp.float32)] * parts,
        scratch_shapes=[pltpu.VMEM((RADIX, WIDE, 2 * QUARTER), jnp.bfloat16)] * 2,
        compiler_params=limits(),
        cost_estimate=pl.CostEstimate(
            flops=12 * OUTER * QUARTER * INNER, bytes_accessed=12 * OUTER * INNER, transcendentals=0
        ),
    )(mid, matrices)


def line_params(roughness, waviness, coherence):
    return jnp.stack(
        [jnp.sqrt(2.0 * roughness * (waviness - 1.0) / ANCHOR), -0.5 * waviness, 1.0 / coherence]
    )


def slot_gram(stretches, groups):
    my_group = lax.axis_index("mem")
    received = []
    for slot in range(groups):
        piece = lax.dynamic_index_in_dim(stretches, my_group ^ slot, 0, keepdims=False)
        if slot:
            piece = lax.ppermute(piece, "mem", [(z, z ^ slot) for z in range(groups)])
        received.append(piece)
    together = jnp.concatenate(received, axis=0)
    return lax.dot_general(together, together, (((1,), (1,)), ((), ())), precision=highest)


def in_order(gram_matrix, members):
    my_group = lax.axis_index("mem")
    row = lax.broadcasted_iota(jnp.int32, gram_matrix.shape, 0)
    column = lax.broadcasted_iota(jnp.int32, gram_matrix.shape, 1)
    to_slot = (row % members == column % members) & ((row // members) ^ my_group == column // members)
    to_slot = to_slot.astype(jnp.float32)
    return jnp.dot(jnp.dot(to_slot, gram_matrix, precision=highest), to_slot.T, precision=highest)


def summed(value):
    for axis in ("len", "mem"):
        value = jnp.sum(lax.all_gather(value, axis), axis=0)
    return value


def per_device_whole(phase_left, phase_right, roughness, waviness, coherence):
    shards, groups = lax.axis_size("len"), lax.axis_size("mem")
    my_index = lax.axis_index("len")
    members = phase_left.shape[0]

    def swap(piece):
        return lax.all_to_all(piece, "len", split_axis=0, concat_axis=0, tiled=True)

    params = lax.dynamic_index_in_dim(
        line_params(roughness, waviness, coherence), my_index, 1, keepdims=False
    )
    outer_tables = jnp.asarray(outer_matrices())
    inner_tables = jnp.asarray(inner_matrices())
    twists = jnp.asarray(twist_tables())
    left = swap(part_call(phase_left))
    right = swap(part_call(phase_right))
    profile, gram_matrix, place = None, 0.0, 0
    for track, phases in enumerate(((left,), (left, right))):
        mid = outer_call(params, phases, outer_tables, twists, track)
        for piece in inner_call(mid, inner_tables, shards, OUT_PARTS):
            profile, stretches = join_call(swap(piece), place, 2 * OUT_PARTS, groups, profile)
            gram_matrix = gram_matrix + slot_gram(stretches, groups)
            place += 1
    gram_matrix = summed(in_order(gram_matrix, members)) * (0.5 / (OUTER * INNER))
    return (profile, upper_of(gram_matrix))


def per_device(phase_left, phase_right, roughness, waviness, coherence):
    whole_members = phase_left.shape[0] == lax.axis_size("len") and lax.axis_size("mem") in (2, 4)
    form = per_device_whole if whole_members else per_device_spread
    return form(phase_left, phase_right, roughness, waviness, coherence)


def solution(mesh):
    placed = (P("mem", "len"), P("mem", "len"), P("mem"), P("mem"), P("mem"))
    return jax.shard_map(
        per_device,
        mesh=mesh,
        in_specs=placed,
        out_specs=(P(None, "mem", "len"), P()),
        check_vma=False,
    )
```

```python
import functools
import math

import jax
import jax.numpy as jnp
import numpy as np
from jax import lax
from jax.experimental import pallas as pl
from jax.experimental.pallas import tpu as pltpu
from jax.sharding import PartitionSpec as P

OUTER = 1024
INNER = 1024
ANCHOR = 64
RADIX = 4
QUARTER = 256
LANES = 128
STEP = 16
WIDE = 256
BLOCK_ROWS = 16
OUTER_TILES = 2
VMEM_LIMIT = 48 * 1024 * 1024
SIN_HALF = (0.49999999785787, -0.02083332246218, 2.604078316692e-4, -1.547581723527e-6, 5.088214043e-9)
COS_HALF = (
    0.99999999977982,
    -0.12499999839235,
    2.604164763023e-3,
    -2.170056380508e-5,
    9.67192778775e-8,
    -2.5440497557e-10,
)


highest = lax.Precision.HIGHEST


def merged(shard, axis, combine):
    everything = lax.all_gather(shard, axis)
    leading = everything[0]

    def step(k, so_far):
        return combine(so_far, everything[k])

    return lax.fori_loop(1, lax.axis_size(axis), step, leading)


def dft_tables(length):
    index = lax.iota(jnp.int32, length)
    product = index[:, None] * index[None, :] % length
    phase_angle = product.astype(jnp.float32) * (2.0 * math.pi / length)
    return (jnp.cos(phase_angle), jnp.sin(phase_angle))


def spectra_of(phase_left, phase_right, roughness, waviness, coherence, freq):
    amplitude = jnp.sqrt(2.0 * roughness * (waviness - 1.0) / ANCHOR)[:, None] * (
        (freq + ANCHOR) / ANCHOR
    ) ** (-0.5 * waviness[:, None])
    freq_ratio = freq / coherence[:, None]
    coherent = 1.0 / (1.0 + freq_ratio * freq_ratio)
    incoherent = freq_ratio * jnp.sqrt(2.0 + freq_ratio * freq_ratio) * coherent
    cos_left = jnp.cos(phase_left)
    sin_left = jnp.sin(phase_left)
    cos_right = jnp.cos(phase_right)
    sin_right = jnp.sin(phase_right)
    real_part = jnp.stack(
        [amplitude * cos_left, amplitude * (coherent * cos_left + incoherent * cos_right)]
    )
    imag_part = jnp.stack(
        [amplitude * sin_left, amplitude * (coherent * sin_left + incoherent * sin_right)]
    )
    return (real_part, imag_part)


def upper_of(gram_matrix):
    return jnp.linalg.cholesky(gram_matrix).T


def combine_factors(upper_a, upper_b):
    gram_matrix = jnp.dot(upper_a.T, upper_a, precision=highest) + jnp.dot(
        upper_b.T, upper_b, precision=highest
    )
    return upper_of(gram_matrix)


def gram_of(snapshot):
    return jnp.einsum("tmr,tnr->mn", snapshot, snapshot, precision=highest)


def per_device_spread(phase_left, phase_right, roughness, waviness, coherence):
    shards = lax.axis_size("len")
    my_index = lax.axis_index("len")
    local_members, local_len = phase_left.shape
    columns = 2 * local_members
    outer_block = OUTER // shards
    inner_block = INNER // shards

    def to_rows(part):
        shaped = part.reshape(2, local_members, inner_block, OUTER)
        return jnp.transpose(shaped, (2, 3, 0, 1)).reshape(
            inner_block, shards, outer_block * columns
        )

    inner_cos, inner_sin = dft_tables(INNER)
    freq = (my_index * local_len + lax.iota(jnp.int32, local_len)).astype(jnp.float32)[None, :]
    real_part, imag_part = spectra_of(phase_left, phase_right, roughness, waviness, coherence, freq)
    pieces = (
        lax.all_to_all(to_rows(real_part), "len", split_axis=1, concat_axis=0, tiled=True),
        lax.all_to_all(to_rows(imag_part), "len", split_axis=1, concat_axis=0, tiled=True),
    )
    real_in = pieces[0].reshape(INNER, -1)
    imag_in = pieces[1].reshape(INNER, -1)
    real_out = jnp.dot(inner_cos, real_in, precision=highest) - jnp.dot(
        inner_sin, imag_in, precision=highest
    )
    imag_out = jnp.dot(inner_cos, imag_in, precision=highest) + jnp.dot(
        inner_sin, real_in, precision=highest
    )
    row_index = lax.iota(jnp.int32, INNER)[:, None]
    outer_index = (my_index * outer_block + lax.iota(jnp.int32, outer_block))[None, :]
    twist = (row_index * outer_index % (OUTER * INNER)).astype(jnp.float32) * (
        2.0 * math.pi / (OUTER * INNER)
    )
    twist_cos = jnp.repeat(jnp.cos(twist), columns, axis=1)
    twist_sin = jnp.repeat(jnp.sin(twist), columns, axis=1)
    rot_real = (real_out * twist_cos - imag_out * twist_sin).reshape(
        shards, inner_block, outer_block * columns
    )
    rot_imag = (real_out * twist_sin + imag_out * twist_cos).reshape(
        shards, inner_block, outer_block * columns
    )
    outer_cos, outer_sin = dft_tables(OUTER)
    outer_cos = outer_cos.reshape(OUTER, shards, outer_block)
    outer_sin = outer_sin.reshape(OUTER, shards, outer_block)
    pieces = (
        lax.all_to_all(rot_real, "len", split_axis=0, concat_axis=0, tiled=True),
        lax.all_to_all(rot_imag, "len", split_axis=0, concat_axis=0, tiled=True),
    )
    item_count = pieces[0].shape[1]
    real_in = pieces[0].reshape(shards, item_count, outer_block, columns)
    imag_in = pieces[1].reshape(shards, item_count, outer_block, columns)
    first = jnp.einsum("jqa,qiac->cij", outer_cos, real_in, precision=highest)
    second = jnp.einsum("jqa,qiac->cij", outer_sin, imag_in, precision=highest)
    profile_block = first - second
    outgoing = jnp.transpose(
        profile_block.reshape(columns, inner_block, shards, outer_block), (2, 0, 1, 3)
    ).reshape(shards, -1)
    arrived = lax.all_to_all(outgoing, "len", split_axis=0, concat_axis=0, tiled=True)
    profile = jnp.transpose(
        arrived.reshape(shards, columns, inner_block, outer_block), (1, 3, 0, 2)
    ).reshape(2, local_members, local_len)
    scale = 1.0 / math.sqrt(2.0 * OUTER * INNER)
    snapshot = profile_block.reshape(2, local_members, inner_block * OUTER) * scale
    gathered = lax.all_gather(snapshot, "mem", axis=1, tiled=True)
    gram_local = gram_of(gathered)
    r_factor = merged(upper_of(gram_local), "len", combine_factors)
    return (profile, r_factor)


def host_cis(product, period):
    angle = product % period * (2.0 * np.pi / period)
    return np.cos(angle), np.sin(angle)


def split_host(table):
    coarse = table.astype(np.float32).astype(jnp.bfloat16)
    fine = (table - coarse.astype(np.float64)).astype(np.float32).astype(jnp.bfloat16)
    return np.stack([coarse, fine])


def outer_matrices():
    c, e, b = np.arange(QUARTER), np.arange(RADIX), np.arange(QUARTER)
    cos_part, sin_part = host_cis((RADIX * c[None, :, None] + e[:, None, None]) * b[None, None, :], OUTER)
    upper = np.concatenate([cos_part, -sin_part], axis=2)
    lower = np.concatenate([sin_part, cos_part], axis=2)
    return split_host(np.concatenate([upper, lower], axis=1))


def inner_matrices():
    c, e, b = np.arange(QUARTER), np.arange(RADIX), np.arange(QUARTER)
    cos_part, sin_part = host_cis((RADIX * c[None, :, None] + e[:, None, None]) * b[None, None, :], INNER)
    return split_host(np.concatenate([cos_part, -sin_part], axis=2))


def twist_tables():
    j1 = RADIX * np.arange(QUARTER)[None, :, None] + np.arange(RADIX)[:, None, None]
    cos_part, sin_part = host_cis(j1 * np.arange(INNER)[None, None, :], OUTER * INNER)
    return np.stack([cos_part, sin_part]).astype(np.float32)


def sin_cos(angle):
    square = angle * angle

    def series(coefficients):
        total = jnp.float32(coefficients[-1])
        for coefficient in coefficients[-2::-1]:
            total = total * square + jnp.float32(coefficient)
        return total

    half_sin = angle * series(SIN_HALF)
    half_cos = series(COS_HALF)
    twice = half_sin + half_sin
    return twice * half_cos, 1.0 - twice * half_sin


def left_lines(left, freq, scale, exponent):
    amplitude = scale * jnp.exp2(exponent * jnp.log2((freq + ANCHOR) * (1.0 / ANCHOR)))
    sin_left, cos_left = sin_cos(left)
    return amplitude * cos_left, amplitude * sin_left


def line_spectra(left, right, freq, scale, exponent, inverse_coherence):
    amplitude = scale * jnp.exp2(exponent * jnp.log2((freq + ANCHOR) * (1.0 / ANCHOR)))
    freq_ratio = freq * inverse_coherence
    ratio_square = freq_ratio * freq_ratio
    coherent = 1.0 / (1.0 + ratio_square)
    incoherent = freq_ratio * jnp.sqrt(2.0 + ratio_square) * coherent
    sin_left, cos_left = sin_cos(left)
    sin_right, cos_right = sin_cos(right)
    independent = amplitude * incoherent
    first = (amplitude * cos_left, amplitude * sin_left)
    second = (
        coherent * first[0] + independent * cos_right,
        coherent * first[1] + independent * sin_right,
    )
    return first, second


def radix_four(parts):
    (r0, i0), (r1, i1), (r2, i2), (r3, i3) = parts
    even_sum, even_gap = (r0 + r2, i0 + i2), (r0 - r2, i0 - i2)
    odd_sum, odd_gap = (r1 + r3, i1 + i3), (r1 - r3, i1 - i3)
    return (
        (even_sum[0] + odd_sum[0], even_sum[1] + odd_sum[1]),
        (even_gap[0] - odd_gap[1], even_gap[1] + odd_gap[0]),
        (even_sum[0] - odd_sum[0], even_sum[1] - odd_sum[1]),
        (even_gap[0] + odd_gap[1], even_gap[1] - odd_gap[0]),
    )


def store_split(coarse_ref, fine_ref, where, value):
    coarse = value.astype(jnp.bfloat16)
    coarse_ref[where] = coarse
    fine_ref[where] = (value - coarse.astype(jnp.float32)).astype(jnp.bfloat16)


def triple_dot(matrix_ref, e, coarse, fine, dims):
    def product(a, b):
        return lax.dot_general(a, b, (dims, ((), ())), preferred_element_type=jnp.float32)

    return product(matrix_ref[0, e], coarse) + (
        product(matrix_ref[0, e], fine) + product(matrix_ref[1, e], coarse)
    )


def outer_kernel(track, params_ref, *refs):
    phase_refs, (matrix_ref, twist_ref, out_ref, coarse_ref, fine_ref) = refs[:-5], refs[-5:]
    scale, exponent, inverse_coherence = params_ref[0], params_ref[1], params_ref[2]
    _, tiles, rows, _ = phase_refs[0].shape
    lane = lax.broadcasted_iota(jnp.int32, (STEP, LANES), 1) + pl.program_id(0) * tiles * LANES
    row = lax.broadcasted_iota(jnp.int32, (STEP, LANES), 0)
    place = row * INNER + lane

    def some_rows(step, carry):
        b = step * STEP
        for tile in range(tiles):
            lines = []
            for a in range(RADIX):
                k1 = a * QUARTER + b
                source, inside = k1 // rows, pl.multiple_of(k1 % rows, STEP)
                freq = (place + (k1 * INNER + tile * LANES)).astype(jnp.float32)
                phases = [ref[source, tile, pl.ds(inside, STEP), :] for ref in phase_refs]
                if track == 0:
                    lines.append(left_lines(*phases, freq, scale, exponent))
                else:
                    lines.append(line_spectra(*phases, freq, scale, exponent, inverse_coherence)[1])
            mixed = radix_four(lines)
            for e in range(RADIX):
                for ri in range(2):
                    at = pl.ds(pl.multiple_of(ri * QUARTER + b, STEP), STEP)
                    where = (e, at, pl.ds(tile * LANES, LANES))
                    store_split(coarse_ref, fine_ref, where, mixed[e][ri])
        return carry

    lax.fori_loop(0, QUARTER // STEP, some_rows, 0)
    for e in range(RADIX):
        mid = triple_dot(matrix_ref, e, coarse_ref[e], fine_ref[e], ((1,), (0,)))
        for tile in range(tiles):
            lanes = slice(tile * LANES, (tile + 1) * LANES)
            cos_part, sin_part = twist_ref[0, e, :, lanes], twist_ref[1, e, :, lanes]
            real, imag = mid[:QUARTER, lanes], mid[QUARTER:, lanes]
            out_ref[tile, 0, pl.ds(e, QUARTER, stride=RADIX), :] = real * cos_part - imag * sin_part
            out_ref[tile, 1, pl.ds(e, QUARTER, stride=RADIX), :] = real * sin_part + imag * cos_part


def inner_kernel(mid_ref, matrix_ref, *refs):
    out_refs, (coarse_ref, fine_ref) = refs[:-2], refs[-2:]
    wide = mid_ref.shape[2]
    shards, _, rows, _ = out_refs[0].shape

    def some_rows(step, carry):
        at = pl.multiple_of(step * STEP, STEP)
        for half in range(0, QUARTER, LANES):
            parts = [
                tuple(mid_ref[(a * QUARTER + half) // LANES, ri, pl.ds(at, STEP), :] for ri in range(2))
                for a in range(RADIX)
            ]
            mixed = radix_four(parts)
            for e in range(RADIX):
                for ri in range(2):
                    where = (e, pl.ds(at, STEP), pl.ds(ri * QUARTER + half, LANES))
                    store_split(coarse_ref, fine_ref, where, mixed[e][ri])
        return carry

    lax.fori_loop(0, wide // STEP, some_rows, 0)
    some = rows // RADIX
    for e in range(RADIX):
        value = triple_dot(matrix_ref, e, coarse_ref[e], fine_ref[e], ((1,), (1,)))
        for f in range(shards):
            for part, out_ref in enumerate(out_refs):
                at = (f * len(out_refs) + part) * some
                for tile in range(wide // LANES):
                    out_ref[f, tile, pl.ds(e, some, stride=RADIX), :] = value[
                        at : at + some, tile * LANES : (tile + 1) * LANES
                    ]


def part_kernel(in_ref, out_ref):
    members, tiles, rows, _ = out_ref.shape
    flat_ref = out_ref.reshape(members * tiles * rows, LANES)
    for r in range(rows):
        for tile in range(tiles):
            at = (r * tiles + tile) * LANES
            flat_ref[pl.ds(tile * rows + r, members, stride=tiles * rows), :] = in_ref[:, at : at + LANES]


def join_kernel(*refs):
    in_ref, out_ref, copy_ref = refs[0], refs[-2], refs[-1]
    members, tiles, rows, _ = in_ref.shape
    flat_ref = in_ref.reshape(members * tiles * rows, LANES)
    for r in range(rows):
        for tile in range(tiles):
            at = (r * tiles + tile) * LANES
            value = flat_ref[pl.ds(tile * rows + r, members, stride=tiles * rows), :]
            out_ref[0, :, at : at + LANES] = value
            copy_ref[0, :, at : at + LANES] = value


def mirror_kernel(base_ref, own_ref, far_ref, edge_ref, out_ref):
    members, length = own_ref.shape
    tiles = length // LANES - 1
    shape = (members, LANES)
    lane = lax.broadcasted_iota(jnp.int32, shape, 1)
    mirror = (LANES - lane) % LANES
    first_group, last_group = base_ref[1] == 0, base_ref[1] == base_ref[2] - 1
    beyond = own_ref[:, tiles * LANES :]
    scale = jnp.broadcast_to(beyond[:, 1:2], shape)
    exponent = jnp.broadcast_to(beyond[:, 2:3], shape)
    half_root = math.sqrt(0.5)

    def tile_of(ref, tile):
        return ref[:, pl.ds(pl.multiple_of(tile * LANES, LANES), LANES)]

    def turned(value):
        return jnp.take_along_axis(value, mirror, axis=1, mode="promise_in_bounds")

    def store(tile, own, far, weight):
        offset = base_ref[0] + tile * LANES + lane
        near = left_lines(own, offset.astype(jnp.float32), scale, exponent)
        far_offset = jnp.where(offset == 0, 0, OUTER * INNER - offset)
        back = left_lines(far, far_offset.astype(jnp.float32), scale, exponent)
        at = pl.ds(pl.multiple_of(tile * LANES, LANES), LANES)
        out_ref[0, :, at] = (near[0] + back[0]) * weight
        out_ref[1, :, at] = (near[1] - back[1]) * weight

    def one_tile(tile, last):
        ahead = turned(tile_of(far_ref, tiles - 1 - tile))
        is_edge = (lane == 0) & (tile == 0) & first_group
        store(tile, tile_of(own_ref, tile), jnp.where(lane == 0, last, ahead), jnp.where(is_edge, half_root, 1.0))
        return ahead

    start = jnp.where(first_group, turned(edge_ref[...]), turned(tile_of(far_ref, tiles)))
    last = lax.fori_loop(0, tiles, one_tile, start)
    lone = (lane == 0) & last_group
    store(tiles, jnp.where(lone, beyond, 0.0), jnp.where(lone, last, 0.0), jnp.where(lone, half_root, 0.0))


def limits():
    return pltpu.CompilerParams(vmem_limit_bytes=VMEM_LIMIT)


def part_call(phase):
    members, length = phase.shape
    rows = length // INNER
    tiles = INNER // LANES
    return pl.pallas_call(
        part_kernel,
        grid=(rows // BLOCK_ROWS,),
        in_specs=[pl.BlockSpec((members, BLOCK_ROWS * INNER), lambda g: (0, g))],
        out_specs=pl.BlockSpec((members, tiles, BLOCK_ROWS, LANES), lambda g: (0, 0, g, 0)),
        out_shape=jax.ShapeDtypeStruct((members, tiles, rows, LANES), jnp.float32),
        compiler_params=limits(),
        cost_estimate=pl.CostEstimate(flops=0, bytes_accessed=8 * members * length, transcendentals=0),
    )(phase)


def join_call(piece, place, places, groups, so_far):
    members, tiles, rows, _ = piece.shape
    stretch = rows * INNER
    steps = rows // BLOCK_ROWS
    track, within = place // (places // 2), place % (places // 2)
    operands = (piece,) if so_far is None else (piece, so_far)
    each = steps // groups
    return pl.pallas_call(
        join_kernel,
        grid=(steps,),
        in_specs=[
            pl.BlockSpec((members, tiles, BLOCK_ROWS, LANES), lambda g: (0, 0, g, 0)),
            pl.BlockSpec(memory_space=pl.ANY),
        ][: len(operands)],
        out_specs=[
            pl.BlockSpec((1, members, BLOCK_ROWS * INNER), lambda g: (track, 0, within * steps + g)),
            pl.BlockSpec((1, members, BLOCK_ROWS * INNER), lambda g: (g // each, 0, g % each)),
        ],
        out_shape=[
            jax.ShapeDtypeStruct((2, members, stretch * places // 2), jnp.float32),
            jax.ShapeDtypeStruct((groups, members, stretch // groups), jnp.float32),
        ],
        input_output_aliases={} if so_far is None else {1: 0},
        compiler_params=limits(),
        cost_estimate=pl.CostEstimate(flops=0, bytes_accessed=12 * members * stretch, transcendentals=0),
    )(*operands)


def outer_call(params, phases, matrices, twists, track):
    sources, tiles, rows, _ = phases[0].shape
    some = OUTER_TILES
    return pl.pallas_call(
        functools.partial(outer_kernel, track),
        grid=(tiles // some,),
        in_specs=[pl.BlockSpec(memory_space=pltpu.SMEM)]
        + [pl.BlockSpec((sources, some, rows, LANES), lambda g: (0, g, 0, 0))] * len(phases)
        + [
            pl.BlockSpec(matrices.shape, lambda g: (0, 0, 0, 0)),
            pl.BlockSpec((2, RADIX, QUARTER, some * LANES), lambda g: (0, 0, 0, g)),
        ],
        out_specs=pl.BlockSpec((some, 2, OUTER, LANES), lambda g: (g, 0, 0, 0)),
        out_shape=jax.ShapeDtypeStruct((tiles, 2, OUTER, LANES), jnp.float32),
        scratch_shapes=[pltpu.VMEM((RADIX, 2 * QUARTER, some * LANES), jnp.bfloat16)] * 2,
        compiler_params=limits(),
        cost_estimate=pl.CostEstimate(
            flops=24 * OUTER * QUARTER * INNER, bytes_accessed=20 * OUTER * INNER, transcendentals=0
        ),
    )(params, *phases, matrices, twists)


def inner_call(mid, matrices, shards, parts):
    rows = INNER // shards // parts
    tiles = OUTER // LANES
    return pl.pallas_call(
        inner_kernel,
        grid=(OUTER // WIDE,),
        in_specs=[
            pl.BlockSpec((INNER // LANES, 2, WIDE, LANES), lambda g: (0, 0, g, 0)),
            pl.BlockSpec(matrices.shape, lambda g: (0, 0, 0, 0)),
        ],
        out_specs=[pl.BlockSpec((shards, WIDE // LANES, rows, LANES), lambda g: (0, g, 0, 0))] * parts,
        out_shape=[jax.ShapeDtypeStruct((shards, tiles, rows, LANES), jnp.float32)] * parts,
        scratch_shapes=[pltpu.VMEM((RADIX, WIDE, 2 * QUARTER), jnp.bfloat16)] * 2,
        compiler_params=limits(),
        cost_estimate=pl.CostEstimate(
            flops=12 * OUTER * QUARTER * INNER, bytes_accessed=12 * OUTER * INNER, transcendentals=0
        ),
    )(mid, matrices)


def mirror_call(base, own, far, edge):
    members, length = own.shape
    return pl.pallas_call(
        mirror_kernel,
        in_specs=[pl.BlockSpec(memory_space=pltpu.SMEM)] + [pl.BlockSpec(memory_space=pltpu.VMEM)] * 3,
        out_specs=pl.BlockSpec(memory_space=pltpu.VMEM),
        out_shape=jax.ShapeDtypeStruct((2, members, length), jnp.float32),
        compiler_params=limits(),
        cost_estimate=pl.CostEstimate(
            flops=200 * members * length, bytes_accessed=16 * members * length, transcendentals=0
        ),
    )(base, own, far, edge)


def line_params(roughness, waviness, coherence):
    return jnp.stack(
        [jnp.sqrt(2.0 * roughness * (waviness - 1.0) / ANCHOR), -0.5 * waviness, 1.0 / coherence]
    )


def to_group(piece, slot):
    groups = lax.axis_size("mem")
    return lax.ppermute(piece, "mem", [(z, z ^ slot) for z in range(groups)]) if slot else piece


def rows_gram(rows):
    return lax.dot_general(rows, rows, (((1,), (1,)), ((), ())), precision=highest)


def slot_rows(stretches, groups):
    my_group = lax.axis_index("mem")
    return jnp.concatenate(
        [
            to_group(lax.dynamic_index_in_dim(stretches, my_group ^ slot, 0, keepdims=False), slot)
            for slot in range(groups)
        ],
        axis=0,
    )


def own_and_far(phase, params):
    groups = lax.axis_size("mem")
    my_group = lax.axis_index("mem")
    half = phase.shape[1] // 2
    width = half // groups
    lane = lax.broadcasted_iota(jnp.int32, (phase.shape[0], LANES), 1)

    def lines(start):
        return (
            lax.dynamic_slice_in_dim(phase, start, width, 1),
            lax.dynamic_slice_in_dim(phase, start + width, LANES, 1),
        )

    own, far = [], []
    for slot in range(groups):
        group = my_group ^ slot
        inner, beyond = lines(group * width)
        for n in range(2):
            beyond = jnp.where(lane == n + 1, params[n][:, None], beyond)
        far_inner, far_beyond = lines(half + (groups - 1 - group) * width)
        message = jnp.concatenate(
            [
                jnp.concatenate([inner, beyond], axis=1)[None],
                jnp.concatenate([far_inner, far_beyond], axis=1)[None],
            ]
        )
        message = to_group(message, slot)
        own.append(message[0])
        far.append(message[1])
    return jnp.concatenate(own, axis=0), jnp.concatenate(far, axis=0)


def edge_of(own):
    shards = lax.axis_size("len")
    return lax.ppermute(own[:, :LANES], "len", [(d, (shards - d) % shards) for d in range(shards)])


def lines_gram(own, far, edge):
    shards, groups = lax.axis_size("len"), lax.axis_size("mem")
    my_index, my_group = lax.axis_index("len"), lax.axis_index("mem")
    width = own.shape[1] - LANES
    far = lax.ppermute(far, "len", [(d, shards - 1 - d) for d in range(shards)])
    base = (my_index * (2 * groups) + my_group) * width
    base = jnp.stack([base, my_group, jnp.full_like(my_group, groups)]).astype(jnp.int32)
    sums = mirror_call(base, own, far, edge)
    return rows_gram(sums[0]) + rows_gram(sums[1])


def in_order(gram_matrix, members):
    my_group = lax.axis_index("mem")
    row = lax.broadcasted_iota(jnp.int32, gram_matrix.shape, 0)
    column = lax.broadcasted_iota(jnp.int32, gram_matrix.shape, 1)
    to_slot = (row % members == column % members) & ((row // members) ^ my_group == column // members)
    to_slot = to_slot.astype(jnp.float32)
    return jnp.dot(jnp.dot(to_slot, gram_matrix, precision=highest), to_slot.T, precision=highest)


def summed(value):
    for axis in ("len", "mem"):
        value = jnp.sum(lax.all_gather(value, axis), axis=0)
    return value


def per_device_whole(phase_left, phase_right, roughness, waviness, coherence):
    shards, groups = lax.axis_size("len"), lax.axis_size("mem")
    my_index = lax.axis_index("len")
    members = phase_left.shape[0]

    def swap(piece):
        return lax.all_to_all(piece, "len", split_axis=0, concat_axis=0, tiled=True)

    all_params = line_params(roughness, waviness, coherence)
    params = lax.dynamic_index_in_dim(all_params, my_index, 1, keepdims=False)
    outer_tables = jnp.asarray(outer_matrices())
    inner_tables = jnp.asarray(inner_matrices())
    twists = jnp.asarray(twist_tables())
    places = 4

    def transform(phases, track):
        mid = outer_call(params, phases, outer_tables, twists, track)
        return list(inner_call(mid, inner_tables, shards, 2))

    left = swap(part_call(phase_left))
    own, far = own_and_far(phase_left, all_params)
    right = swap(part_call(phase_right))
    first = transform((left,), 0)
    left, right, *first = lax.optimization_barrier((left, right, *first))
    early = swap(first[0])
    second = transform((left, right), 1)
    early, second[0] = lax.optimization_barrier((early, second[0]))
    ahead = swap(second[0])
    edge = edge_of(own)
    ahead, edge, second[1] = lax.optimization_barrier((ahead, edge, second[1]))
    profile, ahead = join_call(ahead, 2, places, groups, None)
    behind = swap(second[1])
    behind, first[1], far = lax.optimization_barrier((behind, first[1], far))
    line_gram = lines_gram(own, far, edge)
    profile, behind = join_call(behind, 3, places, groups, profile)
    late = swap(first[1])
    point_gram = rows_gram(slot_rows(ahead, groups)) + rows_gram(slot_rows(behind, groups))
    late, point_gram = lax.optimization_barrier((late, point_gram))
    profile, _ = join_call(early, 0, places, groups, profile)
    profile, _ = join_call(late, 1, places, groups, profile)
    gram_matrix = 0.25 * line_gram + (0.5 / (OUTER * INNER)) * point_gram
    return (profile, upper_of(summed(in_order(gram_matrix, members))))


def per_device(phase_left, phase_right, roughness, waviness, coherence):
    whole_members = phase_left.shape[0] == lax.axis_size("len") and lax.axis_size("mem") in (2, 4)
    form = per_device_whole if whole_members else per_device_spread
    return form(phase_left, phase_right, roughness, waviness, coherence)


def solution(mesh):
    placed = (P("mem", "len"), P("mem", "len"), P("mem"), P("mem"), P("mem"))
    return jax.shard_map(
        per_device,
        mesh=mesh,
        in_specs=placed,
        out_specs=(P(None, "mem", "len"), P()),
        check_vma=False,
    )
```

```python
import functools
import math

import jax
import jax.numpy as jnp
import numpy as np
from jax import lax
from jax.experimental import pallas as pl
from jax.experimental.pallas import tpu as pltpu
from jax.sharding import PartitionSpec as P

OUTER = 1024
INNER = 1024
ANCHOR = 64
RADIX = 4
QUARTER = 256
LANES = 128
STEP = 16
WIDE = 256
BLOCK_ROWS = 16
OUTER_TILES = 2
VMEM_LIMIT = 48 * 1024 * 1024
SIN_HALF = (0.49999999785787, -0.02083332246218, 2.604078316692e-4, -1.547581723527e-6, 5.088214043e-9)
COS_HALF = (
    0.99999999977982,
    -0.12499999839235,
    2.604164763023e-3,
    -2.170056380508e-5,
    9.67192778775e-8,
    -2.5440497557e-10,
)


highest = lax.Precision.HIGHEST


def merged(shard, axis, combine):
    everything = lax.all_gather(shard, axis)
    leading = everything[0]

    def step(k, so_far):
        return combine(so_far, everything[k])

    return lax.fori_loop(1, lax.axis_size(axis), step, leading)


def dft_tables(length):
    index = lax.iota(jnp.int32, length)
    product = index[:, None] * index[None, :] % length
    phase_angle = product.astype(jnp.float32) * (2.0 * math.pi / length)
    return (jnp.cos(phase_angle), jnp.sin(phase_angle))


def spectra_of(phase_left, phase_right, roughness, waviness, coherence, freq):
    amplitude = jnp.sqrt(2.0 * roughness * (waviness - 1.0) / ANCHOR)[:, None] * (
        (freq + ANCHOR) / ANCHOR
    ) ** (-0.5 * waviness[:, None])
    freq_ratio = freq / coherence[:, None]
    coherent = 1.0 / (1.0 + freq_ratio * freq_ratio)
    incoherent = freq_ratio * jnp.sqrt(2.0 + freq_ratio * freq_ratio) * coherent
    cos_left = jnp.cos(phase_left)
    sin_left = jnp.sin(phase_left)
    cos_right = jnp.cos(phase_right)
    sin_right = jnp.sin(phase_right)
    real_part = jnp.stack(
        [amplitude * cos_left, amplitude * (coherent * cos_left + incoherent * cos_right)]
    )
    imag_part = jnp.stack(
        [amplitude * sin_left, amplitude * (coherent * sin_left + incoherent * sin_right)]
    )
    return (real_part, imag_part)


def upper_of(gram_matrix):
    return jnp.linalg.cholesky(gram_matrix).T


def combine_factors(upper_a, upper_b):
    gram_matrix = jnp.dot(upper_a.T, upper_a, precision=highest) + jnp.dot(
        upper_b.T, upper_b, precision=highest
    )
    return upper_of(gram_matrix)


def gram_of(snapshot):
    return jnp.einsum("tmr,tnr->mn", snapshot, snapshot, precision=highest)


def per_device_spread(phase_left, phase_right, roughness, waviness, coherence):
    shards = lax.axis_size("len")
    my_index = lax.axis_index("len")
    local_members, local_len = phase_left.shape
    columns = 2 * local_members
    outer_block = OUTER // shards
    inner_block = INNER // shards

    def to_rows(part):
        shaped = part.reshape(2, local_members, inner_block, OUTER)
        return jnp.transpose(shaped, (2, 3, 0, 1)).reshape(
            inner_block, shards, outer_block * columns
        )

    inner_cos, inner_sin = dft_tables(INNER)
    freq = (my_index * local_len + lax.iota(jnp.int32, local_len)).astype(jnp.float32)[None, :]
    real_part, imag_part = spectra_of(phase_left, phase_right, roughness, waviness, coherence, freq)
    pieces = (
        lax.all_to_all(to_rows(real_part), "len", split_axis=1, concat_axis=0, tiled=True),
        lax.all_to_all(to_rows(imag_part), "len", split_axis=1, concat_axis=0, tiled=True),
    )
    real_in = pieces[0].reshape(INNER, -1)
    imag_in = pieces[1].reshape(INNER, -1)
    real_out = jnp.dot(inner_cos, real_in, precision=highest) - jnp.dot(
        inner_sin, imag_in, precision=highest
    )
    imag_out = jnp.dot(inner_cos, imag_in, precision=highest) + jnp.dot(
        inner_sin, real_in, precision=highest
    )
    row_index = lax.iota(jnp.int32, INNER)[:, None]
    outer_index = (my_index * outer_block + lax.iota(jnp.int32, outer_block))[None, :]
    twist = (row_index * outer_index % (OUTER * INNER)).astype(jnp.float32) * (
        2.0 * math.pi / (OUTER * INNER)
    )
    twist_cos = jnp.repeat(jnp.cos(twist), columns, axis=1)
    twist_sin = jnp.repeat(jnp.sin(twist), columns, axis=1)
    rot_real = (real_out * twist_cos - imag_out * twist_sin).reshape(
        shards, inner_block, outer_block * columns
    )
    rot_imag = (real_out * twist_sin + imag_out * twist_cos).reshape(
        shards, inner_block, outer_block * columns
    )
    outer_cos, outer_sin = dft_tables(OUTER)
    outer_cos = outer_cos.reshape(OUTER, shards, outer_block)
    outer_sin = outer_sin.reshape(OUTER, shards, outer_block)
    pieces = (
        lax.all_to_all(rot_real, "len", split_axis=0, concat_axis=0, tiled=True),
        lax.all_to_all(rot_imag, "len", split_axis=0, concat_axis=0, tiled=True),
    )
    item_count = pieces[0].shape[1]
    real_in = pieces[0].reshape(shards, item_count, outer_block, columns)
    imag_in = pieces[1].reshape(shards, item_count, outer_block, columns)
    first = jnp.einsum("jqa,qiac->cij", outer_cos, real_in, precision=highest)
    second = jnp.einsum("jqa,qiac->cij", outer_sin, imag_in, precision=highest)
    profile_block = first - second
    outgoing = jnp.transpose(
        profile_block.reshape(columns, inner_block, shards, outer_block), (2, 0, 1, 3)
    ).reshape(shards, -1)
    arrived = lax.all_to_all(outgoing, "len", split_axis=0, concat_axis=0, tiled=True)
    profile = jnp.transpose(
        arrived.reshape(shards, columns, inner_block, outer_block), (1, 3, 0, 2)
    ).reshape(2, local_members, local_len)
    scale = 1.0 / math.sqrt(2.0 * OUTER * INNER)
    snapshot = profile_block.reshape(2, local_members, inner_block * OUTER) * scale
    gathered = lax.all_gather(snapshot, "mem", axis=1, tiled=True)
    gram_local = gram_of(gathered)
    r_factor = merged(upper_of(gram_local), "len", combine_factors)
    return (profile, r_factor)


def host_cis(product, period):
    angle = product % period * (2.0 * np.pi / period)
    return np.cos(angle), np.sin(angle)


def split_host(table):
    coarse = table.astype(np.float32).astype(jnp.bfloat16)
    fine = (table - coarse.astype(np.float64)).astype(np.float32).astype(jnp.bfloat16)
    return np.stack([coarse, fine])


def outer_matrices():
    c, e, b = np.arange(QUARTER), np.arange(RADIX), np.arange(QUARTER)
    cos_part, sin_part = host_cis((RADIX * c[None, :, None] + e[:, None, None]) * b[None, None, :], OUTER)
    upper = np.concatenate([cos_part, -sin_part], axis=2)
    lower = np.concatenate([sin_part, cos_part], axis=2)
    return split_host(np.concatenate([upper, lower], axis=1))


def inner_matrices():
    c, e, b = np.arange(QUARTER), np.arange(RADIX), np.arange(QUARTER)
    cos_part, sin_part = host_cis((RADIX * c[None, :, None] + e[:, None, None]) * b[None, None, :], INNER)
    return split_host(np.concatenate([cos_part, -sin_part], axis=2))


def twist_tables():
    j1 = RADIX * np.arange(QUARTER)[None, :, None] + np.arange(RADIX)[:, None, None]
    cos_part, sin_part = host_cis(j1 * np.arange(INNER)[None, None, :], OUTER * INNER)
    return np.stack([cos_part, sin_part]).astype(np.float32)


def sin_cos(angle):
    square = angle * angle

    def series(coefficients):
        total = jnp.float32(coefficients[-1])
        for coefficient in coefficients[-2::-1]:
            total = total * square + jnp.float32(coefficient)
        return total

    half_sin = angle * series(SIN_HALF)
    half_cos = series(COS_HALF)
    twice = half_sin + half_sin
    return twice * half_cos, 1.0 - twice * half_sin


def left_lines(left, freq, scale, exponent):
    amplitude = scale * jnp.exp2(exponent * jnp.log2((freq + ANCHOR) * (1.0 / ANCHOR)))
    sin_left, cos_left = sin_cos(left)
    return amplitude * cos_left, amplitude * sin_left


def line_spectra(left, right, freq, scale, exponent, inverse_coherence):
    amplitude = scale * jnp.exp2(exponent * jnp.log2((freq + ANCHOR) * (1.0 / ANCHOR)))
    freq_ratio = freq * inverse_coherence
    ratio_square = freq_ratio * freq_ratio
    coherent = 1.0 / (1.0 + ratio_square)
    incoherent = freq_ratio * jnp.sqrt(2.0 + ratio_square) * coherent
    sin_left, cos_left = sin_cos(left)
    sin_right, cos_right = sin_cos(right)
    independent = amplitude * incoherent
    first = (amplitude * cos_left, amplitude * sin_left)
    second = (
        coherent * first[0] + independent * cos_right,
        coherent * first[1] + independent * sin_right,
    )
    return first, second


def radix_four(parts):
    (r0, i0), (r1, i1), (r2, i2), (r3, i3) = parts
    even_sum, even_gap = (r0 + r2, i0 + i2), (r0 - r2, i0 - i2)
    odd_sum, odd_gap = (r1 + r3, i1 + i3), (r1 - r3, i1 - i3)
    return (
        (even_sum[0] + odd_sum[0], even_sum[1] + odd_sum[1]),
        (even_gap[0] - odd_gap[1], even_gap[1] + odd_gap[0]),
        (even_sum[0] - odd_sum[0], even_sum[1] - odd_sum[1]),
        (even_gap[0] + odd_gap[1], even_gap[1] - odd_gap[0]),
    )


def store_split(coarse_ref, fine_ref, where, value):
    coarse = value.astype(jnp.bfloat16)
    coarse_ref[where] = coarse
    fine_ref[where] = (value - coarse.astype(jnp.float32)).astype(jnp.bfloat16)


def triple_dot(matrix_ref, e, coarse, fine, dims):
    def product(a, b):
        return lax.dot_general(a, b, (dims, ((), ())), preferred_element_type=jnp.float32)

    return product(matrix_ref[0, e], coarse) + (
        product(matrix_ref[0, e], fine) + product(matrix_ref[1, e], coarse)
    )


def outer_kernel(track, params_ref, *refs):
    phase_refs, (matrix_ref, twist_ref, out_ref, coarse_ref, fine_ref) = refs[:-5], refs[-5:]
    scale, exponent, inverse_coherence = params_ref[0], params_ref[1], params_ref[2]
    _, tiles, rows, _ = phase_refs[0].shape
    lane = lax.broadcasted_iota(jnp.int32, (STEP, LANES), 1) + pl.program_id(0) * tiles * LANES
    row = lax.broadcasted_iota(jnp.int32, (STEP, LANES), 0)
    place = row * INNER + lane

    def some_rows(step, carry):
        b = step * STEP
        for tile in range(tiles):
            lines = []
            for a in range(RADIX):
                k1 = a * QUARTER + b
                source, inside = k1 // rows, pl.multiple_of(k1 % rows, STEP)
                freq = (place + (k1 * INNER + tile * LANES)).astype(jnp.float32)
                phases = [ref[source, tile, pl.ds(inside, STEP), :] for ref in phase_refs]
                if track == 0:
                    lines.append(left_lines(*phases, freq, scale, exponent))
                else:
                    lines.append(line_spectra(*phases, freq, scale, exponent, inverse_coherence)[1])
            mixed = radix_four(lines)
            for e in range(RADIX):
                for ri in range(2):
                    at = pl.ds(pl.multiple_of(ri * QUARTER + b, STEP), STEP)
                    where = (e, at, pl.ds(tile * LANES, LANES))
                    store_split(coarse_ref, fine_ref, where, mixed[e][ri])
        return carry

    lax.fori_loop(0, QUARTER // STEP, some_rows, 0)
    for e in range(RADIX):
        mid = triple_dot(matrix_ref, e, coarse_ref[e], fine_ref[e], ((1,), (0,)))
        for tile in range(tiles):
            lanes = slice(tile * LANES, (tile + 1) * LANES)
            cos_part, sin_part = twist_ref[0, e, :, lanes], twist_ref[1, e, :, lanes]
            real, imag = mid[:QUARTER, lanes], mid[QUARTER:, lanes]
            out_ref[tile, 0, pl.ds(e, QUARTER, stride=RADIX), :] = real * cos_part - imag * sin_part
            out_ref[tile, 1, pl.ds(e, QUARTER, stride=RADIX), :] = real * sin_part + imag * cos_part


def inner_kernel(mid_ref, matrix_ref, *refs):
    out_refs, (coarse_ref, fine_ref) = refs[:-2], refs[-2:]
    wide = mid_ref.shape[2]
    shards, _, rows, _ = out_refs[0].shape

    def some_rows(step, carry):
        at = pl.multiple_of(step * STEP, STEP)
        for half in range(0, QUARTER, LANES):
            parts = [
                tuple(mid_ref[(a * QUARTER + half) // LANES, ri, pl.ds(at, STEP), :] for ri in range(2))
                for a in range(RADIX)
            ]
            mixed = radix_four(parts)
            for e in range(RADIX):
                for ri in range(2):
                    where = (e, pl.ds(at, STEP), pl.ds(ri * QUARTER + half, LANES))
                    store_split(coarse_ref, fine_ref, where, mixed[e][ri])
        return carry

    lax.fori_loop(0, wide // STEP, some_rows, 0)
    some = rows // RADIX
    for e in range(RADIX):
        value = triple_dot(matrix_ref, e, coarse_ref[e], fine_ref[e], ((1,), (1,)))
        for f in range(shards):
            for part, out_ref in enumerate(out_refs):
                at = (f * len(out_refs) + part) * some
                for tile in range(wide // LANES):
                    out_ref[f, tile, pl.ds(e, some, stride=RADIX), :] = value[
                        at : at + some, tile * LANES : (tile + 1) * LANES
                    ]


def part_kernel(in_ref, out_ref):
    members, tiles, rows, _ = out_ref.shape
    flat_ref = out_ref.reshape(members * tiles * rows, LANES)
    for r in range(rows):
        for tile in range(tiles):
            at = (r * tiles + tile) * LANES
            flat_ref[pl.ds(tile * rows + r, members, stride=tiles * rows), :] = in_ref[:, at : at + LANES]


def join_kernel(extra, in_ref, *refs):
    out_refs = refs[-2:] if extra else refs[-1:]
    members, tiles, rows, _ = in_ref.shape
    flat_ref = in_ref.reshape(members * tiles * rows, LANES)
    for r in range(rows):
        for tile in range(tiles):
            at = (r * tiles + tile) * LANES
            value = flat_ref[pl.ds(tile * rows + r, members, stride=tiles * rows), :]
            for out_ref in out_refs:
                out_ref[0, :, at : at + LANES] = value


def mirror_kernel(base_ref, own_ref, far_ref, edge_ref, out_ref):
    members, length = own_ref.shape
    tiles = length // LANES - 1
    shape = (members, LANES)
    lane = lax.broadcasted_iota(jnp.int32, shape, 1)
    mirror = (LANES - lane) % LANES
    first_group, last_group = base_ref[1] == 0, base_ref[1] == base_ref[2] - 1
    beyond = own_ref[:, tiles * LANES :]
    scale = jnp.broadcast_to(beyond[:, 1:2], shape)
    exponent = jnp.broadcast_to(beyond[:, 2:3], shape)
    half_root = math.sqrt(0.5)

    def tile_of(ref, tile):
        return ref[:, pl.ds(pl.multiple_of(tile * LANES, LANES), LANES)]

    def turned(value):
        return jnp.take_along_axis(value, mirror, axis=1, mode="promise_in_bounds")

    def store(tile, own, far, weight):
        offset = base_ref[0] + tile * LANES + lane
        near = left_lines(own, offset.astype(jnp.float32), scale, exponent)
        far_offset = jnp.where(offset == 0, 0, OUTER * INNER - offset)
        back = left_lines(far, far_offset.astype(jnp.float32), scale, exponent)
        at = pl.ds(pl.multiple_of(tile * LANES, LANES), LANES)
        out_ref[0, :, at] = (near[0] + back[0]) * weight
        out_ref[1, :, at] = (near[1] - back[1]) * weight

    def one_tile(tile, last):
        ahead = turned(tile_of(far_ref, tiles - 1 - tile))
        is_edge = (lane == 0) & (tile == 0) & first_group
        store(tile, tile_of(own_ref, tile), jnp.where(lane == 0, last, ahead), jnp.where(is_edge, half_root, 1.0))
        return ahead

    start = jnp.where(first_group, turned(edge_ref[...]), turned(tile_of(far_ref, tiles)))
    last = lax.fori_loop(0, tiles, one_tile, start)
    lone = (lane == 0) & last_group
    store(tiles, jnp.where(lone, beyond, 0.0), jnp.where(lone, last, 0.0), jnp.where(lone, half_root, 0.0))


def limits():
    return pltpu.CompilerParams(vmem_limit_bytes=VMEM_LIMIT)


def part_call(phase):
    members, length = phase.shape
    rows = length // INNER
    tiles = INNER // LANES
    return pl.pallas_call(
        part_kernel,
        grid=(rows // BLOCK_ROWS,),
        in_specs=[pl.BlockSpec((members, BLOCK_ROWS * INNER), lambda g: (0, g))],
        out_specs=pl.BlockSpec((members, tiles, BLOCK_ROWS, LANES), lambda g: (0, 0, g, 0)),
        out_shape=pltpu.HBM((members, tiles, rows, LANES), jnp.float32),
        compiler_params=limits(),
        cost_estimate=pl.CostEstimate(flops=0, bytes_accessed=8 * members * length, transcendentals=0),
    )(phase)


def join_call(piece, track, within, length, groups, so_far):
    members, tiles, rows, _ = piece.shape
    stretch = rows * INNER
    steps = rows // BLOCK_ROWS
    operands = (piece,) if so_far is None else (piece, so_far)
    each = max(steps // max(groups, 1), 1)
    return pl.pallas_call(
        functools.partial(join_kernel, groups > 0),
        grid=(steps,),
        in_specs=[
            pl.BlockSpec((members, tiles, BLOCK_ROWS, LANES), lambda g: (0, 0, g, 0)),
            pl.BlockSpec(memory_space=pl.ANY),
        ][: len(operands)],
        out_specs=[
            pl.BlockSpec((1, members, BLOCK_ROWS * INNER), lambda g: (track, 0, within * steps + g)),
            pl.BlockSpec((1, members, BLOCK_ROWS * INNER), lambda g: (g // each, 0, g % each)),
        ][: 2 if groups else 1],
        out_shape=[
            jax.ShapeDtypeStruct((2, members, length), jnp.float32),
            jax.ShapeDtypeStruct((max(groups, 1), members, stretch // max(groups, 1)), jnp.float32),
        ][: 2 if groups else 1],
        input_output_aliases={} if so_far is None else {1: 0},
        compiler_params=limits(),
        cost_estimate=pl.CostEstimate(flops=0, bytes_accessed=12 * members * stretch, transcendentals=0),
    )(*operands)


def outer_call(params, phases, matrices, twists, track):
    sources, tiles, rows, _ = phases[0].shape
    some = OUTER_TILES
    return pl.pallas_call(
        functools.partial(outer_kernel, track),
        grid=(tiles // some,),
        in_specs=[pl.BlockSpec(memory_space=pltpu.SMEM)]
        + [pl.BlockSpec((sources, some, rows, LANES), lambda g: (0, g, 0, 0))] * len(phases)
        + [
            pl.BlockSpec(matrices.shape, lambda g: (0, 0, 0, 0)),
            pl.BlockSpec((2, RADIX, QUARTER, some * LANES), lambda g: (0, 0, 0, g)),
        ],
        out_specs=pl.BlockSpec((some, 2, OUTER, LANES), lambda g: (g, 0, 0, 0)),
        out_shape=jax.ShapeDtypeStruct((tiles, 2, OUTER, LANES), jnp.float32),
        scratch_shapes=[pltpu.VMEM((RADIX, 2 * QUARTER, some * LANES), jnp.bfloat16)] * 2,
        compiler_params=limits(),
        cost_estimate=pl.CostEstimate(
            flops=24 * OUTER * QUARTER * INNER, bytes_accessed=20 * OUTER * INNER, transcendentals=0
        ),
    )(params, *phases, matrices, twists)


def inner_call(mid, matrices, shards, parts):
    rows = INNER // shards // parts
    tiles = OUTER // LANES
    return pl.pallas_call(
        inner_kernel,
        grid=(OUTER // WIDE,),
        in_specs=[
            pl.BlockSpec((INNER // LANES, 2, WIDE, LANES), lambda g: (0, 0, g, 0)),
            pl.BlockSpec(matrices.shape, lambda g: (0, 0, 0, 0)),
        ],
        out_specs=[pl.BlockSpec((shards, WIDE // LANES, rows, LANES), lambda g: (0, g, 0, 0))] * parts,
        out_shape=[pltpu.HBM((shards, tiles, rows, LANES), jnp.float32)] * parts,
        scratch_shapes=[pltpu.VMEM((RADIX, WIDE, 2 * QUARTER), jnp.bfloat16)] * 2,
        compiler_params=limits(),
        cost_estimate=pl.CostEstimate(
            flops=12 * OUTER * QUARTER * INNER, bytes_accessed=12 * OUTER * INNER, transcendentals=0
        ),
    )(mid, matrices)


def mirror_call(base, own, far, edge):
    members, length = own.shape
    return pl.pallas_call(
        mirror_kernel,
        in_specs=[pl.BlockSpec(memory_space=pltpu.SMEM)] + [pl.BlockSpec(memory_space=pltpu.VMEM)] * 3,
        out_specs=pl.BlockSpec(memory_space=pltpu.VMEM),
        out_shape=jax.ShapeDtypeStruct((2, members, length), jnp.float32),
        compiler_params=limits(),
        cost_estimate=pl.CostEstimate(
            flops=200 * members * length, bytes_accessed=16 * members * length, transcendentals=0
        ),
    )(base, own, far, edge)


def line_params(roughness, waviness, coherence):
    return jnp.stack(
        [jnp.sqrt(2.0 * roughness * (waviness - 1.0) / ANCHOR), -0.5 * waviness, 1.0 / coherence]
    )


def to_group(piece, slot):
    groups = lax.axis_size("mem")
    return lax.ppermute(piece, "mem", [(z, z ^ slot) for z in range(groups)]) if slot else piece


def rows_gram(rows):
    return lax.dot_general(rows, rows, (((1,), (1,)), ((), ())), precision=highest)


def slot_rows(stretches, groups):
    my_group = lax.axis_index("mem")
    return jnp.concatenate(
        [
            to_group(lax.dynamic_index_in_dim(stretches, my_group ^ slot, 0, keepdims=False), slot)
            for slot in range(groups)
        ],
        axis=0,
    )


def own_and_far(phase, params, my_group):
    groups = lax.axis_size("mem")
    half = phase.shape[1] // 2
    width = half // groups
    lane = lax.broadcasted_iota(jnp.int32, (phase.shape[0], LANES), 1)

    def lines(start):
        return (
            lax.dynamic_slice_in_dim(phase, start, width, 1),
            lax.dynamic_slice_in_dim(phase, start + width, LANES, 1),
        )

    own, far = [], []
    for slot in range(groups):
        group = my_group ^ slot
        inner, beyond = lines(group * width)
        for n in range(2):
            beyond = jnp.where(lane == n + 1, params[n][:, None], beyond)
        far_inner, far_beyond = lines(half + (groups - 1 - group) * width)
        message = jnp.concatenate(
            [
                jnp.concatenate([inner, beyond], axis=1)[None],
                jnp.concatenate([far_inner, far_beyond], axis=1)[None],
            ]
        )
        message = to_group(message, slot)
        own.append(message[0])
        far.append(message[1])
    return jnp.concatenate(own, axis=0), jnp.concatenate(far, axis=0)


def edge_of(own):
    shards = lax.axis_size("len")
    return lax.ppermute(own[:, :LANES], "len", [(d, (shards - d) % shards) for d in range(shards)])


def across(far):
    shards = lax.axis_size("len")
    return lax.ppermute(far, "len", [(d, shards - 1 - d) for d in range(shards)])


def lines_gram(own, far, edge):
    groups = lax.axis_size("mem")
    my_index, my_group = lax.axis_index("len"), lax.axis_index("mem")
    width = own.shape[1] - LANES
    base = (my_index * (2 * groups) + my_group) * width
    base = jnp.stack([base, my_group, jnp.full_like(my_group, groups)]).astype(jnp.int32)
    sums = mirror_call(base, own, far, edge)
    return rows_gram(sums[0]) + rows_gram(sums[1])


def in_order(gram_matrix, members):
    my_group = lax.axis_index("mem")
    row = lax.broadcasted_iota(jnp.int32, gram_matrix.shape, 0)
    column = lax.broadcasted_iota(jnp.int32, gram_matrix.shape, 1)
    to_slot = (row % members == column % members) & ((row // members) ^ my_group == column // members)
    to_slot = to_slot.astype(jnp.float32)
    return jnp.dot(jnp.dot(to_slot, gram_matrix, precision=highest), to_slot.T, precision=highest)


def summed(value):
    for axis in ("len", "mem"):
        value = jnp.sum(lax.all_gather(value, axis), axis=0)
    return value


def per_device_whole(phase_left, phase_right, roughness, waviness, coherence):
    shards, groups = lax.axis_size("len"), lax.axis_size("mem")
    my_index = lax.axis_index("len")
    members = phase_left.shape[0]

    def swap(piece):
        return lax.all_to_all(piece, "len", split_axis=0, concat_axis=0, tiled=True)

    all_params = line_params(roughness, waviness, coherence)
    params = lax.dynamic_index_in_dim(all_params, my_index, 1, keepdims=False)
    outer_tables = jnp.asarray(outer_matrices())
    inner_tables = jnp.asarray(inner_matrices())
    twists = jnp.asarray(twist_tables())
    local_len = phase_left.shape[1]

    def transform(phases, track, parts):
        mid = outer_call(params, phases, outer_tables, twists, track)
        return list(inner_call(mid, inner_tables, shards, parts))

    left = part_call(phase_left)
    left, my_group = lax.optimization_barrier((left, lax.axis_index("mem")))
    left = swap(left)
    own, far = own_and_far(phase_left, all_params, my_group)
    right = swap(part_call(phase_right))
    first = transform((left,), 0, 1)[0]
    edge = edge_of(own)
    left, right, first, far, edge = lax.optimization_barrier((left, right, first, far, edge))
    far = across(far)
    second = transform((left, right), 1, 2)
    ahead = swap(second[0])
    line_gram = lines_gram(own, far, edge)
    ahead, line_gram, second[1] = lax.optimization_barrier((ahead, line_gram, second[1]))
    behind = swap(second[1])
    profile, ahead = join_call(ahead, 1, 0, local_len, groups, None)
    point_gram = rows_gram(slot_rows(ahead, groups))
    behind, point_gram, first = lax.optimization_barrier((behind, point_gram, first))
    first = swap(first)
    profile, behind = join_call(behind, 1, 1, local_len, groups, profile)
    point_gram = point_gram + rows_gram(slot_rows(behind, groups))
    first, point_gram = lax.optimization_barrier((first, point_gram))
    (profile,) = join_call(first, 0, 0, local_len, 0, profile)
    gram_matrix = 0.25 * line_gram + (0.5 / (OUTER * INNER)) * point_gram
    return (profile, upper_of(summed(in_order(gram_matrix, members))))


def per_device(phase_left, phase_right, roughness, waviness, coherence):
    whole_members = phase_left.shape[0] == lax.axis_size("len") and lax.axis_size("mem") in (2, 4)
    form = per_device_whole if whole_members else per_device_spread
    return form(phase_left, phase_right, roughness, waviness, coherence)


def solution(mesh):
    placed = (P("mem", "len"), P("mem", "len"), P("mem"), P("mem"), P("mem"))
    return jax.shard_map(
        per_device,
        mesh=mesh,
        in_specs=placed,
        out_specs=(P(None, "mem", "len"), P()),
        check_vma=False,
    )
```

```python
import functools
import math

import jax
import jax.numpy as jnp
import numpy as np
from jax import lax
from jax.experimental import pallas as pl
from jax.experimental.pallas import tpu as pltpu
from jax.sharding import PartitionSpec as P

OUTER = 1024
INNER = 1024
ANCHOR = 64
RADIX = 4
QUARTER = 256
LANES = 128
STEP = 16
WIDE = 256
BLOCK_ROWS = 16
OUTER_TILES = 2
VMEM_LIMIT = 48 * 1024 * 1024
SIN_HALF = (0.49999999785787, -0.02083332246218, 2.604078316692e-4, -1.547581723527e-6, 5.088214043e-9)
COS_HALF = (
    0.99999999977982,
    -0.12499999839235,
    2.604164763023e-3,
    -2.170056380508e-5,
    9.67192778775e-8,
    -2.5440497557e-10,
)


highest = lax.Precision.HIGHEST


def merged(shard, axis, combine):
    everything = lax.all_gather(shard, axis)
    leading = everything[0]

    def step(k, so_far):
        return combine(so_far, everything[k])

    return lax.fori_loop(1, lax.axis_size(axis), step, leading)


def dft_tables(length):
    index = lax.iota(jnp.int32, length)
    product = index[:, None] * index[None, :] % length
    phase_angle = product.astype(jnp.float32) * (2.0 * math.pi / length)
    return (jnp.cos(phase_angle), jnp.sin(phase_angle))


def spectra_of(phase_left, phase_right, roughness, waviness, coherence, freq):
    amplitude = jnp.sqrt(2.0 * roughness * (waviness - 1.0) / ANCHOR)[:, None] * (
        (freq + ANCHOR) / ANCHOR
    ) ** (-0.5 * waviness[:, None])
    freq_ratio = freq / coherence[:, None]
    coherent = 1.0 / (1.0 + freq_ratio * freq_ratio)
    incoherent = freq_ratio * jnp.sqrt(2.0 + freq_ratio * freq_ratio) * coherent
    cos_left = jnp.cos(phase_left)
    sin_left = jnp.sin(phase_left)
    cos_right = jnp.cos(phase_right)
    sin_right = jnp.sin(phase_right)
    real_part = jnp.stack(
        [amplitude * cos_left, amplitude * (coherent * cos_left + incoherent * cos_right)]
    )
    imag_part = jnp.stack(
        [amplitude * sin_left, amplitude * (coherent * sin_left + incoherent * sin_right)]
    )
    return (real_part, imag_part)


def upper_of(gram_matrix):
    return jnp.linalg.cholesky(gram_matrix).T


def combine_factors(upper_a, upper_b):
    gram_matrix = jnp.dot(upper_a.T, upper_a, precision=highest) + jnp.dot(
        upper_b.T, upper_b, precision=highest
    )
    return upper_of(gram_matrix)


def gram_of(snapshot):
    return jnp.einsum("tmr,tnr->mn", snapshot, snapshot, precision=highest)


def per_device_spread(phase_left, phase_right, roughness, waviness, coherence):
    shards = lax.axis_size("len")
    my_index = lax.axis_index("len")
    local_members, local_len = phase_left.shape
    columns = 2 * local_members
    outer_block = OUTER // shards
    inner_block = INNER // shards

    def to_rows(part):
        shaped = part.reshape(2, local_members, inner_block, OUTER)
        return jnp.transpose(shaped, (2, 3, 0, 1)).reshape(
            inner_block, shards, outer_block * columns
        )

    inner_cos, inner_sin = dft_tables(INNER)
    freq = (my_index * local_len + lax.iota(jnp.int32, local_len)).astype(jnp.float32)[None, :]
    real_part, imag_part = spectra_of(phase_left, phase_right, roughness, waviness, coherence, freq)
    pieces = (
        lax.all_to_all(to_rows(real_part), "len", split_axis=1, concat_axis=0, tiled=True),
        lax.all_to_all(to_rows(imag_part), "len", split_axis=1, concat_axis=0, tiled=True),
    )
    real_in = pieces[0].reshape(INNER, -1)
    imag_in = pieces[1].reshape(INNER, -1)
    real_out = jnp.dot(inner_cos, real_in, precision=highest) - jnp.dot(
        inner_sin, imag_in, precision=highest
    )
    imag_out = jnp.dot(inner_cos, imag_in, precision=highest) + jnp.dot(
        inner_sin, real_in, precision=highest
    )
    row_index = lax.iota(jnp.int32, INNER)[:, None]
    outer_index = (my_index * outer_block + lax.iota(jnp.int32, outer_block))[None, :]
    twist = (row_index * outer_index % (OUTER * INNER)).astype(jnp.float32) * (
        2.0 * math.pi / (OUTER * INNER)
    )
    twist_cos = jnp.repeat(jnp.cos(twist), columns, axis=1)
    twist_sin = jnp.repeat(jnp.sin(twist), columns, axis=1)
    rot_real = (real_out * twist_cos - imag_out * twist_sin).reshape(
        shards, inner_block, outer_block * columns
    )
    rot_imag = (real_out * twist_sin + imag_out * twist_cos).reshape(
        shards, inner_block, outer_block * columns
    )
    outer_cos, outer_sin = dft_tables(OUTER)
    outer_cos = outer_cos.reshape(OUTER, shards, outer_block)
    outer_sin = outer_sin.reshape(OUTER, shards, outer_block)
    pieces = (
        lax.all_to_all(rot_real, "len", split_axis=0, concat_axis=0, tiled=True),
        lax.all_to_all(rot_imag, "len", split_axis=0, concat_axis=0, tiled=True),
    )
    item_count = pieces[0].shape[1]
    real_in = pieces[0].reshape(shards, item_count, outer_block, columns)
    imag_in = pieces[1].reshape(shards, item_count, outer_block, columns)
    first = jnp.einsum("jqa,qiac->cij", outer_cos, real_in, precision=highest)
    second = jnp.einsum("jqa,qiac->cij", outer_sin, imag_in, precision=highest)
    profile_block = first - second
    outgoing = jnp.transpose(
        profile_block.reshape(columns, inner_block, shards, outer_block), (2, 0, 1, 3)
    ).reshape(shards, -1)
    arrived = lax.all_to_all(outgoing, "len", split_axis=0, concat_axis=0, tiled=True)
    profile = jnp.transpose(
        arrived.reshape(shards, columns, inner_block, outer_block), (1, 3, 0, 2)
    ).reshape(2, local_members, local_len)
    scale = 1.0 / math.sqrt(2.0 * OUTER * INNER)
    snapshot = profile_block.reshape(2, local_members, inner_block * OUTER) * scale
    gathered = lax.all_gather(snapshot, "mem", axis=1, tiled=True)
    gram_local = gram_of(gathered)
    r_factor = merged(upper_of(gram_local), "len", combine_factors)
    return (profile, r_factor)


def host_cis(product, period):
    angle = product % period * (2.0 * np.pi / period)
    return np.cos(angle), np.sin(angle)


def split_host(table):
    coarse = table.astype(np.float32).astype(jnp.bfloat16)
    fine = (table - coarse.astype(np.float64)).astype(np.float32).astype(jnp.bfloat16)
    return np.stack([coarse, fine])


def outer_matrices():
    c, e, b = np.arange(QUARTER), np.arange(RADIX), np.arange(QUARTER)
    cos_part, sin_part = host_cis((RADIX * c[None, :, None] + e[:, None, None]) * b[None, None, :], OUTER)
    upper = np.concatenate([cos_part, -sin_part], axis=2)
    lower = np.concatenate([sin_part, cos_part], axis=2)
    return split_host(np.concatenate([upper, lower], axis=1))


def inner_matrices():
    c, e, b = np.arange(QUARTER), np.arange(RADIX), np.arange(QUARTER)
    cos_part, sin_part = host_cis((RADIX * c[None, :, None] + e[:, None, None]) * b[None, None, :], INNER)
    return split_host(np.concatenate([cos_part, -sin_part], axis=2))


def twist_tables():
    j1 = RADIX * np.arange(QUARTER)[None, :, None] + np.arange(RADIX)[:, None, None]
    cos_part, sin_part = host_cis(j1 * np.arange(INNER)[None, None, :], OUTER * INNER)
    return np.stack([cos_part, sin_part]).astype(np.float32)


def sin_cos(angle):
    square = angle * angle

    def series(coefficients):
        total = jnp.float32(coefficients[-1])
        for coefficient in coefficients[-2::-1]:
            total = total * square + jnp.float32(coefficient)
        return total

    half_sin = angle * series(SIN_HALF)
    half_cos = series(COS_HALF)
    twice = half_sin + half_sin
    return twice * half_cos, 1.0 - twice * half_sin


def amplitude_of(freq, scale, exponent):
    return scale * jnp.exp2(exponent * jnp.log2((freq + ANCHOR) * (1.0 / ANCHOR)))


def left_lines(left, freq, scale, exponent):
    amplitude = amplitude_of(freq, scale, exponent)
    sin_left, cos_left = sin_cos(left)
    return amplitude * cos_left, amplitude * sin_left


def radix_four(parts):
    (r0, i0), (r1, i1), (r2, i2), (r3, i3) = parts
    even_sum, even_gap = (r0 + r2, i0 + i2), (r0 - r2, i0 - i2)
    odd_sum, odd_gap = (r1 + r3, i1 + i3), (r1 - r3, i1 - i3)
    return (
        (even_sum[0] + odd_sum[0], even_sum[1] + odd_sum[1]),
        (even_gap[0] - odd_gap[1], even_gap[1] + odd_gap[0]),
        (even_sum[0] - odd_sum[0], even_sum[1] - odd_sum[1]),
        (even_gap[0] + odd_gap[1], even_gap[1] - odd_gap[0]),
    )


def store_split(coarse_ref, fine_ref, where, value):
    coarse = value.astype(jnp.bfloat16)
    coarse_ref[where] = coarse
    fine_ref[where] = (value - coarse.astype(jnp.float32)).astype(jnp.bfloat16)


def triple_dot(matrix_ref, e, coarse, fine, dims):
    def product(a, b):
        return lax.dot_general(a, b, (dims, ((), ())), preferred_element_type=jnp.float32)

    return product(matrix_ref[0, e], coarse) + (
        product(matrix_ref[0, e], fine) + product(matrix_ref[1, e], coarse)
    )


def first_lines(params_ref, left_ref, kept_refs, where, freq):
    scale, exponent, inverse_coherence = params_ref[0], params_ref[1], params_ref[2]
    amplitude = amplitude_of(freq, scale, exponent)
    freq_ratio = freq * inverse_coherence
    ratio_square = freq_ratio * freq_ratio
    coherent = 1.0 / (1.0 + ratio_square)
    incoherent = freq_ratio * jnp.sqrt(2.0 + ratio_square) * coherent
    sin_left, cos_left = sin_cos(left_ref[where])
    real, imag = amplitude * cos_left, amplitude * sin_left
    kept_refs[0][where] = coherent * real
    kept_refs[1][where] = coherent * imag
    kept_refs[2][where] = amplitude * incoherent
    return real, imag


def second_lines(right_ref, kept_refs, where):
    sin_right, cos_right = sin_cos(right_ref[where])
    independent = kept_refs[2][where]
    return (
        kept_refs[0][where] + independent * cos_right,
        kept_refs[1][where] + independent * sin_right,
    )


def outer_kernel(track, params_ref, phase_ref, *refs):
    if track == 0:
        matrix_ref, twist_ref, out_ref, *kept_refs, coarse_ref, fine_ref = refs
    else:
        *kept_refs, matrix_ref, twist_ref, out_ref, coarse_ref, fine_ref = refs
    _, tiles, rows, _ = phase_ref.shape
    lane = lax.broadcasted_iota(jnp.int32, (STEP, LANES), 1) + pl.program_id(0) * tiles * LANES
    row = lax.broadcasted_iota(jnp.int32, (STEP, LANES), 0)
    place = row * INNER + lane

    def some_rows(step, carry):
        b = step * STEP
        for tile in range(tiles):
            lines = []
            for a in range(RADIX):
                k1 = a * QUARTER + b
                where = (k1 // rows, tile, pl.ds(pl.multiple_of(k1 % rows, STEP), STEP))
                if track == 0:
                    freq = (place + (k1 * INNER + tile * LANES)).astype(jnp.float32)
                    lines.append(first_lines(params_ref, phase_ref, kept_refs, where, freq))
                else:
                    lines.append(second_lines(phase_ref, kept_refs, where))
            mixed = radix_four(lines)
            for e in range(RADIX):
                for ri in range(2):
                    at = pl.ds(pl.multiple_of(ri * QUARTER + b, STEP), STEP)
                    where = (e, at, pl.ds(tile * LANES, LANES))
                    store_split(coarse_ref, fine_ref, where, mixed[e][ri])
        return carry

    lax.fori_loop(0, QUARTER // STEP, some_rows, 0)
    for e in range(RADIX):
        mid = triple_dot(matrix_ref, e, coarse_ref[e], fine_ref[e], ((1,), (0,)))
        for tile in range(tiles):
            lanes = slice(tile * LANES, (tile + 1) * LANES)
            cos_part, sin_part = twist_ref[0, e, :, lanes], twist_ref[1, e, :, lanes]
            real, imag = mid[:QUARTER, lanes], mid[QUARTER:, lanes]
            out_ref[tile, 0, pl.ds(e, QUARTER, stride=RADIX), :] = real * cos_part - imag * sin_part
            out_ref[tile, 1, pl.ds(e, QUARTER, stride=RADIX), :] = real * sin_part + imag * cos_part


def inner_kernel(mid_ref, matrix_ref, *refs):
    out_refs, (coarse_ref, fine_ref) = refs[:-2], refs[-2:]
    wide = mid_ref.shape[2]
    shards, _, rows, _ = out_refs[0].shape

    def some_rows(step, carry):
        at = pl.multiple_of(step * STEP, STEP)
        for half in range(0, QUARTER, LANES):
            parts = [
                tuple(mid_ref[(a * QUARTER + half) // LANES, ri, pl.ds(at, STEP), :] for ri in range(2))
                for a in range(RADIX)
            ]
            mixed = radix_four(parts)
            for e in range(RADIX):
                for ri in range(2):
                    where = (e, pl.ds(at, STEP), pl.ds(ri * QUARTER + half, LANES))
                    store_split(coarse_ref, fine_ref, where, mixed[e][ri])
        return carry

    lax.fori_loop(0, wide // STEP, some_rows, 0)
    some = rows // RADIX
    for e in range(RADIX):
        value = triple_dot(matrix_ref, e, coarse_ref[e], fine_ref[e], ((1,), (1,)))
        for f in range(shards):
            for part, out_ref in enumerate(out_refs):
                at = (f * len(out_refs) + part) * some
                for tile in range(wide // LANES):
                    out_ref[f, tile, pl.ds(e, some, stride=RADIX), :] = value[
                        at : at + some, tile * LANES : (tile + 1) * LANES
                    ]


def part_kernel(in_ref, out_ref):
    members, tiles, rows, _ = out_ref.shape
    flat_ref = out_ref.reshape(members * tiles * rows, LANES)
    for r in range(rows):
        for tile in range(tiles):
            at = (r * tiles + tile) * LANES
            flat_ref[pl.ds(tile * rows + r, members, stride=tiles * rows), :] = in_ref[:, at : at + LANES]


def join_kernel(extra, in_ref, *refs):
    out_refs = refs[-2:] if extra else refs[-1:]
    members, tiles, rows, _ = in_ref.shape
    flat_ref = in_ref.reshape(members * tiles * rows, LANES)
    for r in range(rows):
        for tile in range(tiles):
            at = (r * tiles + tile) * LANES
            value = flat_ref[pl.ds(tile * rows + r, members, stride=tiles * rows), :]
            for out_ref in out_refs:
                out_ref[0, :, at : at + LANES] = value


def mirror_kernel(base_ref, own_ref, far_ref, edge_ref, out_ref):
    members, length = own_ref.shape
    tiles = length // LANES - 1
    shape = (members, LANES)
    lane = lax.broadcasted_iota(jnp.int32, shape, 1)
    mirror = (LANES - lane) % LANES
    first_group, last_group = base_ref[1] == 0, base_ref[1] == base_ref[2] - 1
    beyond = own_ref[:, tiles * LANES :]
    scale = jnp.broadcast_to(beyond[:, 1:2], shape)
    exponent = jnp.broadcast_to(beyond[:, 2:3], shape)
    half_root = math.sqrt(0.5)

    def tile_of(ref, tile):
        return ref[:, pl.ds(pl.multiple_of(tile * LANES, LANES), LANES)]

    def turned(value):
        return jnp.take_along_axis(value, mirror, axis=1, mode="promise_in_bounds")

    def store(tile, own, far, weight):
        offset = base_ref[0] + tile * LANES + lane
        near = left_lines(own, offset.astype(jnp.float32), scale, exponent)
        far_offset = jnp.where(offset == 0, 0, OUTER * INNER - offset)
        back = left_lines(far, far_offset.astype(jnp.float32), scale, exponent)
        at = pl.ds(pl.multiple_of(tile * LANES, LANES), LANES)
        out_ref[0, :, at] = (near[0] + back[0]) * weight
        out_ref[1, :, at] = (near[1] - back[1]) * weight

    def one_tile(tile, last):
        ahead = turned(tile_of(far_ref, tiles - 1 - tile))
        is_edge = (lane == 0) & (tile == 0) & first_group
        store(tile, tile_of(own_ref, tile), jnp.where(lane == 0, last, ahead), jnp.where(is_edge, half_root, 1.0))
        return ahead

    start = jnp.where(first_group, turned(edge_ref[...]), turned(tile_of(far_ref, tiles)))
    last = lax.fori_loop(0, tiles, one_tile, start)
    lone = (lane == 0) & last_group
    store(tiles, jnp.where(lone, beyond, 0.0), jnp.where(lone, last, 0.0), jnp.where(lone, half_root, 0.0))


def limits():
    return pltpu.CompilerParams(vmem_limit_bytes=VMEM_LIMIT)


def part_call(phase):
    members, length = phase.shape
    rows = length // INNER
    tiles = INNER // LANES
    return pl.pallas_call(
        part_kernel,
        grid=(rows // BLOCK_ROWS,),
        in_specs=[pl.BlockSpec((members, BLOCK_ROWS * INNER), lambda g: (0, g))],
        out_specs=pl.BlockSpec((members, tiles, BLOCK_ROWS, LANES), lambda g: (0, 0, g, 0)),
        out_shape=pltpu.HBM((members, tiles, rows, LANES), jnp.float32),
        compiler_params=limits(),
        cost_estimate=pl.CostEstimate(flops=0, bytes_accessed=8 * members * length, transcendentals=0),
    )(pltpu.with_memory_space_constraint(phase, pltpu.HBM))


def join_call(piece, track, within, length, groups, so_far):
    members, tiles, rows, _ = piece.shape
    stretch = rows * INNER
    steps = rows // BLOCK_ROWS
    operands = (piece,) if so_far is None else (piece, so_far)
    each = max(steps // max(groups, 1), 1)
    return pl.pallas_call(
        functools.partial(join_kernel, groups > 0),
        grid=(steps,),
        in_specs=[
            pl.BlockSpec((members, tiles, BLOCK_ROWS, LANES), lambda g: (0, 0, g, 0)),
            pl.BlockSpec(memory_space=pl.ANY),
        ][: len(operands)],
        out_specs=[
            pl.BlockSpec((1, members, BLOCK_ROWS * INNER), lambda g: (track, 0, within * steps + g)),
            pl.BlockSpec((1, members, BLOCK_ROWS * INNER), lambda g: (g // each, 0, g % each)),
        ][: 2 if groups else 1],
        out_shape=[
            jax.ShapeDtypeStruct((2, members, length), jnp.float32),
            jax.ShapeDtypeStruct((max(groups, 1), members, stretch // max(groups, 1)), jnp.float32),
        ][: 2 if groups else 1],
        input_output_aliases={} if so_far is None else {1: 0},
        compiler_params=limits(),
        cost_estimate=pl.CostEstimate(flops=0, bytes_accessed=12 * members * stretch, transcendentals=0),
    )(*operands)


def outer_call(params, phase, kept, matrices, twists):
    track = 1 if kept else 0
    sources, tiles, rows, _ = phase.shape
    some = OUTER_TILES
    lines = pl.BlockSpec((sources, some, rows, LANES), lambda g: (0, g, 0, 0))
    more = 0 if kept else 3
    return pl.pallas_call(
        functools.partial(outer_kernel, track),
        grid=(tiles // some,),
        in_specs=[pl.BlockSpec(memory_space=pltpu.SMEM)]
        + [lines] * (1 + len(kept))
        + [
            pl.BlockSpec(matrices.shape, lambda g: (0, 0, 0, 0)),
            pl.BlockSpec((2, RADIX, QUARTER, some * LANES), lambda g: (0, 0, 0, g)),
        ],
        out_specs=[pl.BlockSpec((some, 2, OUTER, LANES), lambda g: (g, 0, 0, 0))] + [lines] * more,
        out_shape=[jax.ShapeDtypeStruct((tiles, 2, OUTER, LANES), jnp.float32)]
        + [jax.ShapeDtypeStruct(phase.shape, jnp.float32)] * more,
        scratch_shapes=[pltpu.VMEM((RADIX, 2 * QUARTER, some * LANES), jnp.bfloat16)] * 2,
        compiler_params=limits(),
        cost_estimate=pl.CostEstimate(
            flops=24 * OUTER * QUARTER * INNER, bytes_accessed=32 * OUTER * INNER, transcendentals=0
        ),
    )(params, phase, *kept, matrices, twists)


def inner_call(mid, matrices, shards, parts):
    rows = INNER // shards // parts
    tiles = OUTER // LANES
    return pl.pallas_call(
        inner_kernel,
        grid=(OUTER // WIDE,),
        in_specs=[
            pl.BlockSpec((INNER // LANES, 2, WIDE, LANES), lambda g: (0, 0, g, 0)),
            pl.BlockSpec(matrices.shape, lambda g: (0, 0, 0, 0)),
        ],
        out_specs=[pl.BlockSpec((shards, WIDE // LANES, rows, LANES), lambda g: (0, g, 0, 0))] * parts,
        out_shape=[pltpu.HBM((shards, tiles, rows, LANES), jnp.float32)] * parts,
        scratch_shapes=[pltpu.VMEM((RADIX, WIDE, 2 * QUARTER), jnp.bfloat16)] * 2,
        compiler_params=limits(),
        cost_estimate=pl.CostEstimate(
            flops=12 * OUTER * QUARTER * INNER, bytes_accessed=12 * OUTER * INNER, transcendentals=0
        ),
    )(mid, matrices)


def mirror_call(base, own, far, edge):
    members, length = own.shape
    return pl.pallas_call(
        mirror_kernel,
        in_specs=[pl.BlockSpec(memory_space=pltpu.SMEM)] + [pl.BlockSpec(memory_space=pltpu.VMEM)] * 3,
        out_specs=pl.BlockSpec(memory_space=pltpu.VMEM),
        out_shape=jax.ShapeDtypeStruct((2, members, length), jnp.float32),
        compiler_params=limits(),
        cost_estimate=pl.CostEstimate(
            flops=200 * members * length, bytes_accessed=16 * members * length, transcendentals=0
        ),
    )(base, own, far, edge)


def line_params(roughness, waviness, coherence):
    return jnp.stack(
        [jnp.sqrt(2.0 * roughness * (waviness - 1.0) / ANCHOR), -0.5 * waviness, 1.0 / coherence]
    )


def to_group(piece, slot):
    groups = lax.axis_size("mem")
    return lax.ppermute(piece, "mem", [(z, z ^ slot) for z in range(groups)]) if slot else piece


def rows_gram(rows):
    return lax.dot_general(rows, rows, (((1,), (1,)), ((), ())), precision=highest)


def slot_rows(stretches, groups):
    my_group = lax.axis_index("mem")
    return [
        to_group(lax.dynamic_index_in_dim(stretches, my_group ^ slot, 0, keepdims=False), slot)
        for slot in range(groups)
    ]


def own_and_far(phase, params, my_group):
    groups = lax.axis_size("mem")
    half = phase.shape[1] // 2
    width = half // groups
    lane = lax.broadcasted_iota(jnp.int32, (phase.shape[0], LANES), 1)

    def lines(start):
        return (
            lax.dynamic_slice_in_dim(phase, start, width, 1),
            lax.dynamic_slice_in_dim(phase, start + width, LANES, 1),
        )

    own, far = [], []
    for slot in range(groups):
        group = my_group ^ slot
        inner, beyond = lines(group * width)
        for n in range(2):
            beyond = jnp.where(lane == n + 1, params[n][:, None], beyond)
        far_inner, far_beyond = lines(half + (groups - 1 - group) * width)
        message = jnp.concatenate(
            [
                jnp.concatenate([inner, beyond], axis=1)[None],
                jnp.concatenate([far_inner, far_beyond], axis=1)[None],
            ]
        )
        message = to_group(message, slot)
        own.append(message[0])
        far.append(message[1])
    return jnp.concatenate(own, axis=0), jnp.concatenate(far, axis=0)


def edge_of(own):
    shards = lax.axis_size("len")
    return lax.ppermute(own[:, :LANES], "len", [(d, (shards - d) % shards) for d in range(shards)])


def across(far):
    shards = lax.axis_size("len")
    return lax.ppermute(far, "len", [(d, shards - 1 - d) for d in range(shards)])


def lines_gram(own, far, edge):
    groups = lax.axis_size("mem")
    my_index, my_group = lax.axis_index("len"), lax.axis_index("mem")
    width = own.shape[1] - LANES
    base = (my_index * (2 * groups) + my_group) * width
    base = jnp.stack([base, my_group, jnp.full_like(my_group, groups)]).astype(jnp.int32)
    sums = mirror_call(base, own, far, edge)
    return rows_gram(sums[0]) + rows_gram(sums[1])


def in_order(gram_matrix, members):
    my_group = lax.axis_index("mem")
    row = lax.broadcasted_iota(jnp.int32, gram_matrix.shape, 0)
    column = lax.broadcasted_iota(jnp.int32, gram_matrix.shape, 1)
    to_slot = (row % members == column % members) & ((row // members) ^ my_group == column // members)
    to_slot = to_slot.astype(jnp.float32)
    return jnp.dot(jnp.dot(to_slot, gram_matrix, precision=highest), to_slot.T, precision=highest)


def summed(value):
    for axis in ("len", "mem"):
        value = jnp.sum(lax.all_gather(value, axis), axis=0)
    return value


def per_device_whole(phase_left, phase_right, roughness, waviness, coherence):
    shards, groups = lax.axis_size("len"), lax.axis_size("mem")
    my_index = lax.axis_index("len")
    members = phase_left.shape[0]

    def swap(piece):
        return lax.all_to_all(piece, "len", split_axis=0, concat_axis=0, tiled=True)

    all_params = line_params(roughness, waviness, coherence)
    params = lax.dynamic_index_in_dim(all_params, my_index, 1, keepdims=False)
    outer_tables = jnp.asarray(outer_matrices())
    inner_tables = jnp.asarray(inner_matrices())
    twists = jnp.asarray(twist_tables())
    local_len = phase_left.shape[1]

    left, right = part_call(phase_left), part_call(phase_right)
    right, my_group = lax.optimization_barrier((right, lax.axis_index("mem")))
    left, right = swap(left), swap(right)
    own, far = own_and_far(phase_left, all_params, my_group)
    mid, *kept = outer_call(params, left, (), outer_tables, twists)
    first = list(inner_call(mid, inner_tables, shards, 2))
    right, *first = lax.optimization_barrier((right, *first))
    early = swap(first[0])
    (mid,) = outer_call(params, right, kept, outer_tables, twists)
    (second,) = inner_call(mid, inner_tables, shards, 1)
    early, second = lax.optimization_barrier((early, second))
    second = swap(second)
    second, first[1], own, far = lax.optimization_barrier((second, first[1], own, far))
    profile, points = join_call(second, 1, 0, local_len, groups, None)
    late = swap(first[1])
    line_gram = lines_gram(own, across(far), edge_of(own))
    (profile,) = join_call(early, 0, 0, local_len, 0, profile)
    late, line_gram = lax.optimization_barrier((late, line_gram))
    (profile,) = join_call(late, 0, 1, local_len, 0, profile)
    rows = slot_rows(points, groups)
    profile, line_gram, rows = lax.optimization_barrier((profile, line_gram, rows))
    gram_matrix = 0.25 * line_gram + (0.5 / (OUTER * INNER)) * rows_gram(jnp.concatenate(rows, axis=0))
    return (profile, upper_of(summed(in_order(gram_matrix, members))))


def per_device(phase_left, phase_right, roughness, waviness, coherence):
    whole_members = phase_left.shape[0] == lax.axis_size("len") and lax.axis_size("mem") in (2, 4)
    form = per_device_whole if whole_members else per_device_spread
    return form(phase_left, phase_right, roughness, waviness, coherence)


def solution(mesh):
    placed = (P("mem", "len"), P("mem", "len"), P("mem"), P("mem"), P("mem"))
    return jax.shard_map(
        per_device,
        mesh=mesh,
        in_specs=placed,
        out_specs=(P(None, "mem", "len"), P()),
        check_vma=False,
    )
```

```python
import functools
import math

import jax
import jax.numpy as jnp
import numpy as np
from jax import lax
from jax.experimental import pallas as pl
from jax.experimental.pallas import tpu as pltpu
from jax.sharding import PartitionSpec as P

OUTER = 1024
INNER = 1024
ANCHOR = 64
RADIX = 4
QUARTER = 256
LANES = 128
STEP = 16
IN_PARTS = 2
SUBLANES = 8
WIDE = 256
BLOCK_ROWS = 16
OUTER_TILES = 2
VMEM_LIMIT = 48 * 1024 * 1024
SIN_HALF = (0.49999999785787, -0.02083332246218, 2.604078316692e-4, -1.547581723527e-6, 5.088214043e-9)
COS_HALF = (
    0.99999999977982,
    -0.12499999839235,
    2.604164763023e-3,
    -2.170056380508e-5,
    9.67192778775e-8,
    -2.5440497557e-10,
)


highest = lax.Precision.HIGHEST


def merged(shard, axis, combine):
    everything = lax.all_gather(shard, axis)
    leading = everything[0]

    def step(k, so_far):
        return combine(so_far, everything[k])

    return lax.fori_loop(1, lax.axis_size(axis), step, leading)


def dft_tables(length):
    index = lax.iota(jnp.int32, length)
    product = index[:, None] * index[None, :] % length
    phase_angle = product.astype(jnp.float32) * (2.0 * math.pi / length)
    return (jnp.cos(phase_angle), jnp.sin(phase_angle))


def spectra_of(phase_left, phase_right, roughness, waviness, coherence, freq):
    amplitude = jnp.sqrt(2.0 * roughness * (waviness - 1.0) / ANCHOR)[:, None] * (
        (freq + ANCHOR) / ANCHOR
    ) ** (-0.5 * waviness[:, None])
    freq_ratio = freq / coherence[:, None]
    coherent = 1.0 / (1.0 + freq_ratio * freq_ratio)
    incoherent = freq_ratio * jnp.sqrt(2.0 + freq_ratio * freq_ratio) * coherent
    cos_left = jnp.cos(phase_left)
    sin_left = jnp.sin(phase_left)
    cos_right = jnp.cos(phase_right)
    sin_right = jnp.sin(phase_right)
    real_part = jnp.stack(
        [amplitude * cos_left, amplitude * (coherent * cos_left + incoherent * cos_right)]
    )
    imag_part = jnp.stack(
        [amplitude * sin_left, amplitude * (coherent * sin_left + incoherent * sin_right)]
    )
    return (real_part, imag_part)


def upper_of(gram_matrix):
    return jnp.linalg.cholesky(gram_matrix).T


def combine_factors(upper_a, upper_b):
    gram_matrix = jnp.dot(upper_a.T, upper_a, precision=highest) + jnp.dot(
        upper_b.T, upper_b, precision=highest
    )
    return upper_of(gram_matrix)


def gram_of(snapshot):
    return jnp.einsum("tmr,tnr->mn", snapshot, snapshot, precision=highest)


def per_device_spread(phase_left, phase_right, roughness, waviness, coherence):
    shards = lax.axis_size("len")
    my_index = lax.axis_index("len")
    local_members, local_len = phase_left.shape
    columns = 2 * local_members
    outer_block = OUTER // shards
    inner_block = INNER // shards

    def to_rows(part):
        shaped = part.reshape(2, local_members, inner_block, OUTER)
        return jnp.transpose(shaped, (2, 3, 0, 1)).reshape(
            inner_block, shards, outer_block * columns
        )

    inner_cos, inner_sin = dft_tables(INNER)
    freq = (my_index * local_len + lax.iota(jnp.int32, local_len)).astype(jnp.float32)[None, :]
    real_part, imag_part = spectra_of(phase_left, phase_right, roughness, waviness, coherence, freq)
    pieces = (
        lax.all_to_all(to_rows(real_part), "len", split_axis=1, concat_axis=0, tiled=True),
        lax.all_to_all(to_rows(imag_part), "len", split_axis=1, concat_axis=0, tiled=True),
    )
    real_in = pieces[0].reshape(INNER, -1)
    imag_in = pieces[1].reshape(INNER, -1)
    real_out = jnp.dot(inner_cos, real_in, precision=highest) - jnp.dot(
        inner_sin, imag_in, precision=highest
    )
    imag_out = jnp.dot(inner_cos, imag_in, precision=highest) + jnp.dot(
        inner_sin, real_in, precision=highest
    )
    row_index = lax.iota(jnp.int32, INNER)[:, None]
    outer_index = (my_index * outer_block + lax.iota(jnp.int32, outer_block))[None, :]
    twist = (row_index * outer_index % (OUTER * INNER)).astype(jnp.float32) * (
        2.0 * math.pi / (OUTER * INNER)
    )
    twist_cos = jnp.repeat(jnp.cos(twist), columns, axis=1)
    twist_sin = jnp.repeat(jnp.sin(twist), columns, axis=1)
    rot_real = (real_out * twist_cos - imag_out * twist_sin).reshape(
        shards, inner_block, outer_block * columns
    )
    rot_imag = (real_out * twist_sin + imag_out * twist_cos).reshape(
        shards, inner_block, outer_block * columns
    )
    outer_cos, outer_sin = dft_tables(OUTER)
    outer_cos = outer_cos.reshape(OUTER, shards, outer_block)
    outer_sin = outer_sin.reshape(OUTER, shards, outer_block)
    pieces = (
        lax.all_to_all(rot_real, "len", split_axis=0, concat_axis=0, tiled=True),
        lax.all_to_all(rot_imag, "len", split_axis=0, concat_axis=0, tiled=True),
    )
    item_count = pieces[0].shape[1]
    real_in = pieces[0].reshape(shards, item_count, outer_block, columns)
    imag_in = pieces[1].reshape(shards, item_count, outer_block, columns)
    first = jnp.einsum("jqa,qiac->cij", outer_cos, real_in, precision=highest)
    second = jnp.einsum("jqa,qiac->cij", outer_sin, imag_in, precision=highest)
    profile_block = first - second
    outgoing = jnp.transpose(
        profile_block.reshape(columns, inner_block, shards, outer_block), (2, 0, 1, 3)
    ).reshape(shards, -1)
    arrived = lax.all_to_all(outgoing, "len", split_axis=0, concat_axis=0, tiled=True)
    profile = jnp.transpose(
        arrived.reshape(shards, columns, inner_block, outer_block), (1, 3, 0, 2)
    ).reshape(2, local_members, local_len)
    scale = 1.0 / math.sqrt(2.0 * OUTER * INNER)
    snapshot = profile_block.reshape(2, local_members, inner_block * OUTER) * scale
    gathered = lax.all_gather(snapshot, "mem", axis=1, tiled=True)
    gram_local = gram_of(gathered)
    r_factor = merged(upper_of(gram_local), "len", combine_factors)
    return (profile, r_factor)


def host_cis(product, period):
    angle = product % period * (2.0 * np.pi / period)
    return np.cos(angle), np.sin(angle)


def split_host(table):
    coarse = table.astype(np.float32).astype(jnp.bfloat16)
    fine = (table - coarse.astype(np.float64)).astype(np.float32).astype(jnp.bfloat16)
    return np.stack([coarse, fine])


def outer_matrices():
    c, e, b = np.arange(QUARTER), np.arange(RADIX), np.arange(QUARTER)
    cos_part, sin_part = host_cis((RADIX * c[None, :, None] + e[:, None, None]) * b[None, None, :], OUTER)
    upper = np.concatenate([cos_part, -sin_part], axis=2)
    lower = np.concatenate([sin_part, cos_part], axis=2)
    return split_host(np.concatenate([upper, lower], axis=1))


def inner_matrices():
    c, e, b = np.arange(QUARTER), np.arange(RADIX), np.arange(QUARTER)
    cos_part, sin_part = host_cis((RADIX * c[None, :, None] + e[:, None, None]) * b[None, None, :], INNER)
    return split_host(np.concatenate([cos_part, -sin_part], axis=2))


def twist_tables():
    j1 = RADIX * np.arange(QUARTER)[None, :, None] + np.arange(RADIX)[:, None, None]
    cos_part, sin_part = host_cis(j1 * np.arange(INNER)[None, None, :], OUTER * INNER)
    return np.stack([cos_part, sin_part]).astype(np.float32)


def sin_cos(angle):
    square = angle * angle

    def series(coefficients):
        total = jnp.float32(coefficients[-1])
        for coefficient in coefficients[-2::-1]:
            total = total * square + jnp.float32(coefficient)
        return total

    half_sin = angle * series(SIN_HALF)
    half_cos = series(COS_HALF)
    twice = half_sin + half_sin
    return twice * half_cos, 1.0 - twice * half_sin


def amplitude_of(freq, scale, exponent):
    return scale * jnp.exp2(exponent * jnp.log2((freq + ANCHOR) * (1.0 / ANCHOR)))


def left_lines(left, freq, scale, exponent):
    amplitude = amplitude_of(freq, scale, exponent)
    sin_left, cos_left = sin_cos(left)
    return amplitude * cos_left, amplitude * sin_left


def radix_four(parts):
    (r0, i0), (r1, i1), (r2, i2), (r3, i3) = parts
    even_sum, even_gap = (r0 + r2, i0 + i2), (r0 - r2, i0 - i2)
    odd_sum, odd_gap = (r1 + r3, i1 + i3), (r1 - r3, i1 - i3)
    return (
        (even_sum[0] + odd_sum[0], even_sum[1] + odd_sum[1]),
        (even_gap[0] - odd_gap[1], even_gap[1] + odd_gap[0]),
        (even_sum[0] - odd_sum[0], even_sum[1] - odd_sum[1]),
        (even_gap[0] + odd_gap[1], even_gap[1] - odd_gap[0]),
    )


def store_split(coarse_ref, fine_ref, where, value):
    coarse = value.astype(jnp.bfloat16)
    coarse_ref[where] = coarse
    fine_ref[where] = (value - coarse.astype(jnp.float32)).astype(jnp.bfloat16)


def triple_dot(matrix_ref, e, coarse, fine, dims):
    def product(a, b):
        return lax.dot_general(a, b, (dims, ((), ())), preferred_element_type=jnp.float32)

    return product(matrix_ref[0, e], coarse) + (
        product(matrix_ref[0, e], fine) + product(matrix_ref[1, e], coarse)
    )


def first_lines(params_ref, left_ref, kept_refs, where, freq):
    scale, exponent, inverse_coherence = params_ref[0], params_ref[1], params_ref[2]
    amplitude = amplitude_of(freq, scale, exponent)
    freq_ratio = freq * inverse_coherence
    ratio_square = freq_ratio * freq_ratio
    coherent = 1.0 / (1.0 + ratio_square)
    incoherent = freq_ratio * jnp.sqrt(2.0 + ratio_square) * coherent
    sin_left, cos_left = sin_cos(left_ref[where])
    real, imag = amplitude * cos_left, amplitude * sin_left
    kept_refs[0][where] = coherent * real
    kept_refs[1][where] = coherent * imag
    kept_refs[2][where] = amplitude * incoherent
    return real, imag


def second_lines(right_ref, kept_refs, where):
    sin_right, cos_right = sin_cos(right_ref[where])
    independent = kept_refs[2][where]
    return (
        kept_refs[0][where] + independent * cos_right,
        kept_refs[1][where] + independent * sin_right,
    )


def outer_kernel(track, params_ref, phase_ref, *refs):
    if track == 0:
        matrix_ref, twist_ref, out_ref, *kept_refs, coarse_ref, fine_ref = refs
    else:
        *kept_refs, matrix_ref, twist_ref, out_ref, coarse_ref, fine_ref = refs
    _, tiles, rows, _ = phase_ref.shape
    lane = lax.broadcasted_iota(jnp.int32, (STEP, LANES), 1) + pl.program_id(0) * tiles * LANES
    row = lax.broadcasted_iota(jnp.int32, (STEP, LANES), 0)
    place = row * INNER + lane

    def some_rows(step, carry):
        b = step * STEP
        for tile in range(tiles):
            lines = []
            for a in range(RADIX):
                k1 = a * QUARTER + b
                where = (k1 // rows, tile, pl.ds(pl.multiple_of(k1 % rows, STEP), STEP))
                if track == 0:
                    freq = (place + (k1 * INNER + tile * LANES)).astype(jnp.float32)
                    lines.append(first_lines(params_ref, phase_ref, kept_refs, where, freq))
                else:
                    lines.append(second_lines(phase_ref, kept_refs, where))
            mixed = radix_four(lines)
            for e in range(RADIX):
                for ri in range(2):
                    at = pl.ds(pl.multiple_of(ri * QUARTER + b, STEP), STEP)
                    where = (e, at, pl.ds(tile * LANES, LANES))
                    store_split(coarse_ref, fine_ref, where, mixed[e][ri])
        return carry

    lax.fori_loop(0, QUARTER // STEP, some_rows, 0)
    for e in range(RADIX):
        mid = triple_dot(matrix_ref, e, coarse_ref[e], fine_ref[e], ((1,), (0,)))
        for tile in range(tiles):
            lanes = slice(tile * LANES, (tile + 1) * LANES)
            cos_part, sin_part = twist_ref[0, e, :, lanes], twist_ref[1, e, :, lanes]
            real, imag = mid[:QUARTER, lanes], mid[QUARTER:, lanes]
            out_ref[tile, 0, pl.ds(e, QUARTER, stride=RADIX), :] = real * cos_part - imag * sin_part
            out_ref[tile, 1, pl.ds(e, QUARTER, stride=RADIX), :] = real * sin_part + imag * cos_part


def inner_kernel(*refs):
    mid_refs, (matrix_ref, out_ref, coarse_ref, fine_ref) = refs[:-4], refs[-4:]
    some, _, wide, _ = mid_refs[0].shape
    shards, _, rows, _ = out_ref.shape

    def some_rows(step, carry):
        at = pl.multiple_of(step * STEP, STEP)
        for half in range(0, QUARTER, LANES):
            tiles = [(a * QUARTER + half) // LANES for a in range(RADIX)]
            parts = [
                tuple(mid_refs[tile // some][tile % some, ri, pl.ds(at, STEP), :] for ri in range(2))
                for tile in tiles
            ]
            mixed = radix_four(parts)
            for e in range(RADIX):
                for ri in range(2):
                    where = (e, pl.ds(at, STEP), pl.ds(ri * QUARTER + half, LANES))
                    store_split(coarse_ref, fine_ref, where, mixed[e][ri])
        return carry

    lax.fori_loop(0, wide // STEP, some_rows, 0)
    each = rows // RADIX
    for e in range(RADIX):
        value = triple_dot(matrix_ref, e, coarse_ref[e], fine_ref[e], ((1,), (1,)))
        for f in range(shards):
            for tile in range(wide // LANES):
                out_ref[f, tile, pl.ds(e, each, stride=RADIX), :] = value[
                    f * each : (f + 1) * each, tile * LANES : (tile + 1) * LANES
                ]


def part_kernel(in_ref, *out_refs):
    members, some, rows, _ = out_refs[0].shape
    tiles = some * len(out_refs)
    for tile in range(tiles):
        out_ref = out_refs[tile // some]
        for start in range(0, rows, SUBLANES):
            columns = [((start + r) * tiles + tile) * LANES for r in range(SUBLANES)]
            turned = jnp.transpose(jnp.stack([in_ref[:, at : at + LANES] for at in columns]), (1, 0, 2))
            for m in range(members):
                out_ref[m, tile % some, start : start + SUBLANES, :] = turned[m]


def join_kernel(extra, in_ref, *refs):
    out_refs = refs[-2:] if extra else refs[-1:]
    members, tiles, rows, _ = in_ref.shape
    for tile in range(tiles):
        for start in range(0, rows, SUBLANES):
            turned = jnp.transpose(in_ref[:, tile, start : start + SUBLANES, :], (1, 0, 2))
            for r in range(SUBLANES):
                at = ((start + r) * tiles + tile) * LANES
                for out_ref in out_refs:
                    out_ref[0, :, at : at + LANES] = turned[r]


def mirror_kernel(base_ref, own_ref, far_ref, edge_ref, out_ref):
    members, length = own_ref.shape
    tiles = length // LANES - 1
    shape = (members, LANES)
    lane = lax.broadcasted_iota(jnp.int32, shape, 1)
    mirror = (LANES - lane) % LANES
    first_group, last_group = base_ref[1] == 0, base_ref[1] == base_ref[2] - 1
    beyond = own_ref[:, tiles * LANES :]
    scale = jnp.broadcast_to(beyond[:, 1:2], shape)
    exponent = jnp.broadcast_to(beyond[:, 2:3], shape)
    half_root = math.sqrt(0.5)

    def tile_of(ref, tile):
        return ref[:, pl.ds(pl.multiple_of(tile * LANES, LANES), LANES)]

    def turned(value):
        return jnp.take_along_axis(value, mirror, axis=1, mode="promise_in_bounds")

    def store(tile, own, far, weight):
        offset = base_ref[0] + tile * LANES + lane
        near = left_lines(own, offset.astype(jnp.float32), scale, exponent)
        far_offset = jnp.where(offset == 0, 0, OUTER * INNER - offset)
        back = left_lines(far, far_offset.astype(jnp.float32), scale, exponent)
        at = pl.ds(pl.multiple_of(tile * LANES, LANES), LANES)
        out_ref[0, :, at] = (near[0] + back[0]) * weight
        out_ref[1, :, at] = (near[1] - back[1]) * weight

    def one_tile(tile, last):
        ahead = turned(tile_of(far_ref, tiles - 1 - tile))
        is_edge = (lane == 0) & (tile == 0) & first_group
        store(tile, tile_of(own_ref, tile), jnp.where(lane == 0, last, ahead), jnp.where(is_edge, half_root, 1.0))
        return ahead

    start = jnp.where(first_group, turned(edge_ref[...]), turned(tile_of(far_ref, tiles)))
    last = lax.fori_loop(0, tiles, one_tile, start)
    lone = (lane == 0) & last_group
    store(tiles, jnp.where(lone, beyond, 0.0), jnp.where(lone, last, 0.0), jnp.where(lone, half_root, 0.0))


def limits():
    return pltpu.CompilerParams(vmem_limit_bytes=VMEM_LIMIT)


def part_call(phase, parts):
    members, length = phase.shape
    rows = length // INNER
    tiles = INNER // LANES // parts
    return pl.pallas_call(
        part_kernel,
        grid=(rows // BLOCK_ROWS,),
        in_specs=[pl.BlockSpec((members, BLOCK_ROWS * INNER), lambda g: (0, g))],
        out_specs=[pl.BlockSpec((members, tiles, BLOCK_ROWS, LANES), lambda g: (0, 0, g, 0))] * parts,
        out_shape=[pltpu.HBM((members, tiles, rows, LANES), jnp.float32)] * parts,
        compiler_params=limits(),
        cost_estimate=pl.CostEstimate(flops=0, bytes_accessed=8 * members * length, transcendentals=0),
    )(pltpu.with_memory_space_constraint(phase, pltpu.HBM))


def join_call(piece, track, within, length, groups, so_far):
    members, tiles, rows, _ = piece.shape
    stretch = rows * INNER
    steps = rows // BLOCK_ROWS
    operands = (piece,) if so_far is None else (piece, so_far)
    each = max(steps // max(groups, 1), 1)
    return pl.pallas_call(
        functools.partial(join_kernel, groups > 0),
        grid=(steps,),
        in_specs=[
            pl.BlockSpec((members, tiles, BLOCK_ROWS, LANES), lambda g: (0, 0, g, 0)),
            pl.BlockSpec(memory_space=pl.ANY),
        ][: len(operands)],
        out_specs=[
            pl.BlockSpec((1, members, BLOCK_ROWS * INNER), lambda g: (track, 0, within * steps + g)),
            pl.BlockSpec((1, members, BLOCK_ROWS * INNER), lambda g: (g // each, 0, g % each)),
        ][: 2 if groups else 1],
        out_shape=[
            jax.ShapeDtypeStruct((2, members, length), jnp.float32),
            jax.ShapeDtypeStruct((max(groups, 1), members, stretch // max(groups, 1)), jnp.float32),
        ][: 2 if groups else 1],
        input_output_aliases={} if so_far is None else {1: 0},
        compiler_params=limits(),
        cost_estimate=pl.CostEstimate(flops=0, bytes_accessed=12 * members * stretch, transcendentals=0),
    )(*operands)


def outer_call(params, phase, kept, matrices, twists, part):
    track = 1 if kept else 0
    sources, tiles, rows, _ = phase.shape
    some = OUTER_TILES
    first = part * (tiles // some)

    def lines(first):
        return pl.BlockSpec((sources, some, rows, LANES), lambda g: (0, first + g, 0, 0))

    more = 0 if kept else 3
    return pl.pallas_call(
        functools.partial(outer_kernel, track),
        grid=(tiles // some,),
        in_specs=[pl.BlockSpec(memory_space=pltpu.SMEM), lines(0)]
        + [lines(first)] * len(kept)
        + [
            pl.BlockSpec(matrices.shape, lambda g: (0, 0, 0, 0)),
            pl.BlockSpec((2, RADIX, QUARTER, some * LANES), lambda g: (0, 0, 0, first + g)),
        ],
        out_specs=[pl.BlockSpec((some, 2, OUTER, LANES), lambda g: (g, 0, 0, 0))] + [lines(0)] * more,
        out_shape=[jax.ShapeDtypeStruct((tiles, 2, OUTER, LANES), jnp.float32)]
        + [pltpu.HBM(phase.shape, jnp.float32)] * more,
        scratch_shapes=[pltpu.VMEM((RADIX, 2 * QUARTER, some * LANES), jnp.bfloat16)] * 2,
        compiler_params=limits(),
        cost_estimate=pl.CostEstimate(
            flops=24 * OUTER * QUARTER * tiles * LANES,
            bytes_accessed=32 * OUTER * tiles * LANES,
            transcendentals=0,
        ),
    )(params, phase, *kept, matrices, twists)


def inner_call(mids, matrices, shards):
    rows = INNER // shards
    tiles = OUTER // LANES
    return pl.pallas_call(
        inner_kernel,
        grid=(OUTER // WIDE,),
        in_specs=[pl.BlockSpec((mid.shape[0], 2, WIDE, LANES), lambda g: (0, 0, g, 0)) for mid in mids]
        + [pl.BlockSpec(matrices.shape, lambda g: (0, 0, 0, 0))],
        out_specs=pl.BlockSpec((shards, WIDE // LANES, rows, LANES), lambda g: (0, g, 0, 0)),
        out_shape=pltpu.HBM((shards, tiles, rows, LANES), jnp.float32),
        scratch_shapes=[pltpu.VMEM((RADIX, WIDE, 2 * QUARTER), jnp.bfloat16)] * 2,
        compiler_params=limits(),
        cost_estimate=pl.CostEstimate(
            flops=12 * OUTER * QUARTER * INNER, bytes_accessed=12 * OUTER * INNER, transcendentals=0
        ),
    )(*mids, matrices)


def mirror_call(base, own, far, edge):
    members, length = own.shape
    return pl.pallas_call(
        mirror_kernel,
        in_specs=[pl.BlockSpec(memory_space=pltpu.SMEM)] + [pl.BlockSpec(memory_space=pltpu.VMEM)] * 3,
        out_specs=pl.BlockSpec(memory_space=pltpu.VMEM),
        out_shape=jax.ShapeDtypeStruct((2, members, length), jnp.float32),
        compiler_params=limits(),
        cost_estimate=pl.CostEstimate(
            flops=200 * members * length, bytes_accessed=16 * members * length, transcendentals=0
        ),
    )(base, own, far, edge)


def line_params(roughness, waviness, coherence):
    return jnp.stack(
        [jnp.sqrt(2.0 * roughness * (waviness - 1.0) / ANCHOR), -0.5 * waviness, 1.0 / coherence]
    )


def to_group(piece, slot):
    groups = lax.axis_size("mem")
    return lax.ppermute(piece, "mem", [(z, z ^ slot) for z in range(groups)]) if slot else piece


def rows_gram(rows, precision=highest):
    return lax.dot_general(rows, rows, (((1,), (1,)), ((), ())), precision=precision)


def slot_rows(stretches, groups):
    my_group = lax.axis_index("mem")
    return [
        to_group(lax.dynamic_index_in_dim(stretches, my_group ^ slot, 0, keepdims=False), slot)
        for slot in range(groups)
    ]


def own_and_far(phase, params, my_group):
    groups = lax.axis_size("mem")
    half = phase.shape[1] // 2
    width = half // groups
    lane = lax.broadcasted_iota(jnp.int32, (phase.shape[0], LANES), 1)

    def lines(start):
        return (
            lax.dynamic_slice_in_dim(phase, start, width, 1),
            lax.dynamic_slice_in_dim(phase, start + width, LANES, 1),
        )

    own, far = [], []
    for slot in range(groups):
        group = my_group ^ slot
        inner, beyond = lines(group * width)
        for n in range(2):
            beyond = jnp.where(lane == n + 1, params[n][:, None], beyond)
        far_inner, far_beyond = lines(half + (groups - 1 - group) * width)
        message = jnp.concatenate(
            [
                jnp.concatenate([inner, beyond], axis=1)[None],
                jnp.concatenate([far_inner, far_beyond], axis=1)[None],
            ]
        )
        message = to_group(message, slot)
        own.append(message[0])
        far.append(message[1])
    return jnp.concatenate(own, axis=0), jnp.concatenate(far, axis=0)


def edge_of(own):
    shards = lax.axis_size("len")
    return lax.ppermute(own[:, :LANES], "len", [(d, (shards - d) % shards) for d in range(shards)])


def across(far):
    shards = lax.axis_size("len")
    return lax.ppermute(far, "len", [(d, shards - 1 - d) for d in range(shards)])


def lines_gram(own, far, edge):
    groups = lax.axis_size("mem")
    my_index, my_group = lax.axis_index("len"), lax.axis_index("mem")
    width = own.shape[1] - LANES
    base = (my_index * (2 * groups) + my_group) * width
    base = jnp.stack([base, my_group, jnp.full_like(my_group, groups)]).astype(jnp.int32)
    sums = mirror_call(base, own, far, edge)
    return rows_gram(sums[0]) + rows_gram(sums[1])


def in_order(gram_matrix, members):
    my_group = lax.axis_index("mem")
    row = lax.broadcasted_iota(jnp.int32, gram_matrix.shape, 0)
    column = lax.broadcasted_iota(jnp.int32, gram_matrix.shape, 1)
    to_slot = (row % members == column % members) & ((row // members) ^ my_group == column // members)
    to_slot = to_slot.astype(jnp.float32)
    return jnp.dot(jnp.dot(to_slot, gram_matrix, precision=highest), to_slot.T, precision=highest)


def summed(value):
    for axis in ("len", "mem"):
        value = jnp.sum(lax.all_gather(value, axis), axis=0)
    return value


def per_device_whole(phase_left, phase_right, roughness, waviness, coherence):
    shards, groups = lax.axis_size("len"), lax.axis_size("mem")
    my_index = lax.axis_index("len")
    members = phase_left.shape[0]

    def swap(piece):
        return lax.all_to_all(piece, "len", split_axis=0, concat_axis=0, tiled=True)

    all_params = line_params(roughness, waviness, coherence)
    params = lax.dynamic_index_in_dim(all_params, my_index, 1, keepdims=False)
    outer_tables = jnp.asarray(outer_matrices())
    inner_tables = jnp.asarray(inner_matrices())
    twists = jnp.asarray(twist_tables())
    local_len = phase_left.shape[1]

    (left,), right = part_call(phase_left, 1), part_call(phase_right, IN_PARTS)
    right, my_group = lax.optimization_barrier((right, lax.axis_index("mem")))
    left, right = swap(left), [swap(piece) for piece in right]
    own, far = own_and_far(phase_left, all_params, my_group)
    mid, *kept = outer_call(params, left, (), outer_tables, twists, 0)
    first = inner_call([mid], inner_tables, shards)
    first, kept, right[0] = lax.optimization_barrier((first, kept, right[0]))
    mids = [outer_call(params, piece, kept, outer_tables, twists, n)[0] for n, piece in enumerate(right)]
    second = swap(inner_call(mids, inner_tables, shards))
    profile, points = join_call(second, 1, 0, local_len, groups, None)
    _, own, far = lax.optimization_barrier((points, own, far))
    rows = slot_rows(points, groups)
    far = across(far)
    edge = edge_of(own)
    far, first = lax.optimization_barrier((far, first))
    line_gram = lines_gram(own, far, edge)
    (profile,) = join_call(swap(first), 0, 0, local_len, 0, profile)
    profile, rows, line_gram = lax.optimization_barrier((profile, rows, line_gram))
    point_gram = rows_gram(jnp.concatenate(rows, axis=0), lax.Precision.HIGH)
    gram_matrix = 0.25 * line_gram + (0.5 / (OUTER * INNER)) * point_gram
    return (profile, upper_of(summed(in_order(gram_matrix, members))))


def per_device(phase_left, phase_right, roughness, waviness, coherence):
    whole_members = phase_left.shape[0] == lax.axis_size("len") and lax.axis_size("mem") in (2, 4)
    form = per_device_whole if whole_members else per_device_spread
    return form(phase_left, phase_right, roughness, waviness, coherence)


def solution(mesh):
    placed = (P("mem", "len"), P("mem", "len"), P("mem"), P("mem"), P("mem"))
    return jax.shard_map(
        per_device,
        mesh=mesh,
        in_specs=placed,
        out_specs=(P(None, "mem", "len"), P()),
        check_vma=False,
    )
```

```python
import functools
import math

import jax
import jax.numpy as jnp
import numpy as np
from jax import lax
from jax.experimental import pallas as pl
from jax.experimental.pallas import tpu as pltpu
from jax.sharding import PartitionSpec as P

OUTER = 1024
INNER = 1024
ANCHOR = 64
RADIX = 4
QUARTER = 256
LANES = 128
STEP = 16
SUBLANES = 8
WIDE = 256
BLOCK_ROWS = 16
OUTER_TILES = 2
VMEM_LIMIT = 48 * 1024 * 1024
SIN_HALF = (0.49999999785787, -0.02083332246218, 2.604078316692e-4, -1.547581723527e-6, 5.088214043e-9)
COS_HALF = (
    0.99999999977982,
    -0.12499999839235,
    2.604164763023e-3,
    -2.170056380508e-5,
    9.67192778775e-8,
    -2.5440497557e-10,
)


highest = lax.Precision.HIGHEST


def merged(shard, axis, combine):
    everything = lax.all_gather(shard, axis)
    leading = everything[0]

    def step(k, so_far):
        return combine(so_far, everything[k])

    return lax.fori_loop(1, lax.axis_size(axis), step, leading)


def dft_tables(length):
    index = lax.iota(jnp.int32, length)
    product = index[:, None] * index[None, :] % length
    phase_angle = product.astype(jnp.float32) * (2.0 * math.pi / length)
    return (jnp.cos(phase_angle), jnp.sin(phase_angle))


def spectra_of(phase_left, phase_right, roughness, waviness, coherence, freq):
    amplitude = jnp.sqrt(2.0 * roughness * (waviness - 1.0) / ANCHOR)[:, None] * (
        (freq + ANCHOR) / ANCHOR
    ) ** (-0.5 * waviness[:, None])
    freq_ratio = freq / coherence[:, None]
    coherent = 1.0 / (1.0 + freq_ratio * freq_ratio)
    incoherent = freq_ratio * jnp.sqrt(2.0 + freq_ratio * freq_ratio) * coherent
    cos_left = jnp.cos(phase_left)
    sin_left = jnp.sin(phase_left)
    cos_right = jnp.cos(phase_right)
    sin_right = jnp.sin(phase_right)
    real_part = jnp.stack(
        [amplitude * cos_left, amplitude * (coherent * cos_left + incoherent * cos_right)]
    )
    imag_part = jnp.stack(
        [amplitude * sin_left, amplitude * (coherent * sin_left + incoherent * sin_right)]
    )
    return (real_part, imag_part)


def upper_of(gram_matrix):
    return jnp.linalg.cholesky(gram_matrix).T


def combine_factors(upper_a, upper_b):
    gram_matrix = jnp.dot(upper_a.T, upper_a, precision=highest) + jnp.dot(
        upper_b.T, upper_b, precision=highest
    )
    return upper_of(gram_matrix)


def gram_of(snapshot):
    return jnp.einsum("tmr,tnr->mn", snapshot, snapshot, precision=highest)


def per_device_spread(phase_left, phase_right, roughness, waviness, coherence):
    shards = lax.axis_size("len")
    my_index = lax.axis_index("len")
    local_members, local_len = phase_left.shape
    columns = 2 * local_members
    outer_block = OUTER // shards
    inner_block = INNER // shards

    def to_rows(part):
        shaped = part.reshape(2, local_members, inner_block, OUTER)
        return jnp.transpose(shaped, (2, 3, 0, 1)).reshape(
            inner_block, shards, outer_block * columns
        )

    inner_cos, inner_sin = dft_tables(INNER)
    freq = (my_index * local_len + lax.iota(jnp.int32, local_len)).astype(jnp.float32)[None, :]
    real_part, imag_part = spectra_of(phase_left, phase_right, roughness, waviness, coherence, freq)
    pieces = (
        lax.all_to_all(to_rows(real_part), "len", split_axis=1, concat_axis=0, tiled=True),
        lax.all_to_all(to_rows(imag_part), "len", split_axis=1, concat_axis=0, tiled=True),
    )
    real_in = pieces[0].reshape(INNER, -1)
    imag_in = pieces[1].reshape(INNER, -1)
    real_out = jnp.dot(inner_cos, real_in, precision=highest) - jnp.dot(
        inner_sin, imag_in, precision=highest
    )
    imag_out = jnp.dot(inner_cos, imag_in, precision=highest) + jnp.dot(
        inner_sin, real_in, precision=highest
    )
    row_index = lax.iota(jnp.int32, INNER)[:, None]
    outer_index = (my_index * outer_block + lax.iota(jnp.int32, outer_block))[None, :]
    twist = (row_index * outer_index % (OUTER * INNER)).astype(jnp.float32) * (
        2.0 * math.pi / (OUTER * INNER)
    )
    twist_cos = jnp.repeat(jnp.cos(twist), columns, axis=1)
    twist_sin = jnp.repeat(jnp.sin(twist), columns, axis=1)
    rot_real = (real_out * twist_cos - imag_out * twist_sin).reshape(
        shards, inner_block, outer_block * columns
    )
    rot_imag = (real_out * twist_sin + imag_out * twist_cos).reshape(
        shards, inner_block, outer_block * columns
    )
    outer_cos, outer_sin = dft_tables(OUTER)
    outer_cos = outer_cos.reshape(OUTER, shards, outer_block)
    outer_sin = outer_sin.reshape(OUTER, shards, outer_block)
    pieces = (
        lax.all_to_all(rot_real, "len", split_axis=0, concat_axis=0, tiled=True),
        lax.all_to_all(rot_imag, "len", split_axis=0, concat_axis=0, tiled=True),
    )
    item_count = pieces[0].shape[1]
    real_in = pieces[0].reshape(shards, item_count, outer_block, columns)
    imag_in = pieces[1].reshape(shards, item_count, outer_block, columns)
    first = jnp.einsum("jqa,qiac->cij", outer_cos, real_in, precision=highest)
    second = jnp.einsum("jqa,qiac->cij", outer_sin, imag_in, precision=highest)
    profile_block = first - second
    outgoing = jnp.transpose(
        profile_block.reshape(columns, inner_block, shards, outer_block), (2, 0, 1, 3)
    ).reshape(shards, -1)
    arrived = lax.all_to_all(outgoing, "len", split_axis=0, concat_axis=0, tiled=True)
    profile = jnp.transpose(
        arrived.reshape(shards, columns, inner_block, outer_block), (1, 3, 0, 2)
    ).reshape(2, local_members, local_len)
    scale = 1.0 / math.sqrt(2.0 * OUTER * INNER)
    snapshot = profile_block.reshape(2, local_members, inner_block * OUTER) * scale
    gathered = lax.all_gather(snapshot, "mem", axis=1, tiled=True)
    gram_local = gram_of(gathered)
    r_factor = merged(upper_of(gram_local), "len", combine_factors)
    return (profile, r_factor)


def host_cis(product, period):
    angle = product % period * (2.0 * np.pi / period)
    return np.cos(angle), np.sin(angle)


def split_host(table):
    coarse = table.astype(np.float32).astype(jnp.bfloat16)
    fine = (table - coarse.astype(np.float64)).astype(np.float32).astype(jnp.bfloat16)
    return np.stack([coarse, fine])


def outer_matrices():
    c, e, b = np.arange(QUARTER), np.arange(RADIX), np.arange(QUARTER)
    cos_part, sin_part = host_cis((RADIX * c[None, :, None] + e[:, None, None]) * b[None, None, :], OUTER)
    upper = np.concatenate([cos_part, -sin_part], axis=2)
    lower = np.concatenate([sin_part, cos_part], axis=2)
    return split_host(np.concatenate([upper, lower], axis=1))


def inner_matrices():
    c, e, b = np.arange(QUARTER), np.arange(RADIX), np.arange(QUARTER)
    cos_part, sin_part = host_cis((RADIX * c[None, :, None] + e[:, None, None]) * b[None, None, :], INNER)
    return split_host(np.concatenate([cos_part, -sin_part], axis=2))


def twist_tables():
    j1 = RADIX * np.arange(QUARTER)[None, :, None] + np.arange(RADIX)[:, None, None]
    cos_part, sin_part = host_cis(j1 * np.arange(INNER)[None, None, :], OUTER * INNER)
    return np.stack([cos_part, sin_part]).astype(np.float32)


def sin_cos(angle):
    square = angle * angle

    def series(coefficients):
        total = jnp.float32(coefficients[-1])
        for coefficient in coefficients[-2::-1]:
            total = total * square + jnp.float32(coefficient)
        return total

    half_sin = angle * series(SIN_HALF)
    half_cos = series(COS_HALF)
    twice = half_sin + half_sin
    return twice * half_cos, 1.0 - twice * half_sin


def amplitude_of(freq, scale, exponent):
    return scale * jnp.exp2(exponent * jnp.log2((freq + ANCHOR) * (1.0 / ANCHOR)))


def left_lines(left, freq, scale, exponent):
    amplitude = amplitude_of(freq, scale, exponent)
    sin_left, cos_left = sin_cos(left)
    return amplitude * cos_left, amplitude * sin_left


def radix_four(parts):
    (r0, i0), (r1, i1), (r2, i2), (r3, i3) = parts
    even_sum, even_gap = (r0 + r2, i0 + i2), (r0 - r2, i0 - i2)
    odd_sum, odd_gap = (r1 + r3, i1 + i3), (r1 - r3, i1 - i3)
    return (
        (even_sum[0] + odd_sum[0], even_sum[1] + odd_sum[1]),
        (even_gap[0] - odd_gap[1], even_gap[1] + odd_gap[0]),
        (even_sum[0] - odd_sum[0], even_sum[1] - odd_sum[1]),
        (even_gap[0] + odd_gap[1], even_gap[1] - odd_gap[0]),
    )


def store_split(coarse_ref, fine_ref, where, value):
    coarse = value.astype(jnp.bfloat16)
    coarse_ref[where] = coarse
    fine_ref[where] = (value - coarse.astype(jnp.float32)).astype(jnp.bfloat16)


def triple_dot(matrix_ref, e, coarse, fine, dims):
    def product(a, b):
        return lax.dot_general(a, b, (dims, ((), ())), preferred_element_type=jnp.float32)

    return product(matrix_ref[0, e], coarse) + (
        product(matrix_ref[0, e], fine) + product(matrix_ref[1, e], coarse)
    )


def first_lines(params_ref, left_ref, kept_refs, where, freq):
    scale, exponent, inverse_coherence = params_ref[0], params_ref[1], params_ref[2]
    amplitude = amplitude_of(freq, scale, exponent)
    freq_ratio = freq * inverse_coherence
    ratio_square = freq_ratio * freq_ratio
    coherent = 1.0 / (1.0 + ratio_square)
    incoherent = freq_ratio * jnp.sqrt(2.0 + ratio_square) * coherent
    sin_left, cos_left = sin_cos(left_ref[where])
    real, imag = amplitude * cos_left, amplitude * sin_left
    kept_refs[0][where] = coherent * real
    kept_refs[1][where] = coherent * imag
    kept_refs[2][where] = amplitude * incoherent
    return real, imag


def second_lines(right_ref, kept_refs, where):
    sin_right, cos_right = sin_cos(right_ref[where])
    independent = kept_refs[2][where]
    return (
        kept_refs[0][where] + independent * cos_right,
        kept_refs[1][where] + independent * sin_right,
    )


def outer_kernel(track, params_ref, phase_ref, *refs):
    if track == 0:
        matrix_ref, twist_ref, out_ref, *kept_refs, coarse_ref, fine_ref = refs
    else:
        *kept_refs, matrix_ref, twist_ref, out_ref, coarse_ref, fine_ref = refs
    _, tiles, rows, _ = phase_ref.shape
    lane = lax.broadcasted_iota(jnp.int32, (STEP, LANES), 1) + pl.program_id(0) * tiles * LANES
    row = lax.broadcasted_iota(jnp.int32, (STEP, LANES), 0)
    place = row * INNER + lane

    def some_rows(step, carry):
        b = step * STEP
        for tile in range(tiles):
            lines = []
            for a in range(RADIX):
                k1 = a * QUARTER + b
                where = (k1 // rows, tile, pl.ds(pl.multiple_of(k1 % rows, STEP), STEP))
                if track == 0:
                    freq = (place + (k1 * INNER + tile * LANES)).astype(jnp.float32)
                    lines.append(first_lines(params_ref, phase_ref, kept_refs, where, freq))
                else:
                    lines.append(second_lines(phase_ref, kept_refs, where))
            mixed = radix_four(lines)
            for e in range(RADIX):
                for ri in range(2):
                    at = pl.ds(pl.multiple_of(ri * QUARTER + b, STEP), STEP)
                    where = (e, at, pl.ds(tile * LANES, LANES))
                    store_split(coarse_ref, fine_ref, where, mixed[e][ri])
        return carry

    lax.fori_loop(0, QUARTER // STEP, some_rows, 0)
    for e in range(RADIX):
        mid = triple_dot(matrix_ref, e, coarse_ref[e], fine_ref[e], ((1,), (0,)))
        for tile in range(tiles):
            lanes = slice(tile * LANES, (tile + 1) * LANES)
            cos_part, sin_part = twist_ref[0, e, :, lanes], twist_ref[1, e, :, lanes]
            real, imag = mid[:QUARTER, lanes], mid[QUARTER:, lanes]
            out_ref[tile, 0, pl.ds(e, QUARTER, stride=RADIX), :] = real * cos_part - imag * sin_part
            out_ref[tile, 1, pl.ds(e, QUARTER, stride=RADIX), :] = real * sin_part + imag * cos_part


def inner_kernel(mid_ref, matrix_ref, *refs):
    out_refs, (coarse_ref, fine_ref) = refs[:-2], refs[-2:]
    wide = mid_ref.shape[2]
    shards, _, rows, _ = out_refs[0].shape

    def some_rows(step, carry):
        at = pl.multiple_of(step * STEP, STEP)
        for half in range(0, QUARTER, LANES):
            parts = [
                tuple(mid_ref[(a * QUARTER + half) // LANES, ri, pl.ds(at, STEP), :] for ri in range(2))
                for a in range(RADIX)
            ]
            mixed = radix_four(parts)
            for e in range(RADIX):
                for ri in range(2):
                    where = (e, pl.ds(at, STEP), pl.ds(ri * QUARTER + half, LANES))
                    store_split(coarse_ref, fine_ref, where, mixed[e][ri])
        return carry

    lax.fori_loop(0, wide // STEP, some_rows, 0)
    some = rows // RADIX
    for e in range(RADIX):
        value = triple_dot(matrix_ref, e, coarse_ref[e], fine_ref[e], ((1,), (1,)))
        for f in range(shards):
            for part, out_ref in enumerate(out_refs):
                at = (f * len(out_refs) + part) * some
                for tile in range(wide // LANES):
                    out_ref[f, tile, pl.ds(e, some, stride=RADIX), :] = value[
                        at : at + some, tile * LANES : (tile + 1) * LANES
                    ]


def part_kernel(in_ref, out_ref):
    members, tiles, rows, _ = out_ref.shape
    for tile in range(tiles):
        for start in range(0, rows, SUBLANES):
            columns = [((start + r) * tiles + tile) * LANES for r in range(SUBLANES)]
            turned = jnp.transpose(jnp.stack([in_ref[:, at : at + LANES] for at in columns]), (1, 0, 2))
            for m in range(members):
                out_ref[m, tile, start : start + SUBLANES, :] = turned[m]


def join_kernel(extra, in_ref, *refs):
    out_refs = refs[-2:] if extra else refs[-1:]
    members, tiles, rows, _ = in_ref.shape
    for tile in range(tiles):
        for start in range(0, rows, SUBLANES):
            turned = jnp.transpose(in_ref[:, tile, start : start + SUBLANES, :], (1, 0, 2))
            for r in range(SUBLANES):
                at = ((start + r) * tiles + tile) * LANES
                for out_ref in out_refs:
                    out_ref[0, :, at : at + LANES] = turned[r]


def mirror_kernel(base_ref, own_ref, far_ref, edge_ref, out_ref):
    members, length = own_ref.shape
    tiles = length // LANES - 1
    shape = (members, LANES)
    lane = lax.broadcasted_iota(jnp.int32, shape, 1)
    mirror = (LANES - lane) % LANES
    first_group, last_group = base_ref[1] == 0, base_ref[1] == base_ref[2] - 1
    beyond = own_ref[:, tiles * LANES :]
    scale = jnp.broadcast_to(beyond[:, 1:2], shape)
    exponent = jnp.broadcast_to(beyond[:, 2:3], shape)
    half_root = math.sqrt(0.5)

    def tile_of(ref, tile):
        return ref[:, pl.ds(pl.multiple_of(tile * LANES, LANES), LANES)]

    def turned(value):
        return jnp.take_along_axis(value, mirror, axis=1, mode="promise_in_bounds")

    def store(tile, own, far, weight):
        offset = base_ref[0] + tile * LANES + lane
        near = left_lines(own, offset.astype(jnp.float32), scale, exponent)
        far_offset = jnp.where(offset == 0, 0, OUTER * INNER - offset)
        back = left_lines(far, far_offset.astype(jnp.float32), scale, exponent)
        at = pl.ds(pl.multiple_of(tile * LANES, LANES), LANES)
        out_ref[0, :, at] = (near[0] + back[0]) * weight
        out_ref[1, :, at] = (near[1] - back[1]) * weight

    def one_tile(tile, last):
        ahead = turned(tile_of(far_ref, tiles - 1 - tile))
        is_edge = (lane == 0) & (tile == 0) & first_group
        store(tile, tile_of(own_ref, tile), jnp.where(lane == 0, last, ahead), jnp.where(is_edge, half_root, 1.0))
        return ahead

    start = jnp.where(first_group, turned(edge_ref[...]), turned(tile_of(far_ref, tiles)))
    last = lax.fori_loop(0, tiles, one_tile, start)
    lone = (lane == 0) & last_group
    store(tiles, jnp.where(lone, beyond, 0.0), jnp.where(lone, last, 0.0), jnp.where(lone, half_root, 0.0))


def limits():
    return pltpu.CompilerParams(vmem_limit_bytes=VMEM_LIMIT)


def part_call(phase):
    members, length = phase.shape
    rows = length // INNER
    tiles = INNER // LANES
    return pl.pallas_call(
        part_kernel,
        grid=(rows // BLOCK_ROWS,),
        in_specs=[pl.BlockSpec((members, BLOCK_ROWS * INNER), lambda g: (0, g))],
        out_specs=pl.BlockSpec((members, tiles, BLOCK_ROWS, LANES), lambda g: (0, 0, g, 0)),
        out_shape=pltpu.HBM((members, tiles, rows, LANES), jnp.float32),
        compiler_params=limits(),
        cost_estimate=pl.CostEstimate(flops=0, bytes_accessed=8 * members * length, transcendentals=0),
    )(pltpu.with_memory_space_constraint(phase, pltpu.HBM))


def join_call(piece, track, within, length, groups, so_far):
    members, tiles, rows, _ = piece.shape
    stretch = rows * INNER
    steps = rows // BLOCK_ROWS
    operands = (piece,) if so_far is None else (piece, so_far)
    each = max(steps // max(groups, 1), 1)
    return pl.pallas_call(
        functools.partial(join_kernel, groups > 0),
        grid=(steps,),
        in_specs=[
            pl.BlockSpec((members, tiles, BLOCK_ROWS, LANES), lambda g: (0, 0, g, 0)),
            pl.BlockSpec(memory_space=pl.ANY),
        ][: len(operands)],
        out_specs=[
            pl.BlockSpec((1, members, BLOCK_ROWS * INNER), lambda g: (track, 0, within * steps + g)),
            pl.BlockSpec((1, members, BLOCK_ROWS * INNER), lambda g: (g // each, 0, g % each)),
        ][: 2 if groups else 1],
        out_shape=[
            jax.ShapeDtypeStruct((2, members, length), jnp.float32),
            jax.ShapeDtypeStruct((max(groups, 1), members, stretch // max(groups, 1)), jnp.float32),
        ][: 2 if groups else 1],
        input_output_aliases={} if so_far is None else {1: 0},
        compiler_params=limits(),
        cost_estimate=pl.CostEstimate(flops=0, bytes_accessed=12 * members * stretch, transcendentals=0),
    )(*operands)


def outer_call(params, phase, kept, matrices, twists):
    track = 1 if kept else 0
    sources, tiles, rows, _ = phase.shape
    some = OUTER_TILES
    lines = pl.BlockSpec((sources, some, rows, LANES), lambda g: (0, g, 0, 0))
    more = 0 if kept else 3
    return pl.pallas_call(
        functools.partial(outer_kernel, track),
        grid=(tiles // some,),
        in_specs=[pl.BlockSpec(memory_space=pltpu.SMEM)]
        + [lines] * (1 + len(kept))
        + [
            pl.BlockSpec(matrices.shape, lambda g: (0, 0, 0, 0)),
            pl.BlockSpec((2, RADIX, QUARTER, some * LANES), lambda g: (0, 0, 0, g)),
        ],
        out_specs=[pl.BlockSpec((some, 2, OUTER, LANES), lambda g: (g, 0, 0, 0))] + [lines] * more,
        out_shape=[jax.ShapeDtypeStruct((tiles, 2, OUTER, LANES), jnp.float32)]
        + [pltpu.HBM(phase.shape, jnp.float32)] * more,
        scratch_shapes=[pltpu.VMEM((RADIX, 2 * QUARTER, some * LANES), jnp.bfloat16)] * 2,
        compiler_params=limits(),
        cost_estimate=pl.CostEstimate(
            flops=24 * OUTER * QUARTER * INNER, bytes_accessed=32 * OUTER * INNER, transcendentals=0
        ),
    )(params, phase, *kept, matrices, twists)


def inner_call(mid, matrices, shards, parts):
    rows = INNER // shards // parts
    tiles = OUTER // LANES
    return pl.pallas_call(
        inner_kernel,
        grid=(OUTER // WIDE,),
        in_specs=[
            pl.BlockSpec((INNER // LANES, 2, WIDE, LANES), lambda g: (0, 0, g, 0)),
            pl.BlockSpec(matrices.shape, lambda g: (0, 0, 0, 0)),
        ],
        out_specs=[pl.BlockSpec((shards, WIDE // LANES, rows, LANES), lambda g: (0, g, 0, 0))] * parts,
        out_shape=[pltpu.HBM((shards, tiles, rows, LANES), jnp.float32)] * parts,
        scratch_shapes=[pltpu.VMEM((RADIX, WIDE, 2 * QUARTER), jnp.bfloat16)] * 2,
        compiler_params=limits(),
        cost_estimate=pl.CostEstimate(
            flops=12 * OUTER * QUARTER * INNER, bytes_accessed=12 * OUTER * INNER, transcendentals=0
        ),
    )(mid, matrices)


def mirror_call(base, own, far, edge):
    members, length = own.shape
    return pl.pallas_call(
        mirror_kernel,
        in_specs=[pl.BlockSpec(memory_space=pltpu.SMEM)] + [pl.BlockSpec(memory_space=pltpu.VMEM)] * 3,
        out_specs=pl.BlockSpec(memory_space=pltpu.VMEM),
        out_shape=jax.ShapeDtypeStruct((2, members, length), jnp.float32),
        compiler_params=limits(),
        cost_estimate=pl.CostEstimate(
            flops=200 * members * length, bytes_accessed=16 * members * length, transcendentals=0
        ),
    )(base, own, far, edge)


def line_params(roughness, waviness, coherence):
    return jnp.stack(
        [jnp.sqrt(2.0 * roughness * (waviness - 1.0) / ANCHOR), -0.5 * waviness, 1.0 / coherence]
    )


def to_group(piece, slot):
    groups = lax.axis_size("mem")
    return lax.ppermute(piece, "mem", [(z, z ^ slot) for z in range(groups)]) if slot else piece


def rows_gram(rows, precision=highest):
    return lax.dot_general(rows, rows, (((1,), (1,)), ((), ())), precision=precision)


def slot_rows(stretches, groups):
    my_group = lax.axis_index("mem")
    rows = [
        to_group(lax.dynamic_index_in_dim(stretches, my_group ^ slot, 0, keepdims=False), slot)
        for slot in reversed(range(groups))
    ]
    return rows[::-1]


def own_and_far(phase, params, my_group):
    groups = lax.axis_size("mem")
    half = phase.shape[1] // 2
    width = half // groups
    lane = lax.broadcasted_iota(jnp.int32, (phase.shape[0], LANES), 1)

    def lines(start):
        return (
            lax.dynamic_slice_in_dim(phase, start, width, 1),
            lax.dynamic_slice_in_dim(phase, start + width, LANES, 1),
        )

    own, far = [], []
    for slot in range(groups):
        group = my_group ^ slot
        inner, beyond = lines(group * width)
        for n in range(2):
            beyond = jnp.where(lane == n + 1, params[n][:, None], beyond)
        far_inner, far_beyond = lines(half + (groups - 1 - group) * width)
        message = jnp.concatenate(
            [
                jnp.concatenate([inner, beyond], axis=1)[None],
                jnp.concatenate([far_inner, far_beyond], axis=1)[None],
            ]
        )
        message = to_group(message, slot)
        own.append(message[0])
        far.append(message[1])
    return jnp.concatenate(own, axis=0), jnp.concatenate(far, axis=0)


def edge_of(own):
    shards = lax.axis_size("len")
    return lax.ppermute(own[:, :LANES], "len", [(d, (shards - d) % shards) for d in range(shards)])


def across(far):
    shards = lax.axis_size("len")
    return lax.ppermute(far, "len", [(d, shards - 1 - d) for d in range(shards)])


def lines_gram(own, far, edge):
    groups = lax.axis_size("mem")
    my_index, my_group = lax.axis_index("len"), lax.axis_index("mem")
    width = own.shape[1] - LANES
    base = (my_index * (2 * groups) + my_group) * width
    base = jnp.stack([base, my_group, jnp.full_like(my_group, groups)]).astype(jnp.int32)
    sums = mirror_call(base, own, far, edge)
    return rows_gram(sums[0]) + rows_gram(sums[1])


def in_order(gram_matrix, members):
    my_group = lax.axis_index("mem")
    row = lax.broadcasted_iota(jnp.int32, gram_matrix.shape, 0)
    column = lax.broadcasted_iota(jnp.int32, gram_matrix.shape, 1)
    to_slot = (row % members == column % members) & ((row // members) ^ my_group == column // members)
    to_slot = to_slot.astype(jnp.float32)
    return jnp.dot(jnp.dot(to_slot, gram_matrix, precision=highest), to_slot.T, precision=highest)


def summed(value):
    for axis in ("len", "mem"):
        value = jnp.sum(lax.all_gather(value, axis), axis=0)
    return value


def per_device_whole(phase_left, phase_right, roughness, waviness, coherence):
    shards, groups = lax.axis_size("len"), lax.axis_size("mem")
    my_index = lax.axis_index("len")
    members = phase_left.shape[0]

    def swap(piece):
        return lax.all_to_all(piece, "len", split_axis=0, concat_axis=0, tiled=True)

    all_params = line_params(roughness, waviness, coherence)
    params = lax.dynamic_index_in_dim(all_params, my_index, 1, keepdims=False)
    outer_tables = jnp.asarray(outer_matrices())
    inner_tables = jnp.asarray(inner_matrices())
    twists = jnp.asarray(twist_tables())
    local_len = phase_left.shape[1]

    left, right = part_call(phase_left), part_call(phase_right)
    right, my_group = lax.optimization_barrier((right, lax.axis_index("mem")))
    left, right = lax.optimization_barrier((swap(left), right))
    right = swap(right)
    own, far = own_and_far(phase_left, all_params, my_group)
    mid, *kept = outer_call(params, left, (), outer_tables, twists)
    first = list(inner_call(mid, inner_tables, shards, 2))
    right, *first = lax.optimization_barrier((right, *first))
    early = swap(first[0])
    (mid,) = outer_call(params, right, kept, outer_tables, twists)
    (second,) = inner_call(mid, inner_tables, shards, 1)
    early, second = lax.optimization_barrier((early, second))
    second, own, far = lax.optimization_barrier((swap(second), own, far))
    profile, points = join_call(second, 1, 0, local_len, groups, None)
    rows = slot_rows(points, groups)
    _, first[1], own, far = lax.optimization_barrier((points, first[1], own, far))
    late = swap(first[1])
    line_gram = lines_gram(own, across(far), edge_of(own))
    (profile,) = join_call(early, 0, 0, local_len, 0, profile)
    late, line_gram = lax.optimization_barrier((late, line_gram))
    (profile,) = join_call(late, 0, 1, local_len, 0, profile)
    profile, line_gram, rows = lax.optimization_barrier((profile, line_gram, rows))
    gram_matrix = 0.25 * line_gram + (0.5 / (OUTER * INNER)) * rows_gram(jnp.concatenate(rows, axis=0), lax.Precision.HIGH)
    return (profile, upper_of(summed(in_order(gram_matrix, members))))


def per_device(phase_left, phase_right, roughness, waviness, coherence):
    whole_members = phase_left.shape[0] == lax.axis_size("len") and lax.axis_size("mem") in (2, 4)
    form = per_device_whole if whole_members else per_device_spread
    return form(phase_left, phase_right, roughness, waviness, coherence)


def solution(mesh):
    placed = (P("mem", "len"), P("mem", "len"), P("mem"), P("mem"), P("mem"))
    return jax.shard_map(
        per_device,
        mesh=mesh,
        in_specs=placed,
        out_specs=(P(None, "mem", "len"), P()),
        check_vma=False,
    )
```

```python
import functools
import math

import jax
import jax.numpy as jnp
import numpy as np
from jax import lax
from jax.experimental import pallas as pl
from jax.experimental.pallas import tpu as pltpu
from jax.sharding import PartitionSpec as P

OUTER = 1024
INNER = 1024
ANCHOR = 64
RADIX = 4
QUARTER = 256
LANES = 128
STEP = 16
SUBLANES = 8
WIDE = 256
BLOCK_ROWS = 16
OUTER_TILES = 2
VMEM_LIMIT = 48 * 1024 * 1024
SIN_HALF = (0.49999999785787, -0.02083332246218, 2.604078316692e-4, -1.547581723527e-6, 5.088214043e-9)
COS_HALF = (
    0.99999999977982,
    -0.12499999839235,
    2.604164763023e-3,
    -2.170056380508e-5,
    9.67192778775e-8,
    -2.5440497557e-10,
)


highest = lax.Precision.HIGHEST


def merged(shard, axis, combine):
    everything = lax.all_gather(shard, axis)
    leading = everything[0]

    def step(k, so_far):
        return combine(so_far, everything[k])

    return lax.fori_loop(1, lax.axis_size(axis), step, leading)


def dft_tables(length):
    index = lax.iota(jnp.int32, length)
    product = index[:, None] * index[None, :] % length
    phase_angle = product.astype(jnp.float32) * (2.0 * math.pi / length)
    return (jnp.cos(phase_angle), jnp.sin(phase_angle))


def spectra_of(phase_left, phase_right, roughness, waviness, coherence, freq):
    amplitude = jnp.sqrt(2.0 * roughness * (waviness - 1.0) / ANCHOR)[:, None] * (
        (freq + ANCHOR) / ANCHOR
    ) ** (-0.5 * waviness[:, None])
    freq_ratio = freq / coherence[:, None]
    coherent = 1.0 / (1.0 + freq_ratio * freq_ratio)
    incoherent = freq_ratio * jnp.sqrt(2.0 + freq_ratio * freq_ratio) * coherent
    cos_left = jnp.cos(phase_left)
    sin_left = jnp.sin(phase_left)
    cos_right = jnp.cos(phase_right)
    sin_right = jnp.sin(phase_right)
    real_part = jnp.stack(
        [amplitude * cos_left, amplitude * (coherent * cos_left + incoherent * cos_right)]
    )
    imag_part = jnp.stack(
        [amplitude * sin_left, amplitude * (coherent * sin_left + incoherent * sin_right)]
    )
    return (real_part, imag_part)


def upper_of(gram_matrix):
    return jnp.linalg.cholesky(gram_matrix).T


def combine_factors(upper_a, upper_b):
    gram_matrix = jnp.dot(upper_a.T, upper_a, precision=highest) + jnp.dot(
        upper_b.T, upper_b, precision=highest
    )
    return upper_of(gram_matrix)


def gram_of(snapshot):
    return jnp.einsum("tmr,tnr->mn", snapshot, snapshot, precision=highest)


def per_device_spread(phase_left, phase_right, roughness, waviness, coherence):
    shards = lax.axis_size("len")
    my_index = lax.axis_index("len")
    local_members, local_len = phase_left.shape
    columns = 2 * local_members
    outer_block = OUTER // shards
    inner_block = INNER // shards

    def to_rows(part):
        shaped = part.reshape(2, local_members, inner_block, OUTER)
        return jnp.transpose(shaped, (2, 3, 0, 1)).reshape(
            inner_block, shards, outer_block * columns
        )

    inner_cos, inner_sin = dft_tables(INNER)
    freq = (my_index * local_len + lax.iota(jnp.int32, local_len)).astype(jnp.float32)[None, :]
    real_part, imag_part = spectra_of(phase_left, phase_right, roughness, waviness, coherence, freq)
    pieces = (
        lax.all_to_all(to_rows(real_part), "len", split_axis=1, concat_axis=0, tiled=True),
        lax.all_to_all(to_rows(imag_part), "len", split_axis=1, concat_axis=0, tiled=True),
    )
    real_in = pieces[0].reshape(INNER, -1)
    imag_in = pieces[1].reshape(INNER, -1)
    real_out = jnp.dot(inner_cos, real_in, precision=highest) - jnp.dot(
        inner_sin, imag_in, precision=highest
    )
    imag_out = jnp.dot(inner_cos, imag_in, precision=highest) + jnp.dot(
        inner_sin, real_in, precision=highest
    )
    row_index = lax.iota(jnp.int32, INNER)[:, None]
    outer_index = (my_index * outer_block + lax.iota(jnp.int32, outer_block))[None, :]
    twist = (row_index * outer_index % (OUTER * INNER)).astype(jnp.float32) * (
        2.0 * math.pi / (OUTER * INNER)
    )
    twist_cos = jnp.repeat(jnp.cos(twist), columns, axis=1)
    twist_sin = jnp.repeat(jnp.sin(twist), columns, axis=1)
    rot_real = (real_out * twist_cos - imag_out * twist_sin).reshape(
        shards, inner_block, outer_block * columns
    )
    rot_imag = (real_out * twist_sin + imag_out * twist_cos).reshape(
        shards, inner_block, outer_block * columns
    )
    outer_cos, outer_sin = dft_tables(OUTER)
    outer_cos = outer_cos.reshape(OUTER, shards, outer_block)
    outer_sin = outer_sin.reshape(OUTER, shards, outer_block)
    pieces = (
        lax.all_to_all(rot_real, "len", split_axis=0, concat_axis=0, tiled=True),
        lax.all_to_all(rot_imag, "len", split_axis=0, concat_axis=0, tiled=True),
    )
    item_count = pieces[0].shape[1]
    real_in = pieces[0].reshape(shards, item_count, outer_block, columns)
    imag_in = pieces[1].reshape(shards, item_count, outer_block, columns)
    first = jnp.einsum("jqa,qiac->cij", outer_cos, real_in, precision=highest)
    second = jnp.einsum("jqa,qiac->cij", outer_sin, imag_in, precision=highest)
    profile_block = first - second
    outgoing = jnp.transpose(
        profile_block.reshape(columns, inner_block, shards, outer_block), (2, 0, 1, 3)
    ).reshape(shards, -1)
    arrived = lax.all_to_all(outgoing, "len", split_axis=0, concat_axis=0, tiled=True)
    profile = jnp.transpose(
        arrived.reshape(shards, columns, inner_block, outer_block), (1, 3, 0, 2)
    ).reshape(2, local_members, local_len)
    scale = 1.0 / math.sqrt(2.0 * OUTER * INNER)
    snapshot = profile_block.reshape(2, local_members, inner_block * OUTER) * scale
    gathered = lax.all_gather(snapshot, "mem", axis=1, tiled=True)
    gram_local = gram_of(gathered)
    r_factor = merged(upper_of(gram_local), "len", combine_factors)
    return (profile, r_factor)


def host_cis(product, period):
    angle = product % period * (2.0 * np.pi / period)
    return np.cos(angle), np.sin(angle)


def split_host(table):
    coarse = table.astype(np.float32).astype(jnp.bfloat16)
    fine = (table - coarse.astype(np.float64)).astype(np.float32).astype(jnp.bfloat16)
    return np.stack([coarse, fine])


def outer_matrices():
    c, e, b = np.arange(QUARTER), np.arange(RADIX), np.arange(QUARTER)
    cos_part, sin_part = host_cis((RADIX * c[None, :, None] + e[:, None, None]) * b[None, None, :], OUTER)
    upper = np.concatenate([cos_part, -sin_part], axis=2)
    lower = np.concatenate([sin_part, cos_part], axis=2)
    return split_host(np.concatenate([upper, lower], axis=1))


def inner_matrices():
    c, e, b = np.arange(QUARTER), np.arange(RADIX), np.arange(QUARTER)
    cos_part, sin_part = host_cis((RADIX * c[None, :, None] + e[:, None, None]) * b[None, None, :], INNER)
    return split_host(np.concatenate([cos_part, -sin_part], axis=2))


def twist_tables():
    j1 = RADIX * np.arange(QUARTER)[None, :, None] + np.arange(RADIX)[:, None, None]
    cos_part, sin_part = host_cis(j1 * np.arange(INNER)[None, None, :], OUTER * INNER)
    return np.stack([cos_part, sin_part]).astype(np.float32)


def sin_cos(angle):
    square = angle * angle

    def series(coefficients):
        total = jnp.float32(coefficients[-1])
        for coefficient in coefficients[-2::-1]:
            total = total * square + jnp.float32(coefficient)
        return total

    half_sin = angle * series(SIN_HALF)
    half_cos = series(COS_HALF)
    twice = half_sin + half_sin
    return twice * half_cos, 1.0 - twice * half_sin


def amplitude_of(freq, scale, exponent):
    return scale * jnp.exp2(exponent * jnp.log2((freq + ANCHOR) * (1.0 / ANCHOR)))


def left_lines(left, freq, scale, exponent):
    amplitude = amplitude_of(freq, scale, exponent)
    sin_left, cos_left = sin_cos(left)
    return amplitude * cos_left, amplitude * sin_left


def radix_four(parts):
    (r0, i0), (r1, i1), (r2, i2), (r3, i3) = parts
    even_sum, even_gap = (r0 + r2, i0 + i2), (r0 - r2, i0 - i2)
    odd_sum, odd_gap = (r1 + r3, i1 + i3), (r1 - r3, i1 - i3)
    return (
        (even_sum[0] + odd_sum[0], even_sum[1] + odd_sum[1]),
        (even_gap[0] - odd_gap[1], even_gap[1] + odd_gap[0]),
        (even_sum[0] - odd_sum[0], even_sum[1] - odd_sum[1]),
        (even_gap[0] + odd_gap[1], even_gap[1] - odd_gap[0]),
    )


def store_split(coarse_ref, fine_ref, where, value):
    coarse = value.astype(jnp.bfloat16)
    coarse_ref[where] = coarse
    fine_ref[where] = (value - coarse.astype(jnp.float32)).astype(jnp.bfloat16)


def triple_dot(matrix_ref, e, coarse, fine, dims):
    def product(a, b):
        return lax.dot_general(a, b, (dims, ((), ())), preferred_element_type=jnp.float32)

    return product(matrix_ref[0, e], coarse) + (
        product(matrix_ref[0, e], fine) + product(matrix_ref[1, e], coarse)
    )


def first_lines(params_ref, left_ref, kept_refs, where, freq):
    scale, exponent, inverse_coherence = params_ref[0], params_ref[1], params_ref[2]
    amplitude = amplitude_of(freq, scale, exponent)
    freq_ratio = freq * inverse_coherence
    ratio_square = freq_ratio * freq_ratio
    coherent = 1.0 / (1.0 + ratio_square)
    incoherent = freq_ratio * jnp.sqrt(2.0 + ratio_square) * coherent
    sin_left, cos_left = sin_cos(left_ref[where])
    real, imag = amplitude * cos_left, amplitude * sin_left
    kept_refs[0][where] = coherent * real
    kept_refs[1][where] = coherent * imag
    kept_refs[2][where] = amplitude * incoherent
    return real, imag


def second_lines(right_ref, kept_refs, where):
    sin_right, cos_right = sin_cos(right_ref[where])
    independent = kept_refs[2][where]
    return (
        kept_refs[0][where] + independent * cos_right,
        kept_refs[1][where] + independent * sin_right,
    )


def outer_kernel(track, params_ref, phase_ref, *refs):
    if track == 0:
        matrix_ref, twist_ref, out_ref, *kept_refs, coarse_ref, fine_ref = refs
    else:
        *kept_refs, matrix_ref, twist_ref, out_ref, coarse_ref, fine_ref = refs
    _, tiles, rows, _ = phase_ref.shape
    lane = lax.broadcasted_iota(jnp.int32, (STEP, LANES), 1) + pl.program_id(0) * tiles * LANES
    row = lax.broadcasted_iota(jnp.int32, (STEP, LANES), 0)
    place = row * INNER + lane

    def some_rows(step, carry):
        b = step * STEP
        for tile in range(tiles):
            lines = []
            for a in range(RADIX):
                k1 = a * QUARTER + b
                where = (k1 // rows, tile, pl.ds(pl.multiple_of(k1 % rows, STEP), STEP))
                if track == 0:
                    freq = (place + (k1 * INNER + tile * LANES)).astype(jnp.float32)
                    lines.append(first_lines(params_ref, phase_ref, kept_refs, where, freq))
                else:
                    lines.append(second_lines(phase_ref, kept_refs, where))
            mixed = radix_four(lines)
            for e in range(RADIX):
                for ri in range(2):
                    at = pl.ds(pl.multiple_of(ri * QUARTER + b, STEP), STEP)
                    where = (e, at, pl.ds(tile * LANES, LANES))
                    store_split(coarse_ref, fine_ref, where, mixed[e][ri])
        return carry

    lax.fori_loop(0, QUARTER // STEP, some_rows, 0)
    for e in range(RADIX):
        mid = triple_dot(matrix_ref, e, coarse_ref[e], fine_ref[e], ((1,), (0,)))
        for tile in range(tiles):
            lanes = slice(tile * LANES, (tile + 1) * LANES)
            cos_part, sin_part = twist_ref[0, e, :, lanes], twist_ref[1, e, :, lanes]
            real, imag = mid[:QUARTER, lanes], mid[QUARTER:, lanes]
            out_ref[tile, 0, pl.ds(e, QUARTER, stride=RADIX), :] = real * cos_part - imag * sin_part
            out_ref[tile, 1, pl.ds(e, QUARTER, stride=RADIX), :] = real * sin_part + imag * cos_part


def inner_kernel(mid_ref, matrix_ref, *refs):
    out_refs, (coarse_ref, fine_ref) = refs[:-2], refs[-2:]
    wide = mid_ref.shape[2]
    shards, _, rows, _ = out_refs[0].shape

    def some_rows(step, carry):
        at = pl.multiple_of(step * STEP, STEP)
        for half in range(0, QUARTER, LANES):
            parts = [
                tuple(mid_ref[(a * QUARTER + half) // LANES, ri, pl.ds(at, STEP), :] for ri in range(2))
                for a in range(RADIX)
            ]
            mixed = radix_four(parts)
            for e in range(RADIX):
                for ri in range(2):
                    where = (e, pl.ds(at, STEP), pl.ds(ri * QUARTER + half, LANES))
                    store_split(coarse_ref, fine_ref, where, mixed[e][ri])
        return carry

    lax.fori_loop(0, wide // STEP, some_rows, 0)
    some = rows // RADIX
    for e in range(RADIX):
        value = triple_dot(matrix_ref, e, coarse_ref[e], fine_ref[e], ((1,), (1,)))
        for f in range(shards):
            for part, out_ref in enumerate(out_refs):
                at = (f * len(out_refs) + part) * some
                for tile in range(wide // LANES):
                    out_ref[f, tile, pl.ds(e, some, stride=RADIX), :] = value[
                        at : at + some, tile * LANES : (tile + 1) * LANES
                    ]


def part_kernel(in_ref, out_ref):
    members, tiles, rows, _ = out_ref.shape
    for tile in range(tiles):
        for start in range(0, rows, SUBLANES):
            columns = [((start + r) * tiles + tile) * LANES for r in range(SUBLANES)]
            turned = jnp.transpose(jnp.stack([in_ref[:, at : at + LANES] for at in columns]), (1, 0, 2))
            for m in range(members):
                out_ref[m, tile, start : start + SUBLANES, :] = turned[m]


def join_kernel(extra, in_ref, *refs):
    out_refs = refs[-2:] if extra else refs[-1:]
    members, tiles, rows, _ = in_ref.shape
    for tile in range(tiles):
        for start in range(0, rows, SUBLANES):
            turned = jnp.transpose(in_ref[:, tile, start : start + SUBLANES, :], (1, 0, 2))
            for r in range(SUBLANES):
                at = ((start + r) * tiles + tile) * LANES
                for out_ref in out_refs:
                    out_ref[0, :, at : at + LANES] = turned[r]


def near_kernel(base_ref, own_ref, out_ref):
    members, length = own_ref.shape
    tiles = length // LANES - 1
    scale, exponent = tile_params(own_ref[:, tiles * LANES :])
    lane = lax.broadcasted_iota(jnp.int32, (members, LANES), 1)

    def one_tile(tile, carry):
        at = pl.ds(pl.multiple_of(tile * LANES, LANES), LANES)
        freq = (base_ref[0] + tile * LANES + lane).astype(jnp.float32)
        out_ref[0, :, at], out_ref[1, :, at] = left_lines(own_ref[:, at], freq, scale, exponent)
        return carry

    lax.fori_loop(0, tiles + 1, one_tile, 0)


def tile_params(beyond):
    return (jnp.broadcast_to(beyond[:, n : n + 1], beyond.shape) for n in (1, 2))


def mirror_kernel(base_ref, near_ref, far_ref, edge_ref, beyond_ref, out_ref):
    members, length = far_ref.shape
    tiles = length // LANES - 1
    shape = (members, LANES)
    lane = lax.broadcasted_iota(jnp.int32, shape, 1)
    mirror = (LANES - lane) % LANES
    first_group, last_group = base_ref[1] == 0, base_ref[1] == base_ref[2] - 1
    scale, exponent = tile_params(beyond_ref[...])
    half_root = math.sqrt(0.5)

    def tile_of(ref, tile):
        return ref[:, pl.ds(pl.multiple_of(tile * LANES, LANES), LANES)]

    def turned(value):
        return jnp.take_along_axis(value, mirror, axis=1, mode="promise_in_bounds")

    def store(tile, far, keep, weight):
        offset = base_ref[0] + tile * LANES + lane
        far_offset = jnp.where(offset == 0, 0, OUTER * INNER - offset)
        back = left_lines(far, far_offset.astype(jnp.float32), scale, exponent)
        at = pl.ds(pl.multiple_of(tile * LANES, LANES), LANES)
        real, imag = near_ref[0, :, at] + back[0], near_ref[1, :, at] - back[1]
        out_ref[0, :, at] = jnp.where(keep, real * weight, 0.0)
        out_ref[1, :, at] = jnp.where(keep, imag * weight, 0.0)

    def one_tile(tile, last):
        ahead = turned(tile_of(far_ref, tiles - 1 - tile))
        is_edge = (lane == 0) & (tile == 0) & first_group
        store(tile, jnp.where(lane == 0, last, ahead), lane >= 0, jnp.where(is_edge, half_root, 1.0))
        return ahead

    start = jnp.where(first_group, turned(edge_ref[...]), turned(tile_of(far_ref, tiles)))
    last = lax.fori_loop(0, tiles, one_tile, start)
    store(tiles, jnp.where(lane == 0, last, 0.0), (lane == 0) & last_group, half_root)


def limits():
    return pltpu.CompilerParams(vmem_limit_bytes=VMEM_LIMIT)


def part_call(phase):
    members, length = phase.shape
    rows = length // INNER
    tiles = INNER // LANES
    return pl.pallas_call(
        part_kernel,
        grid=(rows // BLOCK_ROWS,),
        in_specs=[pl.BlockSpec((members, BLOCK_ROWS * INNER), lambda g: (0, g))],
        out_specs=pl.BlockSpec((members, tiles, BLOCK_ROWS, LANES), lambda g: (0, 0, g, 0)),
        out_shape=pltpu.HBM((members, tiles, rows, LANES), jnp.float32),
        compiler_params=limits(),
        cost_estimate=pl.CostEstimate(flops=0, bytes_accessed=8 * members * length, transcendentals=0),
    )(pltpu.with_memory_space_constraint(phase, pltpu.HBM))


def join_call(piece, track, within, length, groups, so_far):
    members, tiles, rows, _ = piece.shape
    stretch = rows * INNER
    steps = rows // BLOCK_ROWS
    operands = (piece,) if so_far is None else (piece, so_far)
    each = max(steps // max(groups, 1), 1)
    return pl.pallas_call(
        functools.partial(join_kernel, groups > 0),
        grid=(steps,),
        in_specs=[
            pl.BlockSpec((members, tiles, BLOCK_ROWS, LANES), lambda g: (0, 0, g, 0)),
            pl.BlockSpec(memory_space=pl.ANY),
        ][: len(operands)],
        out_specs=[
            pl.BlockSpec((1, members, BLOCK_ROWS * INNER), lambda g: (track, 0, within * steps + g)),
            pl.BlockSpec((1, members, BLOCK_ROWS * INNER), lambda g: (g // each, 0, g % each)),
        ][: 2 if groups else 1],
        out_shape=[
            jax.ShapeDtypeStruct((2, members, length), jnp.float32),
            pltpu.HBM((max(groups, 1), members, stretch // max(groups, 1)), jnp.float32),
        ][: 2 if groups else 1],
        input_output_aliases={} if so_far is None else {1: 0},
        compiler_params=limits(),
        cost_estimate=pl.CostEstimate(flops=0, bytes_accessed=12 * members * stretch, transcendentals=0),
    )(*operands)


def outer_call(params, phase, kept, matrices, twists):
    track = 1 if kept else 0
    sources, tiles, rows, _ = phase.shape
    some = OUTER_TILES
    lines = pl.BlockSpec((sources, some, rows, LANES), lambda g: (0, g, 0, 0))
    more = 0 if kept else 3
    return pl.pallas_call(
        functools.partial(outer_kernel, track),
        grid=(tiles // some,),
        in_specs=[pl.BlockSpec(memory_space=pltpu.SMEM)]
        + [lines] * (1 + len(kept))
        + [
            pl.BlockSpec(matrices.shape, lambda g: (0, 0, 0, 0)),
            pl.BlockSpec((2, RADIX, QUARTER, some * LANES), lambda g: (0, 0, 0, g)),
        ],
        out_specs=[pl.BlockSpec((some, 2, OUTER, LANES), lambda g: (g, 0, 0, 0))] + [lines] * more,
        out_shape=[jax.ShapeDtypeStruct((tiles, 2, OUTER, LANES), jnp.float32)]
        + [pltpu.HBM(phase.shape, jnp.float32)] * more,
        scratch_shapes=[pltpu.VMEM((RADIX, 2 * QUARTER, some * LANES), jnp.bfloat16)] * 2,
        compiler_params=limits(),
        cost_estimate=pl.CostEstimate(
            flops=24 * OUTER * QUARTER * INNER, bytes_accessed=32 * OUTER * INNER, transcendentals=0
        ),
    )(params, phase, *kept, matrices, twists)


def inner_call(mid, matrices, shards, parts):
    rows = INNER // shards // parts
    tiles = OUTER // LANES
    return pl.pallas_call(
        inner_kernel,
        grid=(OUTER // WIDE,),
        in_specs=[
            pl.BlockSpec((INNER // LANES, 2, WIDE, LANES), lambda g: (0, 0, g, 0)),
            pl.BlockSpec(matrices.shape, lambda g: (0, 0, 0, 0)),
        ],
        out_specs=[pl.BlockSpec((shards, WIDE // LANES, rows, LANES), lambda g: (0, g, 0, 0))] * parts,
        out_shape=[pltpu.HBM((shards, tiles, rows, LANES), jnp.float32)] * parts,
        scratch_shapes=[pltpu.VMEM((RADIX, WIDE, 2 * QUARTER), jnp.bfloat16)] * 2,
        compiler_params=limits(),
        cost_estimate=pl.CostEstimate(
            flops=12 * OUTER * QUARTER * INNER, bytes_accessed=12 * OUTER * INNER, transcendentals=0
        ),
    )(mid, matrices)


def near_call(base, own):
    members, length = own.shape
    return pl.pallas_call(
        near_kernel,
        in_specs=[pl.BlockSpec(memory_space=pltpu.SMEM), pl.BlockSpec(memory_space=pltpu.VMEM)],
        out_specs=pl.BlockSpec(memory_space=pltpu.VMEM),
        out_shape=jax.ShapeDtypeStruct((2, members, length), jnp.float32),
        compiler_params=limits(),
        cost_estimate=pl.CostEstimate(
            flops=100 * members * length, bytes_accessed=12 * members * length, transcendentals=0
        ),
    )(base, own)


def mirror_call(base, near, far, edge, beyond):
    members, length = far.shape
    return pl.pallas_call(
        mirror_kernel,
        in_specs=[pl.BlockSpec(memory_space=pltpu.SMEM)] + [pl.BlockSpec(memory_space=pltpu.VMEM)] * 4,
        out_specs=pl.BlockSpec(memory_space=pltpu.VMEM),
        out_shape=jax.ShapeDtypeStruct((2, members, length), jnp.float32),
        compiler_params=limits(),
        cost_estimate=pl.CostEstimate(
            flops=100 * members * length, bytes_accessed=20 * members * length, transcendentals=0
        ),
    )(base, near, far, edge, beyond)


def line_params(roughness, waviness, coherence):
    return jnp.stack(
        [jnp.sqrt(2.0 * roughness * (waviness - 1.0) / ANCHOR), -0.5 * waviness, 1.0 / coherence]
    )


def to_group(piece, slot):
    groups = lax.axis_size("mem")
    return lax.ppermute(piece, "mem", [(z, z ^ slot) for z in range(groups)]) if slot else piece


def rows_gram(rows):
    return lax.dot_general(rows, rows, (((1,), (1,)), ((), ())), precision=lax.Precision.HIGH)


def by_slot(stretches, groups):
    my_group = lax.axis_index("mem")
    return [lax.dynamic_index_in_dim(stretches, my_group ^ slot, 0, keepdims=False) for slot in range(groups)]


def own_and_far(phase, params, my_group):
    groups = lax.axis_size("mem")
    half = phase.shape[1] // 2
    width = half // groups
    lane = lax.broadcasted_iota(jnp.int32, (phase.shape[0], LANES), 1)

    def lines(start):
        return (
            lax.dynamic_slice_in_dim(phase, start, width, 1),
            lax.dynamic_slice_in_dim(phase, start + width, LANES, 1),
        )

    own, far = [], []
    for slot in range(groups):
        group = my_group ^ slot
        inner, beyond = lines(group * width)
        for n in range(2):
            beyond = jnp.where(lane == n + 1, params[n][:, None], beyond)
        far_inner, far_beyond = lines(half + (groups - 1 - group) * width)
        message = jnp.concatenate(
            [
                jnp.concatenate([inner, beyond], axis=1)[None],
                jnp.concatenate([far_inner, far_beyond], axis=1)[None],
            ]
        )
        message = to_group(message, slot)
        own.append(message[0])
        far.append(message[1])
    return jnp.concatenate(own, axis=0), jnp.concatenate(far, axis=0)


def edge_of(own):
    shards = lax.axis_size("len")
    return lax.ppermute(own[:, :LANES], "len", [(d, (shards - d) % shards) for d in range(shards)])


def across(far):
    shards = lax.axis_size("len")
    return lax.ppermute(far, "len", [(d, shards - 1 - d) for d in range(shards)])


def line_base(width):
    groups = lax.axis_size("mem")
    my_index, my_group = lax.axis_index("len"), lax.axis_index("mem")
    base = (my_index * (2 * groups) + my_group) * width
    return jnp.stack([base, my_group, jnp.full_like(my_group, groups)]).astype(jnp.int32)


def lines_gram(base, near, far, edge, beyond):
    sums = mirror_call(base, near, far, edge, beyond)
    return rows_gram(sums[0]) + rows_gram(sums[1])


def in_order(gram_matrix, members):
    my_group = lax.axis_index("mem")
    row = lax.broadcasted_iota(jnp.int32, gram_matrix.shape, 0)
    column = lax.broadcasted_iota(jnp.int32, gram_matrix.shape, 1)
    to_slot = (row % members == column % members) & ((row // members) ^ my_group == column // members)
    to_slot = to_slot.astype(jnp.float32)
    return jnp.dot(jnp.dot(to_slot, gram_matrix, precision=highest), to_slot.T, precision=highest)


def summed(value):
    for axis in ("len", "mem"):
        value = jnp.sum(lax.all_gather(value, axis), axis=0)
    return value


def per_device_whole(phase_left, phase_right, roughness, waviness, coherence):
    shards, groups = lax.axis_size("len"), lax.axis_size("mem")
    my_index = lax.axis_index("len")
    members = phase_left.shape[0]

    def swap(piece):
        return lax.all_to_all(piece, "len", split_axis=0, concat_axis=0, tiled=True)

    all_params = line_params(roughness, waviness, coherence)
    params = lax.dynamic_index_in_dim(all_params, my_index, 1, keepdims=False)
    outer_tables = jnp.asarray(outer_matrices())
    inner_tables = jnp.asarray(inner_matrices())
    twists = jnp.asarray(twist_tables())
    local_len = phase_left.shape[1]

    left, right = part_call(phase_left), part_call(phase_right)
    right, my_group = lax.optimization_barrier((right, lax.axis_index("mem")))
    left, right = lax.optimization_barrier((swap(left), right))
    right = swap(right)
    own, far = own_and_far(phase_left, all_params, my_group)
    mid, *kept = outer_call(params, left, (), outer_tables, twists)
    first = list(inner_call(mid, inner_tables, shards, 2))
    right, *first = lax.optimization_barrier((right, *first))
    early = swap(first[0])
    (mid,) = outer_call(params, right, kept, outer_tables, twists)
    (second,) = inner_call(mid, inner_tables, shards, 1)
    early, second = lax.optimization_barrier((early, second))
    base = line_base(own.shape[1] - LANES)
    near = near_call(base, own)
    second, near, far = lax.optimization_barrier((swap(second), near, far))
    profile, points = join_call(second, 1, 0, local_len, groups, None)
    pieces = by_slot(points, groups)
    rows = [to_group(piece, slot) for slot, piece in enumerate(pieces)]
    _, first[1], edge, far = lax.optimization_barrier((pieces, first[1], own, far))
    late = swap(first[1])
    line_gram = lines_gram(base, near, across(far), edge_of(edge), own[:, -LANES:])
    (profile,) = join_call(early, 0, 0, local_len, 0, profile)
    late, line_gram = lax.optimization_barrier((late, line_gram))
    (profile,) = join_call(late, 0, 1, local_len, 0, profile)
    profile, line_gram, rows = lax.optimization_barrier((profile, line_gram, rows))
    gram_matrix = 0.25 * line_gram + (0.5 / (OUTER * INNER)) * rows_gram(jnp.concatenate(rows, axis=0))
    return (profile, upper_of(summed(in_order(gram_matrix, members))))


def per_device(phase_left, phase_right, roughness, waviness, coherence):
    whole_members = phase_left.shape[0] == lax.axis_size("len") and lax.axis_size("mem") in (2, 4)
    form = per_device_whole if whole_members else per_device_spread
    return form(phase_left, phase_right, roughness, waviness, coherence)


def solution(mesh):
    placed = (P("mem", "len"), P("mem", "len"), P("mem"), P("mem"), P("mem"))
    return jax.shard_map(
        per_device,
        mesh=mesh,
        in_specs=placed,
        out_specs=(P(None, "mem", "len"), P()),
        check_vma=False,
    )
```

```python
import functools
import math

import jax
import jax.numpy as jnp
import numpy as np
from jax import lax
from jax.experimental import pallas as pl
from jax.experimental.pallas import tpu as pltpu
from jax.sharding import PartitionSpec as P

OUTER = 1024
INNER = 1024
ANCHOR = 64
RADIX = 4
QUARTER = 256
LANES = 128
STEP = 16
SUBLANES = 8
WIDE = 256
BLOCK_ROWS = 16
OUTER_TILES = 2
VMEM_LIMIT = 48 * 1024 * 1024
SIN_HALF = (0.49999999785787, -0.02083332246218, 2.604078316692e-4, -1.547581723527e-6, 5.088214043e-9)
COS_HALF = (
    0.99999999977982,
    -0.12499999839235,
    2.604164763023e-3,
    -2.170056380508e-5,
    9.67192778775e-8,
    -2.5440497557e-10,
)


highest = lax.Precision.HIGHEST


def merged(shard, axis, combine):
    everything = lax.all_gather(shard, axis)
    leading = everything[0]

    def step(k, so_far):
        return combine(so_far, everything[k])

    return lax.fori_loop(1, lax.axis_size(axis), step, leading)


def dft_tables(length):
    index = lax.iota(jnp.int32, length)
    product = index[:, None] * index[None, :] % length
    phase_angle = product.astype(jnp.float32) * (2.0 * math.pi / length)
    return (jnp.cos(phase_angle), jnp.sin(phase_angle))


def spectra_of(phase_left, phase_right, roughness, waviness, coherence, freq):
    amplitude = jnp.sqrt(2.0 * roughness * (waviness - 1.0) / ANCHOR)[:, None] * (
        (freq + ANCHOR) / ANCHOR
    ) ** (-0.5 * waviness[:, None])
    freq_ratio = freq / coherence[:, None]
    coherent = 1.0 / (1.0 + freq_ratio * freq_ratio)
    incoherent = freq_ratio * jnp.sqrt(2.0 + freq_ratio * freq_ratio) * coherent
    cos_left = jnp.cos(phase_left)
    sin_left = jnp.sin(phase_left)
    cos_right = jnp.cos(phase_right)
    sin_right = jnp.sin(phase_right)
    real_part = jnp.stack(
        [amplitude * cos_left, amplitude * (coherent * cos_left + incoherent * cos_right)]
    )
    imag_part = jnp.stack(
        [amplitude * sin_left, amplitude * (coherent * sin_left + incoherent * sin_right)]
    )
    return (real_part, imag_part)


def upper_of(gram_matrix):
    return jnp.linalg.cholesky(gram_matrix).T


def combine_factors(upper_a, upper_b):
    gram_matrix = jnp.dot(upper_a.T, upper_a, precision=highest) + jnp.dot(
        upper_b.T, upper_b, precision=highest
    )
    return upper_of(gram_matrix)


def gram_of(snapshot):
    return jnp.einsum("tmr,tnr->mn", snapshot, snapshot, precision=highest)


def per_device_spread(phase_left, phase_right, roughness, waviness, coherence):
    shards = lax.axis_size("len")
    my_index = lax.axis_index("len")
    local_members, local_len = phase_left.shape
    columns = 2 * local_members
    outer_block = OUTER // shards
    inner_block = INNER // shards

    def to_rows(part):
        shaped = part.reshape(2, local_members, inner_block, OUTER)
        return jnp.transpose(shaped, (2, 3, 0, 1)).reshape(
            inner_block, shards, outer_block * columns
        )

    inner_cos, inner_sin = dft_tables(INNER)
    freq = (my_index * local_len + lax.iota(jnp.int32, local_len)).astype(jnp.float32)[None, :]
    real_part, imag_part = spectra_of(phase_left, phase_right, roughness, waviness, coherence, freq)
    pieces = (
        lax.all_to_all(to_rows(real_part), "len", split_axis=1, concat_axis=0, tiled=True),
        lax.all_to_all(to_rows(imag_part), "len", split_axis=1, concat_axis=0, tiled=True),
    )
    real_in = pieces[0].reshape(INNER, -1)
    imag_in = pieces[1].reshape(INNER, -1)
    real_out = jnp.dot(inner_cos, real_in, precision=highest) - jnp.dot(
        inner_sin, imag_in, precision=highest
    )
    imag_out = jnp.dot(inner_cos, imag_in, precision=highest) + jnp.dot(
        inner_sin, real_in, precision=highest
    )
    row_index = lax.iota(jnp.int32, INNER)[:, None]
    outer_index = (my_index * outer_block + lax.iota(jnp.int32, outer_block))[None, :]
    twist = (row_index * outer_index % (OUTER * INNER)).astype(jnp.float32) * (
        2.0 * math.pi / (OUTER * INNER)
    )
    twist_cos = jnp.repeat(jnp.cos(twist), columns, axis=1)
    twist_sin = jnp.repeat(jnp.sin(twist), columns, axis=1)
    rot_real = (real_out * twist_cos - imag_out * twist_sin).reshape(
        shards, inner_block, outer_block * columns
    )
    rot_imag = (real_out * twist_sin + imag_out * twist_cos).reshape(
        shards, inner_block, outer_block * columns
    )
    outer_cos, outer_sin = dft_tables(OUTER)
    outer_cos = outer_cos.reshape(OUTER, shards, outer_block)
    outer_sin = outer_sin.reshape(OUTER, shards, outer_block)
    pieces = (
        lax.all_to_all(rot_real, "len", split_axis=0, concat_axis=0, tiled=True),
        lax.all_to_all(rot_imag, "len", split_axis=0, concat_axis=0, tiled=True),
    )
    item_count = pieces[0].shape[1]
    real_in = pieces[0].reshape(shards, item_count, outer_block, columns)
    imag_in = pieces[1].reshape(shards, item_count, outer_block, columns)
    first = jnp.einsum("jqa,qiac->cij", outer_cos, real_in, precision=highest)
    second = jnp.einsum("jqa,qiac->cij", outer_sin, imag_in, precision=highest)
    profile_block = first - second
    outgoing = jnp.transpose(
        profile_block.reshape(columns, inner_block, shards, outer_block), (2, 0, 1, 3)
    ).reshape(shards, -1)
    arrived = lax.all_to_all(outgoing, "len", split_axis=0, concat_axis=0, tiled=True)
    profile = jnp.transpose(
        arrived.reshape(shards, columns, inner_block, outer_block), (1, 3, 0, 2)
    ).reshape(2, local_members, local_len)
    scale = 1.0 / math.sqrt(2.0 * OUTER * INNER)
    snapshot = profile_block.reshape(2, local_members, inner_block * OUTER) * scale
    gathered = lax.all_gather(snapshot, "mem", axis=1, tiled=True)
    gram_local = gram_of(gathered)
    r_factor = merged(upper_of(gram_local), "len", combine_factors)
    return (profile, r_factor)


def host_cis(product, period):
    angle = product % period * (2.0 * np.pi / period)
    return np.cos(angle), np.sin(angle)


def split_host(table):
    coarse = table.astype(np.float32).astype(jnp.bfloat16)
    fine = (table - coarse.astype(np.float64)).astype(np.float32).astype(jnp.bfloat16)
    return np.stack([coarse, fine])


def outer_matrices():
    c, e, b = np.arange(QUARTER), np.arange(RADIX), np.arange(QUARTER)
    cos_part, sin_part = host_cis((RADIX * c[None, :, None] + e[:, None, None]) * b[None, None, :], OUTER)
    upper = np.concatenate([cos_part, -sin_part], axis=2)
    lower = np.concatenate([sin_part, cos_part], axis=2)
    return split_host(np.concatenate([upper, lower], axis=1))


def inner_matrices():
    c, e, b = np.arange(QUARTER), np.arange(RADIX), np.arange(QUARTER)
    cos_part, sin_part = host_cis((RADIX * c[None, :, None] + e[:, None, None]) * b[None, None, :], INNER)
    return split_host(np.concatenate([cos_part, -sin_part], axis=2))


def twist_tables():
    j1 = RADIX * np.arange(QUARTER)[None, :, None] + np.arange(RADIX)[:, None, None]
    cos_part, sin_part = host_cis(j1 * np.arange(INNER)[None, None, :], OUTER * INNER)
    return np.stack([cos_part, sin_part]).astype(np.float32)


def sin_cos(angle):
    square = angle * angle

    def series(coefficients):
        total = jnp.float32(coefficients[-1])
        for coefficient in coefficients[-2::-1]:
            total = total * square + jnp.float32(coefficient)
        return total

    half_sin = angle * series(SIN_HALF)
    half_cos = series(COS_HALF)
    twice = half_sin + half_sin
    return twice * half_cos, 1.0 - twice * half_sin


def amplitude_of(freq, scale, exponent):
    return scale * jnp.exp2(exponent * jnp.log2((freq + ANCHOR) * (1.0 / ANCHOR)))


def left_lines(left, freq, scale, exponent):
    amplitude = amplitude_of(freq, scale, exponent)
    sin_left, cos_left = sin_cos(left)
    return amplitude * cos_left, amplitude * sin_left


def radix_four(parts):
    (r0, i0), (r1, i1), (r2, i2), (r3, i3) = parts
    even_sum, even_gap = (r0 + r2, i0 + i2), (r0 - r2, i0 - i2)
    odd_sum, odd_gap = (r1 + r3, i1 + i3), (r1 - r3, i1 - i3)
    return (
        (even_sum[0] + odd_sum[0], even_sum[1] + odd_sum[1]),
        (even_gap[0] - odd_gap[1], even_gap[1] + odd_gap[0]),
        (even_sum[0] - odd_sum[0], even_sum[1] - odd_sum[1]),
        (even_gap[0] + odd_gap[1], even_gap[1] - odd_gap[0]),
    )


def store_split(coarse_ref, fine_ref, where, value):
    coarse = value.astype(jnp.bfloat16)
    coarse_ref[where] = coarse
    fine_ref[where] = (value - coarse.astype(jnp.float32)).astype(jnp.bfloat16)


def triple_dot(matrix_ref, e, coarse, fine, dims):
    def product(a, b):
        return lax.dot_general(a, b, (dims, ((), ())), preferred_element_type=jnp.float32)

    return product(matrix_ref[0, e], coarse) + (
        product(matrix_ref[0, e], fine) + product(matrix_ref[1, e], coarse)
    )


def first_lines(params_ref, left_ref, kept_refs, where, freq):
    scale, exponent, inverse_coherence = params_ref[0], params_ref[1], params_ref[2]
    amplitude = amplitude_of(freq, scale, exponent)
    freq_ratio = freq * inverse_coherence
    ratio_square = freq_ratio * freq_ratio
    coherent = 1.0 / (1.0 + ratio_square)
    incoherent = freq_ratio * jnp.sqrt(2.0 + ratio_square) * coherent
    sin_left, cos_left = sin_cos(left_ref[where])
    real, imag = amplitude * cos_left, amplitude * sin_left
    kept_refs[0][where] = coherent * real
    kept_refs[1][where] = coherent * imag
    kept_refs[2][where] = amplitude * incoherent
    return real, imag


def second_lines(right_ref, kept_refs, where):
    sin_right, cos_right = sin_cos(right_ref[where])
    independent = kept_refs[2][where]
    return (
        kept_refs[0][where] + independent * cos_right,
        kept_refs[1][where] + independent * sin_right,
    )


def outer_kernel(track, params_ref, phase_ref, *refs):
    if track == 0:
        matrix_ref, twist_ref, out_ref, *kept_refs, coarse_ref, fine_ref = refs
    else:
        *kept_refs, matrix_ref, twist_ref, out_ref, coarse_ref, fine_ref = refs
    _, tiles, rows, _ = phase_ref.shape
    lane = lax.broadcasted_iota(jnp.int32, (STEP, LANES), 1) + pl.program_id(0) * tiles * LANES
    row = lax.broadcasted_iota(jnp.int32, (STEP, LANES), 0)
    place = row * INNER + lane

    def some_rows(step, carry):
        b = step * STEP
        for tile in range(tiles):
            lines = []
            for a in range(RADIX):
                k1 = a * QUARTER + b
                where = (k1 // rows, tile, pl.ds(pl.multiple_of(k1 % rows, STEP), STEP))
                if track == 0:
                    freq = (place + (k1 * INNER + tile * LANES)).astype(jnp.float32)
                    lines.append(first_lines(params_ref, phase_ref, kept_refs, where, freq))
                else:
                    lines.append(second_lines(phase_ref, kept_refs, where))
            mixed = radix_four(lines)
            for e in range(RADIX):
                for ri in range(2):
                    at = pl.ds(pl.multiple_of(ri * QUARTER + b, STEP), STEP)
                    where = (e, at, pl.ds(tile * LANES, LANES))
                    store_split(coarse_ref, fine_ref, where, mixed[e][ri])
        return carry

    lax.fori_loop(0, QUARTER // STEP, some_rows, 0)
    for e in range(RADIX):
        mid = triple_dot(matrix_ref, e, coarse_ref[e], fine_ref[e], ((1,), (0,)))
        for tile in range(tiles):
            lanes = slice(tile * LANES, (tile + 1) * LANES)
            cos_part, sin_part = twist_ref[0, e, :, lanes], twist_ref[1, e, :, lanes]
            real, imag = mid[:QUARTER, lanes], mid[QUARTER:, lanes]
            out_ref[tile, 0, pl.ds(e, QUARTER, stride=RADIX), :] = real * cos_part - imag * sin_part
            out_ref[tile, 1, pl.ds(e, QUARTER, stride=RADIX), :] = real * sin_part + imag * cos_part


def inner_kernel(mid_ref, matrix_ref, *refs):
    out_refs, (coarse_ref, fine_ref) = refs[:-2], refs[-2:]
    wide = mid_ref.shape[2]
    shards, _, rows, _ = out_refs[0].shape

    def some_rows(step, carry):
        at = pl.multiple_of(step * STEP, STEP)
        for half in range(0, QUARTER, LANES):
            parts = [
                tuple(mid_ref[(a * QUARTER + half) // LANES, ri, pl.ds(at, STEP), :] for ri in range(2))
                for a in range(RADIX)
            ]
            mixed = radix_four(parts)
            for e in range(RADIX):
                for ri in range(2):
                    where = (e, pl.ds(at, STEP), pl.ds(ri * QUARTER + half, LANES))
                    store_split(coarse_ref, fine_ref, where, mixed[e][ri])
        return carry

    lax.fori_loop(0, wide // STEP, some_rows, 0)
    some = rows // RADIX
    for e in range(RADIX):
        value = triple_dot(matrix_ref, e, coarse_ref[e], fine_ref[e], ((1,), (1,)))
        for f in range(shards):
            for part, out_ref in enumerate(out_refs):
                at = (f * len(out_refs) + part) * some
                for tile in range(wide // LANES):
                    out_ref[f, tile, pl.ds(e, some, stride=RADIX), :] = value[
                        at : at + some, tile * LANES : (tile + 1) * LANES
                    ]


def part_kernel(in_ref, out_ref):
    members, tiles, rows, _ = out_ref.shape
    for tile in range(tiles):
        for start in range(0, rows, SUBLANES):
            columns = [((start + r) * tiles + tile) * LANES for r in range(SUBLANES)]
            turned = jnp.transpose(jnp.stack([in_ref[:, at : at + LANES] for at in columns]), (1, 0, 2))
            for m in range(members):
                out_ref[m, tile, start : start + SUBLANES, :] = turned[m]


def join_kernel(extra, in_ref, *refs):
    out_refs = refs[-2:] if extra else refs[-1:]
    members, tiles, rows, _ = in_ref.shape
    for tile in range(tiles):
        for start in range(0, rows, SUBLANES):
            turned = jnp.transpose(in_ref[:, tile, start : start + SUBLANES, :], (1, 0, 2))
            for r in range(SUBLANES):
                at = ((start + r) * tiles + tile) * LANES
                for out_ref in out_refs:
                    out_ref[0, :, at : at + LANES] = turned[r]


def near_kernel(base_ref, own_ref, out_ref):
    members, length = own_ref.shape
    tiles = length // LANES - 1
    scale, exponent = tile_params(own_ref[:, tiles * LANES :])
    lane = lax.broadcasted_iota(jnp.int32, (members, LANES), 1)

    def one_tile(tile, carry):
        at = pl.ds(pl.multiple_of(tile * LANES, LANES), LANES)
        freq = (base_ref[0] + tile * LANES + lane).astype(jnp.float32)
        out_ref[0, :, at], out_ref[1, :, at] = left_lines(own_ref[:, at], freq, scale, exponent)
        return carry

    lax.fori_loop(0, tiles + 1, one_tile, 0)


def tile_params(beyond):
    return (jnp.broadcast_to(beyond[:, n : n + 1], beyond.shape) for n in (1, 2))


def mirror_kernel(base_ref, near_ref, far_ref, edge_ref, beyond_ref, out_ref):
    members, length = far_ref.shape
    tiles = length // LANES - 1
    shape = (members, LANES)
    lane = lax.broadcasted_iota(jnp.int32, shape, 1)
    mirror = (LANES - lane) % LANES
    first_group, last_group = base_ref[1] == 0, base_ref[1] == base_ref[2] - 1
    scale, exponent = tile_params(beyond_ref[...])
    half_root = math.sqrt(0.5)

    def tile_of(ref, tile):
        return ref[:, pl.ds(pl.multiple_of(tile * LANES, LANES), LANES)]

    def turned(value):
        return jnp.take_along_axis(value, mirror, axis=1, mode="promise_in_bounds")

    def store(tile, far, keep, weight):
        offset = base_ref[0] + tile * LANES + lane
        far_offset = jnp.where(offset == 0, 0, OUTER * INNER - offset)
        back = left_lines(far, far_offset.astype(jnp.float32), scale, exponent)
        at = pl.ds(pl.multiple_of(tile * LANES, LANES), LANES)
        real, imag = near_ref[0, :, at] + back[0], near_ref[1, :, at] - back[1]
        out_ref[0, :, at] = jnp.where(keep, real * weight, 0.0)
        out_ref[1, :, at] = jnp.where(keep, imag * weight, 0.0)

    def one_tile(tile, last):
        ahead = turned(tile_of(far_ref, tiles - 1 - tile))
        is_edge = (lane == 0) & (tile == 0) & first_group
        store(tile, jnp.where(lane == 0, last, ahead), lane >= 0, jnp.where(is_edge, half_root, 1.0))
        return ahead

    start = jnp.where(first_group, turned(edge_ref[...]), turned(tile_of(far_ref, tiles)))
    last = lax.fori_loop(0, tiles, one_tile, start)
    store(tiles, jnp.where(lane == 0, last, 0.0), (lane == 0) & last_group, half_root)


def limits():
    return pltpu.CompilerParams(vmem_limit_bytes=VMEM_LIMIT)


def part_call(phase):
    members, length = phase.shape
    rows = length // INNER
    tiles = INNER // LANES
    return pl.pallas_call(
        part_kernel,
        grid=(rows // BLOCK_ROWS,),
        in_specs=[pl.BlockSpec((members, BLOCK_ROWS * INNER), lambda g: (0, g))],
        out_specs=pl.BlockSpec((members, tiles, BLOCK_ROWS, LANES), lambda g: (0, 0, g, 0)),
        out_shape=pltpu.HBM((members, tiles, rows, LANES), jnp.float32),
        compiler_params=limits(),
        cost_estimate=pl.CostEstimate(flops=0, bytes_accessed=8 * members * length, transcendentals=0),
    )(pltpu.with_memory_space_constraint(phase, pltpu.HBM))


def join_call(piece, track, within, length, groups, so_far):
    members, tiles, rows, _ = piece.shape
    stretch = rows * INNER
    steps = rows // BLOCK_ROWS
    piece = pltpu.with_memory_space_constraint(piece, pltpu.HBM)
    operands = (piece,) if so_far is None else (piece, so_far)
    each = max(steps // max(groups, 1), 1)
    return pl.pallas_call(
        functools.partial(join_kernel, groups > 0),
        grid=(steps,),
        in_specs=[
            pl.BlockSpec((members, tiles, BLOCK_ROWS, LANES), lambda g: (0, 0, g, 0)),
            pl.BlockSpec(memory_space=pl.ANY),
        ][: len(operands)],
        out_specs=[
            pl.BlockSpec((1, members, BLOCK_ROWS * INNER), lambda g: (track, 0, within * steps + g)),
            pl.BlockSpec((1, members, BLOCK_ROWS * INNER), lambda g: (g // each, 0, g % each)),
        ][: 2 if groups else 1],
        out_shape=[
            jax.ShapeDtypeStruct((2, members, length), jnp.float32),
            pltpu.HBM((max(groups, 1), members, stretch // max(groups, 1)), jnp.float32),
        ][: 2 if groups else 1],
        input_output_aliases={} if so_far is None else {1: 0},
        compiler_params=limits(),
        cost_estimate=pl.CostEstimate(flops=0, bytes_accessed=12 * members * stretch, transcendentals=0),
    )(*operands)


def outer_call(params, phase, kept, matrices, twists):
    track = 1 if kept else 0
    sources, tiles, rows, _ = phase.shape
    some = OUTER_TILES
    lines = pl.BlockSpec((sources, some, rows, LANES), lambda g: (0, g, 0, 0))
    more = 0 if kept else 3
    return pl.pallas_call(
        functools.partial(outer_kernel, track),
        grid=(tiles // some,),
        in_specs=[pl.BlockSpec(memory_space=pltpu.SMEM)]
        + [lines] * (1 + len(kept))
        + [
            pl.BlockSpec(matrices.shape, lambda g: (0, 0, 0, 0)),
            pl.BlockSpec((2, RADIX, QUARTER, some * LANES), lambda g: (0, 0, 0, g)),
        ],
        out_specs=[pl.BlockSpec((some, 2, OUTER, LANES), lambda g: (g, 0, 0, 0))] + [lines] * more,
        out_shape=[jax.ShapeDtypeStruct((tiles, 2, OUTER, LANES), jnp.float32)]
        + [pltpu.HBM(phase.shape, jnp.float32)] * more,
        scratch_shapes=[pltpu.VMEM((RADIX, 2 * QUARTER, some * LANES), jnp.bfloat16)] * 2,
        compiler_params=limits(),
        cost_estimate=pl.CostEstimate(
            flops=24 * OUTER * QUARTER * INNER, bytes_accessed=32 * OUTER * INNER, transcendentals=0
        ),
    )(params, phase, *kept, matrices, twists)


def inner_call(mid, matrices, shards, parts):
    rows = INNER // shards // parts
    tiles = OUTER // LANES
    return pl.pallas_call(
        inner_kernel,
        grid=(OUTER // WIDE,),
        in_specs=[
            pl.BlockSpec((INNER // LANES, 2, WIDE, LANES), lambda g: (0, 0, g, 0)),
            pl.BlockSpec(matrices.shape, lambda g: (0, 0, 0, 0)),
        ],
        out_specs=[pl.BlockSpec((shards, WIDE // LANES, rows, LANES), lambda g: (0, g, 0, 0))] * parts,
        out_shape=[pltpu.HBM((shards, tiles, rows, LANES), jnp.float32)] * parts,
        scratch_shapes=[pltpu.VMEM((RADIX, WIDE, 2 * QUARTER), jnp.bfloat16)] * 2,
        compiler_params=limits(),
        cost_estimate=pl.CostEstimate(
            flops=12 * OUTER * QUARTER * INNER, bytes_accessed=12 * OUTER * INNER, transcendentals=0
        ),
    )(mid, matrices)


def near_call(base, own):
    members, length = own.shape
    return pl.pallas_call(
        near_kernel,
        in_specs=[pl.BlockSpec(memory_space=pltpu.SMEM), pl.BlockSpec(memory_space=pltpu.VMEM)],
        out_specs=pl.BlockSpec(memory_space=pltpu.VMEM),
        out_shape=jax.ShapeDtypeStruct((2, members, length), jnp.float32),
        compiler_params=limits(),
        cost_estimate=pl.CostEstimate(
            flops=100 * members * length, bytes_accessed=12 * members * length, transcendentals=0
        ),
    )(base, own)


def mirror_call(base, near, far, edge, beyond):
    members, length = far.shape
    return pl.pallas_call(
        mirror_kernel,
        in_specs=[pl.BlockSpec(memory_space=pltpu.SMEM)] + [pl.BlockSpec(memory_space=pltpu.VMEM)] * 4,
        out_specs=pl.BlockSpec(memory_space=pltpu.VMEM),
        out_shape=jax.ShapeDtypeStruct((2, members, length), jnp.float32),
        compiler_params=limits(),
        cost_estimate=pl.CostEstimate(
            flops=100 * members * length, bytes_accessed=20 * members * length, transcendentals=0
        ),
    )(base, near, far, edge, beyond)


def line_params(roughness, waviness, coherence):
    return jnp.stack(
        [jnp.sqrt(2.0 * roughness * (waviness - 1.0) / ANCHOR), -0.5 * waviness, 1.0 / coherence]
    )


def to_group(piece, slot):
    groups = lax.axis_size("mem")
    return lax.ppermute(piece, "mem", [(z, z ^ slot) for z in range(groups)]) if slot else piece


def rows_gram(rows):
    return lax.dot_general(rows, rows, (((1,), (1,)), ((), ())), precision=lax.Precision.HIGH)


def by_slot(stretches, groups):
    my_group = lax.axis_index("mem")
    return [
        lax.dynamic_index_in_dim(stretches, my_group ^ slot, 0, keepdims=False)
        for slot in nearest_last(groups)
    ]


def nearest_last(groups):
    return [(groups - n) % groups for n in range(groups)]


def own_and_far(phase, params, my_group):
    groups = lax.axis_size("mem")
    half = phase.shape[1] // 2
    width = half // groups
    lane = lax.broadcasted_iota(jnp.int32, (phase.shape[0], LANES), 1)

    def lines(start):
        return (
            lax.dynamic_slice_in_dim(phase, start, width, 1),
            lax.dynamic_slice_in_dim(phase, start + width, LANES, 1),
        )

    own, far = [], []
    for slot in nearest_last(groups):
        group = my_group ^ slot
        inner, beyond = lines(group * width)
        for n in range(2):
            beyond = jnp.where(lane == n + 1, params[n][:, None], beyond)
        far_inner, far_beyond = lines(half + (groups - 1 - group) * width)
        message = jnp.concatenate(
            [
                jnp.concatenate([inner, beyond], axis=1)[None],
                jnp.concatenate([far_inner, far_beyond], axis=1)[None],
            ]
        )
        message = to_group(message, slot)
        own.append(message[0])
        far.append(message[1])
    return jnp.concatenate(own, axis=0), jnp.concatenate(far, axis=0)


def edge_of(own):
    shards = lax.axis_size("len")
    return lax.ppermute(own[:, :LANES], "len", [(d, (shards - d) % shards) for d in range(shards)])


def across(far):
    shards = lax.axis_size("len")
    return lax.ppermute(far, "len", [(d, shards - 1 - d) for d in range(shards)])


def line_base(width):
    groups = lax.axis_size("mem")
    my_index, my_group = lax.axis_index("len"), lax.axis_index("mem")
    base = (my_index * (2 * groups) + my_group) * width
    return jnp.stack([base, my_group, jnp.full_like(my_group, groups)]).astype(jnp.int32)


def lines_gram(base, near, far, edge, beyond):
    sums = mirror_call(base, near, far, edge, beyond)
    return rows_gram(sums[0]) + rows_gram(sums[1])


def in_order(gram_matrix, members, slots):
    my_group = lax.axis_index("mem")
    row = lax.broadcasted_iota(jnp.int32, gram_matrix.shape, 0)
    column = lax.broadcasted_iota(jnp.int32, gram_matrix.shape, 1)
    to_slot = False
    for n, slot in enumerate(slots):
        to_slot = to_slot | (((row // members) ^ slot == my_group) & (column // members == n))
    to_slot = (to_slot & (row % members == column % members)).astype(jnp.float32)
    return jnp.dot(jnp.dot(to_slot, gram_matrix, precision=highest), to_slot.T, precision=highest)


def summed(value):
    for axis in ("len", "mem"):
        value = jnp.sum(lax.all_gather(value, axis), axis=0)
    return value


def per_device_whole(phase_left, phase_right, roughness, waviness, coherence):
    shards, groups = lax.axis_size("len"), lax.axis_size("mem")
    my_index = lax.axis_index("len")
    members = phase_left.shape[0]

    def swap(piece):
        return lax.all_to_all(piece, "len", split_axis=0, concat_axis=0, tiled=True)

    all_params = line_params(roughness, waviness, coherence)
    params = lax.dynamic_index_in_dim(all_params, my_index, 1, keepdims=False)
    outer_tables = jnp.asarray(outer_matrices())
    inner_tables = jnp.asarray(inner_matrices())
    twists = jnp.asarray(twist_tables())
    local_len = phase_left.shape[1]

    left, right = part_call(phase_left), part_call(phase_right)
    right, my_group = lax.optimization_barrier((right, lax.axis_index("mem")))
    left, right = lax.optimization_barrier((swap(left), right))
    right = swap(right)
    own, far = own_and_far(phase_left, all_params, my_group)
    mid, *kept = outer_call(params, left, (), outer_tables, twists)
    first = list(inner_call(mid, inner_tables, shards, 2))
    right, *first = lax.optimization_barrier((right, *first))
    early = swap(first[0])
    (mid,) = outer_call(params, right, kept, outer_tables, twists)
    (second,) = inner_call(mid, inner_tables, shards, 1)
    early, second = lax.optimization_barrier((early, second))
    base = line_base(own.shape[1] - LANES)
    near = near_call(base, own)
    second, near, far = lax.optimization_barrier((swap(second), near, far))
    profile, points = join_call(second, 1, 0, local_len, groups, None)
    pieces = by_slot(points, groups)
    rows = [to_group(piece, slot) for slot, piece in zip(nearest_last(groups), pieces)]
    _, first[1], edge, far = lax.optimization_barrier((pieces, first[1], own, far))
    late = swap(first[1])
    line_gram = lines_gram(base, near, across(far), edge_of(edge), own[:, -LANES:])
    (profile,) = join_call(early, 0, 0, local_len, 0, profile)
    late, line_gram = lax.optimization_barrier((late, line_gram))
    (profile,) = join_call(late, 0, 1, local_len, 0, profile)
    profile, line_gram, rows = lax.optimization_barrier((profile, line_gram, rows))
    gram_matrix = 0.25 * line_gram + (0.5 / (OUTER * INNER)) * rows_gram(jnp.concatenate(rows, axis=0))
    return (profile, upper_of(summed(in_order(gram_matrix, members, nearest_last(groups)))))


def per_device(phase_left, phase_right, roughness, waviness, coherence):
    whole_members = phase_left.shape[0] == lax.axis_size("len") and lax.axis_size("mem") in (2, 4)
    form = per_device_whole if whole_members else per_device_spread
    return form(phase_left, phase_right, roughness, waviness, coherence)


def solution(mesh):
    placed = (P("mem", "len"), P("mem", "len"), P("mem"), P("mem"), P("mem"))
    return jax.shard_map(
        per_device,
        mesh=mesh,
        in_specs=placed,
        out_specs=(P(None, "mem", "len"), P()),
        check_vma=False,
    )
```

```python
import functools
import math

import jax
import jax.numpy as jnp
import numpy as np
from jax import lax
from jax.experimental import pallas as pl
from jax.experimental.pallas import tpu as pltpu
from jax.sharding import PartitionSpec as P

OUTER = 1024
INNER = 1024
ANCHOR = 64
RADIX = 4
QUARTER = 256
LANES = 128
STEP = 16
SUBLANES = 8
WIDE = 256
BLOCK_ROWS = 16
OUTER_TILES = 2
VMEM_LIMIT = 48 * 1024 * 1024
SIN_HALF = (0.49999999785787, -0.02083332246218, 2.604078316692e-4, -1.547581723527e-6, 5.088214043e-9)
COS_HALF = (
    0.99999999977982,
    -0.12499999839235,
    2.604164763023e-3,
    -2.170056380508e-5,
    9.67192778775e-8,
    -2.5440497557e-10,
)


highest = lax.Precision.HIGHEST


def merged(shard, axis, combine):
    everything = lax.all_gather(shard, axis)
    leading = everything[0]

    def step(k, so_far):
        return combine(so_far, everything[k])

    return lax.fori_loop(1, lax.axis_size(axis), step, leading)


def dft_tables(length):
    index = lax.iota(jnp.int32, length)
    product = index[:, None] * index[None, :] % length
    phase_angle = product.astype(jnp.float32) * (2.0 * math.pi / length)
    return (jnp.cos(phase_angle), jnp.sin(phase_angle))


def spectra_of(phase_left, phase_right, roughness, waviness, coherence, freq):
    amplitude = jnp.sqrt(2.0 * roughness * (waviness - 1.0) / ANCHOR)[:, None] * (
        (freq + ANCHOR) / ANCHOR
    ) ** (-0.5 * waviness[:, None])
    freq_ratio = freq / coherence[:, None]
    coherent = 1.0 / (1.0 + freq_ratio * freq_ratio)
    incoherent = freq_ratio * jnp.sqrt(2.0 + freq_ratio * freq_ratio) * coherent
    cos_left = jnp.cos(phase_left)
    sin_left = jnp.sin(phase_left)
    cos_right = jnp.cos(phase_right)
    sin_right = jnp.sin(phase_right)
    real_part = jnp.stack(
        [amplitude * cos_left, amplitude * (coherent * cos_left + incoherent * cos_right)]
    )
    imag_part = jnp.stack(
        [amplitude * sin_left, amplitude * (coherent * sin_left + incoherent * sin_right)]
    )
    return (real_part, imag_part)


def upper_of(gram_matrix):
    return jnp.linalg.cholesky(gram_matrix).T


def combine_factors(upper_a, upper_b):
    gram_matrix = jnp.dot(upper_a.T, upper_a, precision=highest) + jnp.dot(
        upper_b.T, upper_b, precision=highest
    )
    return upper_of(gram_matrix)


def gram_of(snapshot):
    return jnp.einsum("tmr,tnr->mn", snapshot, snapshot, precision=highest)


def per_device_spread(phase_left, phase_right, roughness, waviness, coherence):
    shards = lax.axis_size("len")
    my_index = lax.axis_index("len")
    local_members, local_len = phase_left.shape
    columns = 2 * local_members
    outer_block = OUTER // shards
    inner_block = INNER // shards

    def to_rows(part):
        shaped = part.reshape(2, local_members, inner_block, OUTER)
        return jnp.transpose(shaped, (2, 3, 0, 1)).reshape(
            inner_block, shards, outer_block * columns
        )

    inner_cos, inner_sin = dft_tables(INNER)
    freq = (my_index * local_len + lax.iota(jnp.int32, local_len)).astype(jnp.float32)[None, :]
    real_part, imag_part = spectra_of(phase_left, phase_right, roughness, waviness, coherence, freq)
    pieces = (
        lax.all_to_all(to_rows(real_part), "len", split_axis=1, concat_axis=0, tiled=True),
        lax.all_to_all(to_rows(imag_part), "len", split_axis=1, concat_axis=0, tiled=True),
    )
    real_in = pieces[0].reshape(INNER, -1)
    imag_in = pieces[1].reshape(INNER, -1)
    real_out = jnp.dot(inner_cos, real_in, precision=highest) - jnp.dot(
        inner_sin, imag_in, precision=highest
    )
    imag_out = jnp.dot(inner_cos, imag_in, precision=highest) + jnp.dot(
        inner_sin, real_in, precision=highest
    )
    row_index = lax.iota(jnp.int32, INNER)[:, None]
    outer_index = (my_index * outer_block + lax.iota(jnp.int32, outer_block))[None, :]
    twist = (row_index * outer_index % (OUTER * INNER)).astype(jnp.float32) * (
        2.0 * math.pi / (OUTER * INNER)
    )
    twist_cos = jnp.repeat(jnp.cos(twist), columns, axis=1)
    twist_sin = jnp.repeat(jnp.sin(twist), columns, axis=1)
    rot_real = (real_out * twist_cos - imag_out * twist_sin).reshape(
        shards, inner_block, outer_block * columns
    )
    rot_imag = (real_out * twist_sin + imag_out * twist_cos).reshape(
        shards, inner_block, outer_block * columns
    )
    outer_cos, outer_sin = dft_tables(OUTER)
    outer_cos = outer_cos.reshape(OUTER, shards, outer_block)
    outer_sin = outer_sin.reshape(OUTER, shards, outer_block)
    pieces = (
        lax.all_to_all(rot_real, "len", split_axis=0, concat_axis=0, tiled=True),
        lax.all_to_all(rot_imag, "len", split_axis=0, concat_axis=0, tiled=True),
    )
    item_count = pieces[0].shape[1]
    real_in = pieces[0].reshape(shards, item_count, outer_block, columns)
    imag_in = pieces[1].reshape(shards, item_count, outer_block, columns)
    first = jnp.einsum("jqa,qiac->cij", outer_cos, real_in, precision=highest)
    second = jnp.einsum("jqa,qiac->cij", outer_sin, imag_in, precision=highest)
    profile_block = first - second
    outgoing = jnp.transpose(
        profile_block.reshape(columns, inner_block, shards, outer_block), (2, 0, 1, 3)
    ).reshape(shards, -1)
    arrived = lax.all_to_all(outgoing, "len", split_axis=0, concat_axis=0, tiled=True)
    profile = jnp.transpose(
        arrived.reshape(shards, columns, inner_block, outer_block), (1, 3, 0, 2)
    ).reshape(2, local_members, local_len)
    scale = 1.0 / math.sqrt(2.0 * OUTER * INNER)
    snapshot = profile_block.reshape(2, local_members, inner_block * OUTER) * scale
    gathered = lax.all_gather(snapshot, "mem", axis=1, tiled=True)
    gram_local = gram_of(gathered)
    r_factor = merged(upper_of(gram_local), "len", combine_factors)
    return (profile, r_factor)


def host_cis(product, period):
    angle = product % period * (2.0 * np.pi / period)
    return np.cos(angle), np.sin(angle)


def split_host(table):
    coarse = table.astype(np.float32).astype(jnp.bfloat16)
    fine = (table - coarse.astype(np.float64)).astype(np.float32).astype(jnp.bfloat16)
    return np.stack([coarse, fine])


def outer_matrices():
    c, e, b = np.arange(QUARTER), np.arange(RADIX), np.arange(QUARTER)
    cos_part, sin_part = host_cis((RADIX * c[None, :, None] + e[:, None, None]) * b[None, None, :], OUTER)
    upper = np.concatenate([cos_part, -sin_part], axis=2)
    lower = np.concatenate([sin_part, cos_part], axis=2)
    return split_host(np.concatenate([upper, lower], axis=1))


def inner_matrices():
    c, e, b = np.arange(QUARTER), np.arange(RADIX), np.arange(QUARTER)
    cos_part, sin_part = host_cis((RADIX * c[None, :, None] + e[:, None, None]) * b[None, None, :], INNER)
    return split_host(np.concatenate([cos_part, -sin_part], axis=2))


def twist_tables():
    j1 = RADIX * np.arange(QUARTER)[None, :, None] + np.arange(RADIX)[:, None, None]
    cos_part, sin_part = host_cis(j1 * np.arange(INNER)[None, None, :], OUTER * INNER)
    return np.stack([cos_part, sin_part]).astype(np.float32)


def sin_cos(angle):
    square = angle * angle

    def series(coefficients):
        total = jnp.float32(coefficients[-1])
        for coefficient in coefficients[-2::-1]:
            total = total * square + jnp.float32(coefficient)
        return total

    half_sin = angle * series(SIN_HALF)
    half_cos = series(COS_HALF)
    twice = half_sin + half_sin
    return twice * half_cos, 1.0 - twice * half_sin


def amplitude_of(freq, scale, exponent):
    return scale * jnp.exp2(exponent * jnp.log2((freq + ANCHOR) * (1.0 / ANCHOR)))


def left_lines(left, freq, scale, exponent):
    amplitude = amplitude_of(freq, scale, exponent)
    sin_left, cos_left = sin_cos(left)
    return amplitude * cos_left, amplitude * sin_left


def radix_four(parts):
    (r0, i0), (r1, i1), (r2, i2), (r3, i3) = parts
    even_sum, even_gap = (r0 + r2, i0 + i2), (r0 - r2, i0 - i2)
    odd_sum, odd_gap = (r1 + r3, i1 + i3), (r1 - r3, i1 - i3)
    return (
        (even_sum[0] + odd_sum[0], even_sum[1] + odd_sum[1]),
        (even_gap[0] - odd_gap[1], even_gap[1] + odd_gap[0]),
        (even_sum[0] - odd_sum[0], even_sum[1] - odd_sum[1]),
        (even_gap[0] + odd_gap[1], even_gap[1] - odd_gap[0]),
    )


def store_split(coarse_ref, fine_ref, where, value):
    coarse = value.astype(jnp.bfloat16)
    coarse_ref[where] = coarse
    fine_ref[where] = (value - coarse.astype(jnp.float32)).astype(jnp.bfloat16)


def triple_dot(matrix_ref, e, coarse, fine, dims):
    def product(a, b):
        return lax.dot_general(a, b, (dims, ((), ())), preferred_element_type=jnp.float32)

    return product(matrix_ref[0, e], coarse) + (
        product(matrix_ref[0, e], fine) + product(matrix_ref[1, e], coarse)
    )


def first_lines(params_ref, left_ref, kept_refs, where, freq):
    scale, exponent, inverse_coherence = params_ref[0], params_ref[1], params_ref[2]
    amplitude = amplitude_of(freq, scale, exponent)
    freq_ratio = freq * inverse_coherence
    ratio_square = freq_ratio * freq_ratio
    coherent = 1.0 / (1.0 + ratio_square)
    incoherent = freq_ratio * jnp.sqrt(2.0 + ratio_square) * coherent
    sin_left, cos_left = sin_cos(left_ref[where])
    real, imag = amplitude * cos_left, amplitude * sin_left
    kept_refs[0][where] = coherent * real
    kept_refs[1][where] = coherent * imag
    kept_refs[2][where] = amplitude * incoherent
    return real, imag


def second_lines(right_ref, kept_refs, where):
    sin_right, cos_right = sin_cos(right_ref[where])
    independent = kept_refs[2][where]
    return (
        kept_refs[0][where] + independent * cos_right,
        kept_refs[1][where] + independent * sin_right,
    )


def outer_kernel(track, params_ref, phase_ref, *refs):
    if track == 0:
        matrix_ref, twist_ref, out_ref, *kept_refs, coarse_ref, fine_ref = refs
    else:
        *kept_refs, matrix_ref, twist_ref, out_ref, coarse_ref, fine_ref = refs
    _, tiles, rows, _ = phase_ref.shape
    lane = lax.broadcasted_iota(jnp.int32, (STEP, LANES), 1) + pl.program_id(0) * tiles * LANES
    row = lax.broadcasted_iota(jnp.int32, (STEP, LANES), 0)
    place = row * INNER + lane

    def some_rows(step, carry):
        b = step * STEP
        for tile in range(tiles):
            lines = []
            for a in range(RADIX):
                k1 = a * QUARTER + b
                where = (k1 // rows, tile, pl.ds(pl.multiple_of(k1 % rows, STEP), STEP))
                if track == 0:
                    freq = (place + (k1 * INNER + tile * LANES)).astype(jnp.float32)
                    lines.append(first_lines(params_ref, phase_ref, kept_refs, where, freq))
                else:
                    lines.append(second_lines(phase_ref, kept_refs, where))
            mixed = radix_four(lines)
            for e in range(RADIX):
                for ri in range(2):
                    at = pl.ds(pl.multiple_of(ri * QUARTER + b, STEP), STEP)
                    where = (e, at, pl.ds(tile * LANES, LANES))
                    store_split(coarse_ref, fine_ref, where, mixed[e][ri])
        return carry

    lax.fori_loop(0, QUARTER // STEP, some_rows, 0)
    for e in range(RADIX):
        mid = triple_dot(matrix_ref, e, coarse_ref[e], fine_ref[e], ((1,), (0,)))
        for tile in range(tiles):
            lanes = slice(tile * LANES, (tile + 1) * LANES)
            cos_part, sin_part = twist_ref[0, e, :, lanes], twist_ref[1, e, :, lanes]
            real, imag = mid[:QUARTER, lanes], mid[QUARTER:, lanes]
            out_ref[tile, 0, pl.ds(e, QUARTER, stride=RADIX), :] = real * cos_part - imag * sin_part
            out_ref[tile, 1, pl.ds(e, QUARTER, stride=RADIX), :] = real * sin_part + imag * cos_part


def inner_kernel(mid_ref, matrix_ref, *refs):
    out_refs, (coarse_ref, fine_ref) = refs[:-2], refs[-2:]
    wide = mid_ref.shape[2]
    shards, _, rows, _ = out_refs[0].shape

    def some_rows(step, carry):
        at = pl.multiple_of(step * STEP, STEP)
        for half in range(0, QUARTER, LANES):
            parts = [
                tuple(mid_ref[(a * QUARTER + half) // LANES, ri, pl.ds(at, STEP), :] for ri in range(2))
                for a in range(RADIX)
            ]
            mixed = radix_four(parts)
            for e in range(RADIX):
                for ri in range(2):
                    where = (e, pl.ds(at, STEP), pl.ds(ri * QUARTER + half, LANES))
                    store_split(coarse_ref, fine_ref, where, mixed[e][ri])
        return carry

    lax.fori_loop(0, wide // STEP, some_rows, 0)
    some = rows // RADIX
    for e in range(RADIX):
        value = triple_dot(matrix_ref, e, coarse_ref[e], fine_ref[e], ((1,), (1,)))
        for f in range(shards):
            for part, out_ref in enumerate(out_refs):
                at = (f * len(out_refs) + part) * some
                for tile in range(wide // LANES):
                    out_ref[f, tile, pl.ds(e, some, stride=RADIX), :] = value[
                        at : at + some, tile * LANES : (tile + 1) * LANES
                    ]


def part_kernel(in_ref, out_ref):
    members, tiles, rows, _ = out_ref.shape
    for tile in range(tiles):
        for start in range(0, rows, SUBLANES):
            columns = [((start + r) * tiles + tile) * LANES for r in range(SUBLANES)]
            turned = jnp.transpose(jnp.stack([in_ref[:, at : at + LANES] for at in columns]), (1, 0, 2))
            for m in range(members):
                out_ref[m, tile, start : start + SUBLANES, :] = turned[m]


def join_kernel(in_ref, *refs):
    join_rows(in_ref, refs[-1].at[0])


def join_rows(in_ref, out_ref):
    _, tiles, rows, _ = in_ref.shape
    for tile in range(tiles):
        for start in range(0, rows, SUBLANES):
            turned = jnp.transpose(in_ref[:, tile, start : start + SUBLANES, :], (1, 0, 2))
            for r in range(SUBLANES):
                at = ((start + r) * tiles + tile) * LANES
                out_ref[:, at : at + LANES] = turned[r]


def pieces_kernel(each, group_ref, in_ref, *out_refs):
    for n, out_ref in enumerate(out_refs):

        @pl.when(pl.program_id(0) // each == n)
        def _(out_ref=out_ref):
            join_rows(in_ref, out_ref)


def near_kernel(base_ref, own_ref, out_ref):
    members, length = own_ref.shape
    tiles = length // LANES - 1
    scale, exponent = tile_params(own_ref[:, tiles * LANES :])
    lane = lax.broadcasted_iota(jnp.int32, (members, LANES), 1)

    def one_tile(tile, carry):
        at = pl.ds(pl.multiple_of(tile * LANES, LANES), LANES)
        freq = (base_ref[0] + tile * LANES + lane).astype(jnp.float32)
        out_ref[0, :, at], out_ref[1, :, at] = left_lines(own_ref[:, at], freq, scale, exponent)
        return carry

    lax.fori_loop(0, tiles + 1, one_tile, 0)


def tile_params(beyond):
    return (jnp.broadcast_to(beyond[:, n : n + 1], beyond.shape) for n in (1, 2))


def mirror_kernel(base_ref, near_ref, far_ref, edge_ref, beyond_ref, out_ref):
    members, length = far_ref.shape
    tiles = length // LANES - 1
    shape = (members, LANES)
    lane = lax.broadcasted_iota(jnp.int32, shape, 1)
    mirror = (LANES - lane) % LANES
    first_group, last_group = base_ref[1] == 0, base_ref[1] == base_ref[2] - 1
    scale, exponent = tile_params(beyond_ref[...])
    half_root = math.sqrt(0.5)

    def tile_of(ref, tile):
        return ref[:, pl.ds(pl.multiple_of(tile * LANES, LANES), LANES)]

    def turned(value):
        return jnp.take_along_axis(value, mirror, axis=1, mode="promise_in_bounds")

    def store(tile, far, keep, weight):
        offset = base_ref[0] + tile * LANES + lane
        far_offset = jnp.where(offset == 0, 0, OUTER * INNER - offset)
        back = left_lines(far, far_offset.astype(jnp.float32), scale, exponent)
        at = pl.ds(pl.multiple_of(tile * LANES, LANES), LANES)
        real, imag = near_ref[0, :, at] + back[0], near_ref[1, :, at] - back[1]
        out_ref[0, :, at] = jnp.where(keep, real * weight, 0.0)
        out_ref[1, :, at] = jnp.where(keep, imag * weight, 0.0)

    def one_tile(tile, last):
        ahead = turned(tile_of(far_ref, tiles - 1 - tile))
        is_edge = (lane == 0) & (tile == 0) & first_group
        store(tile, jnp.where(lane == 0, last, ahead), lane >= 0, jnp.where(is_edge, half_root, 1.0))
        return ahead

    start = jnp.where(first_group, turned(edge_ref[...]), turned(tile_of(far_ref, tiles)))
    last = lax.fori_loop(0, tiles, one_tile, start)
    store(tiles, jnp.where(lane == 0, last, 0.0), (lane == 0) & last_group, half_root)


def limits():
    return pltpu.CompilerParams(vmem_limit_bytes=VMEM_LIMIT)


def part_call(phase):
    members, length = phase.shape
    rows = length // INNER
    tiles = INNER // LANES
    return pl.pallas_call(
        part_kernel,
        grid=(rows // BLOCK_ROWS,),
        in_specs=[pl.BlockSpec((members, BLOCK_ROWS * INNER), lambda g: (0, g))],
        out_specs=pl.BlockSpec((members, tiles, BLOCK_ROWS, LANES), lambda g: (0, 0, g, 0)),
        out_shape=pltpu.HBM((members, tiles, rows, LANES), jnp.float32),
        compiler_params=limits(),
        cost_estimate=pl.CostEstimate(flops=0, bytes_accessed=8 * members * length, transcendentals=0),
    )(pltpu.with_memory_space_constraint(phase, pltpu.HBM))


def join_call(piece, track, within, length, so_far):
    members, tiles, rows, _ = piece.shape
    steps = rows // BLOCK_ROWS
    piece = pltpu.with_memory_space_constraint(piece, pltpu.HBM)
    operands = (piece,) if so_far is None else (piece, so_far)
    return pl.pallas_call(
        join_kernel,
        grid=(steps,),
        in_specs=[
            pl.BlockSpec((members, tiles, BLOCK_ROWS, LANES), lambda g: (0, 0, g, 0)),
            pl.BlockSpec(memory_space=pl.ANY),
        ][: len(operands)],
        out_specs=pl.BlockSpec((1, members, BLOCK_ROWS * INNER), lambda g: (track, 0, within * steps + g)),
        out_shape=jax.ShapeDtypeStruct((2, members, length), jnp.float32),
        input_output_aliases={} if so_far is None else {1: 0},
        compiler_params=limits(),
        cost_estimate=pl.CostEstimate(flops=0, bytes_accessed=8 * members * rows * INNER, transcendentals=0),
    )(*operands)


def pieces_call(my_group, piece, groups):
    members, tiles, rows, _ = piece.shape
    each = rows // BLOCK_ROWS // groups

    def source(g, group_ref):
        slot = (groups - g // each) % groups
        return (0, 0, (slot ^ group_ref[0]) * each + g % each, 0)

    def place(n):
        return lambda g, group_ref: (0, jnp.clip(g - n * each, 0, each - 1))

    return pl.pallas_call(
        functools.partial(pieces_kernel, each),
        grid_spec=pltpu.PrefetchScalarGridSpec(
            num_scalar_prefetch=1,
            grid=(groups * each,),
            in_specs=[pl.BlockSpec((members, tiles, BLOCK_ROWS, LANES), source)],
            out_specs=[pl.BlockSpec((members, BLOCK_ROWS * INNER), place(n)) for n in range(groups)],
        ),
        out_shape=[pltpu.HBM((members, rows // groups * INNER), jnp.float32)] * groups,
        compiler_params=limits(),
        cost_estimate=pl.CostEstimate(flops=0, bytes_accessed=8 * members * rows * INNER, transcendentals=0),
    )(my_group.astype(jnp.int32).reshape(1), pltpu.with_memory_space_constraint(piece, pltpu.HBM))


def outer_call(params, phase, kept, matrices, twists):
    track = 1 if kept else 0
    sources, tiles, rows, _ = phase.shape
    some = OUTER_TILES
    lines = pl.BlockSpec((sources, some, rows, LANES), lambda g: (0, g, 0, 0))
    more = 0 if kept else 3
    return pl.pallas_call(
        functools.partial(outer_kernel, track),
        grid=(tiles // some,),
        in_specs=[pl.BlockSpec(memory_space=pltpu.SMEM)]
        + [lines] * (1 + len(kept))
        + [
            pl.BlockSpec(matrices.shape, lambda g: (0, 0, 0, 0)),
            pl.BlockSpec((2, RADIX, QUARTER, some * LANES), lambda g: (0, 0, 0, g)),
        ],
        out_specs=[pl.BlockSpec((some, 2, OUTER, LANES), lambda g: (g, 0, 0, 0))] + [lines] * more,
        out_shape=[jax.ShapeDtypeStruct((tiles, 2, OUTER, LANES), jnp.float32)]
        + [pltpu.HBM(phase.shape, jnp.float32)] * more,
        scratch_shapes=[pltpu.VMEM((RADIX, 2 * QUARTER, some * LANES), jnp.bfloat16)] * 2,
        compiler_params=limits(),
        cost_estimate=pl.CostEstimate(
            flops=24 * OUTER * QUARTER * INNER, bytes_accessed=32 * OUTER * INNER, transcendentals=0
        ),
    )(params, phase, *kept, matrices, twists)


def inner_call(mid, matrices, shards, parts):
    rows = INNER // shards // parts
    tiles = OUTER // LANES
    return pl.pallas_call(
        inner_kernel,
        grid=(OUTER // WIDE,),
        in_specs=[
            pl.BlockSpec((INNER // LANES, 2, WIDE, LANES), lambda g: (0, 0, g, 0)),
            pl.BlockSpec(matrices.shape, lambda g: (0, 0, 0, 0)),
        ],
        out_specs=[pl.BlockSpec((shards, WIDE // LANES, rows, LANES), lambda g: (0, g, 0, 0))] * parts,
        out_shape=[pltpu.HBM((shards, tiles, rows, LANES), jnp.float32)] * parts,
        scratch_shapes=[pltpu.VMEM((RADIX, WIDE, 2 * QUARTER), jnp.bfloat16)] * 2,
        compiler_params=limits(),
        cost_estimate=pl.CostEstimate(
            flops=12 * OUTER * QUARTER * INNER, bytes_accessed=12 * OUTER * INNER, transcendentals=0
        ),
    )(mid, matrices)


def near_call(base, own):
    members, length = own.shape
    return pl.pallas_call(
        near_kernel,
        in_specs=[pl.BlockSpec(memory_space=pltpu.SMEM), pl.BlockSpec(memory_space=pltpu.VMEM)],
        out_specs=pl.BlockSpec(memory_space=pltpu.VMEM),
        out_shape=jax.ShapeDtypeStruct((2, members, length), jnp.float32),
        compiler_params=limits(),
        cost_estimate=pl.CostEstimate(
            flops=100 * members * length, bytes_accessed=12 * members * length, transcendentals=0
        ),
    )(base, own)


def mirror_call(base, near, far, edge, beyond):
    members, length = far.shape
    return pl.pallas_call(
        mirror_kernel,
        in_specs=[pl.BlockSpec(memory_space=pltpu.SMEM)] + [pl.BlockSpec(memory_space=pltpu.VMEM)] * 4,
        out_specs=pl.BlockSpec(memory_space=pltpu.VMEM),
        out_shape=jax.ShapeDtypeStruct((2, members, length), jnp.float32),
        compiler_params=limits(),
        cost_estimate=pl.CostEstimate(
            flops=100 * members * length, bytes_accessed=20 * members * length, transcendentals=0
        ),
    )(base, near, far, edge, beyond)


def line_params(roughness, waviness, coherence):
    return jnp.stack(
        [jnp.sqrt(2.0 * roughness * (waviness - 1.0) / ANCHOR), -0.5 * waviness, 1.0 / coherence]
    )


def to_group(piece, slot):
    groups = lax.axis_size("mem")
    return lax.ppermute(piece, "mem", [(z, z ^ slot) for z in range(groups)]) if slot else piece


def rows_gram(rows):
    return lax.dot_general(rows, rows, (((1,), (1,)), ((), ())), precision=lax.Precision.HIGH)


def nearest_last(groups):
    return [(groups - n) % groups for n in range(groups)]


def own_and_far(phase, params, my_group):
    groups = lax.axis_size("mem")
    half = phase.shape[1] // 2
    width = half // groups
    lane = lax.broadcasted_iota(jnp.int32, (phase.shape[0], LANES), 1)

    def lines(start):
        return (
            lax.dynamic_slice_in_dim(phase, start, width, 1),
            lax.dynamic_slice_in_dim(phase, start + width, LANES, 1),
        )

    own, far = [], []
    for slot in nearest_last(groups):
        group = my_group ^ slot
        inner, beyond = lines(group * width)
        for n in range(2):
            beyond = jnp.where(lane == n + 1, params[n][:, None], beyond)
        far_inner, far_beyond = lines(half + (groups - 1 - group) * width)
        message = jnp.concatenate(
            [
                jnp.concatenate([inner, beyond], axis=1)[None],
                jnp.concatenate([far_inner, far_beyond], axis=1)[None],
            ]
        )
        message = to_group(message, slot)
        own.append(message[0])
        far.append(message[1])
    return jnp.concatenate(own, axis=0), jnp.concatenate(far, axis=0)


def edge_of(own):
    shards = lax.axis_size("len")
    return lax.ppermute(own[:, :LANES], "len", [(d, (shards - d) % shards) for d in range(shards)])


def across(far):
    shards = lax.axis_size("len")
    return lax.ppermute(far, "len", [(d, shards - 1 - d) for d in range(shards)])


def line_base(width):
    groups = lax.axis_size("mem")
    my_index, my_group = lax.axis_index("len"), lax.axis_index("mem")
    base = (my_index * (2 * groups) + my_group) * width
    return jnp.stack([base, my_group, jnp.full_like(my_group, groups)]).astype(jnp.int32)


def lines_gram(base, near, far, edge, beyond):
    sums = mirror_call(base, near, far, edge, beyond)
    return rows_gram(sums[0]) + rows_gram(sums[1])


def in_order(gram_matrix, members, slots):
    my_group = lax.axis_index("mem")
    row = lax.broadcasted_iota(jnp.int32, gram_matrix.shape, 0)
    column = lax.broadcasted_iota(jnp.int32, gram_matrix.shape, 1)
    to_slot = False
    for n, slot in enumerate(slots):
        to_slot = to_slot | (((row // members) ^ slot == my_group) & (column // members == n))
    to_slot = (to_slot & (row % members == column % members)).astype(jnp.float32)
    return jnp.dot(jnp.dot(to_slot, gram_matrix, precision=highest), to_slot.T, precision=highest)


def summed(value):
    for axis in ("len", "mem"):
        value = jnp.sum(lax.all_gather(value, axis), axis=0)
    return value


def per_device_whole(phase_left, phase_right, roughness, waviness, coherence):
    shards, groups = lax.axis_size("len"), lax.axis_size("mem")
    my_index = lax.axis_index("len")
    members = phase_left.shape[0]

    def swap(piece):
        return lax.all_to_all(piece, "len", split_axis=0, concat_axis=0, tiled=True)

    all_params = line_params(roughness, waviness, coherence)
    params = lax.dynamic_index_in_dim(all_params, my_index, 1, keepdims=False)
    outer_tables = jnp.asarray(outer_matrices())
    inner_tables = jnp.asarray(inner_matrices())
    twists = jnp.asarray(twist_tables())
    local_len = phase_left.shape[1]

    left, right = part_call(phase_left), part_call(phase_right)
    right, my_group = lax.optimization_barrier((right, lax.axis_index("mem")))
    left, right = lax.optimization_barrier((swap(left), right))
    right = swap(right)
    own, far = own_and_far(phase_left, all_params, my_group)
    mid, *kept = outer_call(params, left, (), outer_tables, twists)
    first = list(inner_call(mid, inner_tables, shards, 2))
    right, *first = lax.optimization_barrier((right, *first))
    early = swap(first[0])
    (mid,) = outer_call(params, right, kept, outer_tables, twists)
    (second,) = inner_call(mid, inner_tables, shards, 1)
    early, second = lax.optimization_barrier((early, second))
    base = line_base(own.shape[1] - LANES)
    near = near_call(base, own)
    second, near, far = lax.optimization_barrier((swap(second), near, far))
    pieces = pieces_call(lax.axis_index("mem"), second, groups)
    rows = [to_group(piece, slot) for slot, piece in zip(nearest_last(groups), pieces)]
    _, first[1], edge, far, second = lax.optimization_barrier((pieces, first[1], own, far, second))
    profile = join_call(second, 1, 0, local_len, None)
    late = swap(first[1])
    line_gram = lines_gram(base, near, across(far), edge_of(edge), own[:, -LANES:])
    profile = join_call(early, 0, 0, local_len, profile)
    late, line_gram = lax.optimization_barrier((late, line_gram))
    profile = join_call(late, 0, 1, local_len, profile)
    profile, line_gram, rows = lax.optimization_barrier((profile, line_gram, rows))
    gram_matrix = 0.25 * line_gram + (0.5 / (OUTER * INNER)) * rows_gram(jnp.concatenate(rows, axis=0))
    return (profile, upper_of(summed(in_order(gram_matrix, members, nearest_last(groups)))))


def per_device(phase_left, phase_right, roughness, waviness, coherence):
    whole_members = phase_left.shape[0] == lax.axis_size("len") and lax.axis_size("mem") in (2, 4)
    form = per_device_whole if whole_members else per_device_spread
    return form(phase_left, phase_right, roughness, waviness, coherence)


def solution(mesh):
    placed = (P("mem", "len"), P("mem", "len"), P("mem"), P("mem"), P("mem"))
    return jax.shard_map(
        per_device,
        mesh=mesh,
        in_specs=placed,
        out_specs=(P(None, "mem", "len"), P()),
        check_vma=False,
    )
```

```python
import functools
import math

import jax
import jax.numpy as jnp
import numpy as np
from jax import lax
from jax.experimental import pallas as pl
from jax.experimental.pallas import tpu as pltpu
from jax.sharding import PartitionSpec as P

OUTER = 1024
INNER = 1024
ANCHOR = 64
RADIX = 4
QUARTER = 256
LANES = 128
STEP = 16
SUBLANES = 8
WIDE = 256
BLOCK_ROWS = 16
OUTER_TILES = 2
VMEM_LIMIT = 48 * 1024 * 1024
SIN_HALF = (0.49999999785787, -0.02083332246218, 2.604078316692e-4, -1.547581723527e-6, 5.088214043e-9)
COS_HALF = (
    0.99999999977982,
    -0.12499999839235,
    2.604164763023e-3,
    -2.170056380508e-5,
    9.67192778775e-8,
    -2.5440497557e-10,
)


highest = lax.Precision.HIGHEST


def merged(shard, axis, combine):
    everything = lax.all_gather(shard, axis)
    leading = everything[0]

    def step(k, so_far):
        return combine(so_far, everything[k])

    return lax.fori_loop(1, lax.axis_size(axis), step, leading)


def dft_tables(length):
    index = lax.iota(jnp.int32, length)
    product = index[:, None] * index[None, :] % length
    phase_angle = product.astype(jnp.float32) * (2.0 * math.pi / length)
    return (jnp.cos(phase_angle), jnp.sin(phase_angle))


def spectra_of(phase_left, phase_right, roughness, waviness, coherence, freq):
    amplitude = jnp.sqrt(2.0 * roughness * (waviness - 1.0) / ANCHOR)[:, None] * (
        (freq + ANCHOR) / ANCHOR
    ) ** (-0.5 * waviness[:, None])
    freq_ratio = freq / coherence[:, None]
    coherent = 1.0 / (1.0 + freq_ratio * freq_ratio)
    incoherent = freq_ratio * jnp.sqrt(2.0 + freq_ratio * freq_ratio) * coherent
    cos_left = jnp.cos(phase_left)
    sin_left = jnp.sin(phase_left)
    cos_right = jnp.cos(phase_right)
    sin_right = jnp.sin(phase_right)
    real_part = jnp.stack(
        [amplitude * cos_left, amplitude * (coherent * cos_left + incoherent * cos_right)]
    )
    imag_part = jnp.stack(
        [amplitude * sin_left, amplitude * (coherent * sin_left + incoherent * sin_right)]
    )
    return (real_part, imag_part)


def upper_of(gram_matrix):
    return jnp.linalg.cholesky(gram_matrix).T


def combine_factors(upper_a, upper_b):
    gram_matrix = jnp.dot(upper_a.T, upper_a, precision=highest) + jnp.dot(
        upper_b.T, upper_b, precision=highest
    )
    return upper_of(gram_matrix)


def gram_of(snapshot):
    return jnp.einsum("tmr,tnr->mn", snapshot, snapshot, precision=highest)


def per_device_spread(phase_left, phase_right, roughness, waviness, coherence):
    shards = lax.axis_size("len")
    my_index = lax.axis_index("len")
    local_members, local_len = phase_left.shape
    columns = 2 * local_members
    outer_block = OUTER // shards
    inner_block = INNER // shards

    def to_rows(part):
        shaped = part.reshape(2, local_members, inner_block, OUTER)
        return jnp.transpose(shaped, (2, 3, 0, 1)).reshape(
            inner_block, shards, outer_block * columns
        )

    inner_cos, inner_sin = dft_tables(INNER)
    freq = (my_index * local_len + lax.iota(jnp.int32, local_len)).astype(jnp.float32)[None, :]
    real_part, imag_part = spectra_of(phase_left, phase_right, roughness, waviness, coherence, freq)
    pieces = (
        lax.all_to_all(to_rows(real_part), "len", split_axis=1, concat_axis=0, tiled=True),
        lax.all_to_all(to_rows(imag_part), "len", split_axis=1, concat_axis=0, tiled=True),
    )
    real_in = pieces[0].reshape(INNER, -1)
    imag_in = pieces[1].reshape(INNER, -1)
    real_out = jnp.dot(inner_cos, real_in, precision=highest) - jnp.dot(
        inner_sin, imag_in, precision=highest
    )
    imag_out = jnp.dot(inner_cos, imag_in, precision=highest) + jnp.dot(
        inner_sin, real_in, precision=highest
    )
    row_index = lax.iota(jnp.int32, INNER)[:, None]
    outer_index = (my_index * outer_block + lax.iota(jnp.int32, outer_block))[None, :]
    twist = (row_index * outer_index % (OUTER * INNER)).astype(jnp.float32) * (
        2.0 * math.pi / (OUTER * INNER)
    )
    twist_cos = jnp.repeat(jnp.cos(twist), columns, axis=1)
    twist_sin = jnp.repeat(jnp.sin(twist), columns, axis=1)
    rot_real = (real_out * twist_cos - imag_out * twist_sin).reshape(
        shards, inner_block, outer_block * columns
    )
    rot_imag = (real_out * twist_sin + imag_out * twist_cos).reshape(
        shards, inner_block, outer_block * columns
    )
    outer_cos, outer_sin = dft_tables(OUTER)
    outer_cos = outer_cos.reshape(OUTER, shards, outer_block)
    outer_sin = outer_sin.reshape(OUTER, shards, outer_block)
    pieces = (
        lax.all_to_all(rot_real, "len", split_axis=0, concat_axis=0, tiled=True),
        lax.all_to_all(rot_imag, "len", split_axis=0, concat_axis=0, tiled=True),
    )
    item_count = pieces[0].shape[1]
    real_in = pieces[0].reshape(shards, item_count, outer_block, columns)
    imag_in = pieces[1].reshape(shards, item_count, outer_block, columns)
    first = jnp.einsum("jqa,qiac->cij", outer_cos, real_in, precision=highest)
    second = jnp.einsum("jqa,qiac->cij", outer_sin, imag_in, precision=highest)
    profile_block = first - second
    outgoing = jnp.transpose(
        profile_block.reshape(columns, inner_block, shards, outer_block), (2, 0, 1, 3)
    ).reshape(shards, -1)
    arrived = lax.all_to_all(outgoing, "len", split_axis=0, concat_axis=0, tiled=True)
    profile = jnp.transpose(
        arrived.reshape(shards, columns, inner_block, outer_block), (1, 3, 0, 2)
    ).reshape(2, local_members, local_len)
    scale = 1.0 / math.sqrt(2.0 * OUTER * INNER)
    snapshot = profile_block.reshape(2, local_members, inner_block * OUTER) * scale
    gathered = lax.all_gather(snapshot, "mem", axis=1, tiled=True)
    gram_local = gram_of(gathered)
    r_factor = merged(upper_of(gram_local), "len", combine_factors)
    return (profile, r_factor)


def host_cis(product, period):
    angle = product % period * (2.0 * np.pi / period)
    return np.cos(angle), np.sin(angle)


def split_host(table):
    coarse = table.astype(np.float32).astype(jnp.bfloat16)
    fine = (table - coarse.astype(np.float64)).astype(np.float32).astype(jnp.bfloat16)
    return np.stack([coarse, fine])


def outer_matrices():
    c, e, b = np.arange(QUARTER), np.arange(RADIX), np.arange(QUARTER)
    cos_part, sin_part = host_cis((RADIX * c[None, :, None] + e[:, None, None]) * b[None, None, :], OUTER)
    upper = np.concatenate([cos_part, -sin_part], axis=2)
    lower = np.concatenate([sin_part, cos_part], axis=2)
    return split_host(np.concatenate([upper, lower], axis=1))


def inner_matrices():
    c, e, b = np.arange(QUARTER), np.arange(RADIX), np.arange(QUARTER)
    cos_part, sin_part = host_cis((RADIX * c[None, :, None] + e[:, None, None]) * b[None, None, :], INNER)
    return split_host(np.concatenate([cos_part, -sin_part], axis=2))


def twist_tables():
    j1 = RADIX * np.arange(QUARTER)[None, :, None] + np.arange(RADIX)[:, None, None]
    cos_part, sin_part = host_cis(j1 * np.arange(INNER)[None, None, :], OUTER * INNER)
    return np.stack([cos_part, sin_part]).astype(np.float32)


def sin_cos(angle):
    square = angle * angle

    def series(coefficients):
        total = jnp.float32(coefficients[-1])
        for coefficient in coefficients[-2::-1]:
            total = total * square + jnp.float32(coefficient)
        return total

    half_sin = angle * series(SIN_HALF)
    half_cos = series(COS_HALF)
    twice = half_sin + half_sin
    return twice * half_cos, 1.0 - twice * half_sin


def amplitude_of(freq, scale, exponent):
    return scale * jnp.exp2(exponent * jnp.log2((freq + ANCHOR) * (1.0 / ANCHOR)))


def left_lines(left, freq, scale, exponent):
    amplitude = amplitude_of(freq, scale, exponent)
    sin_left, cos_left = sin_cos(left)
    return amplitude * cos_left, amplitude * sin_left


def radix_four(parts):
    (r0, i0), (r1, i1), (r2, i2), (r3, i3) = parts
    even_sum, even_gap = (r0 + r2, i0 + i2), (r0 - r2, i0 - i2)
    odd_sum, odd_gap = (r1 + r3, i1 + i3), (r1 - r3, i1 - i3)
    return (
        (even_sum[0] + odd_sum[0], even_sum[1] + odd_sum[1]),
        (even_gap[0] - odd_gap[1], even_gap[1] + odd_gap[0]),
        (even_sum[0] - odd_sum[0], even_sum[1] - odd_sum[1]),
        (even_gap[0] + odd_gap[1], even_gap[1] - odd_gap[0]),
    )


def store_split(coarse_ref, fine_ref, where, value):
    coarse = value.astype(jnp.bfloat16)
    coarse_ref[where] = coarse
    fine_ref[where] = (value - coarse.astype(jnp.float32)).astype(jnp.bfloat16)


def triple_dot(matrix_ref, e, coarse, fine, dims):
    def product(a, b):
        return lax.dot_general(a, b, (dims, ((), ())), preferred_element_type=jnp.float32)

    return product(matrix_ref[0, e], coarse) + (
        product(matrix_ref[0, e], fine) + product(matrix_ref[1, e], coarse)
    )


def first_lines(params_ref, left_ref, kept_refs, where, freq):
    scale, exponent, inverse_coherence = params_ref[0], params_ref[1], params_ref[2]
    amplitude = amplitude_of(freq, scale, exponent)
    freq_ratio = freq * inverse_coherence
    ratio_square = freq_ratio * freq_ratio
    coherent = 1.0 / (1.0 + ratio_square)
    incoherent = freq_ratio * jnp.sqrt(2.0 + ratio_square) * coherent
    sin_left, cos_left = sin_cos(left_ref[where])
    real, imag = amplitude * cos_left, amplitude * sin_left
    kept_refs[0][where] = coherent * real
    kept_refs[1][where] = coherent * imag
    kept_refs[2][where] = amplitude * incoherent
    return real, imag


def second_lines(right_ref, kept_refs, where):
    sin_right, cos_right = sin_cos(right_ref[where])
    independent = kept_refs[2][where]
    return (
        kept_refs[0][where] + independent * cos_right,
        kept_refs[1][where] + independent * sin_right,
    )


def outer_kernel(track, params_ref, phase_ref, *refs):
    if track == 0:
        matrix_ref, twist_ref, out_ref, *kept_refs, coarse_ref, fine_ref = refs
    else:
        *kept_refs, matrix_ref, twist_ref, out_ref, coarse_ref, fine_ref = refs
    _, tiles, rows, _ = phase_ref.shape
    lane = lax.broadcasted_iota(jnp.int32, (STEP, LANES), 1) + pl.program_id(0) * tiles * LANES
    row = lax.broadcasted_iota(jnp.int32, (STEP, LANES), 0)
    place = row * INNER + lane

    def some_rows(step, carry):
        b = step * STEP
        for tile in range(tiles):
            lines = []
            for a in range(RADIX):
                k1 = a * QUARTER + b
                where = (k1 // rows, tile, pl.ds(pl.multiple_of(k1 % rows, STEP), STEP))
                if track == 0:
                    freq = (place + (k1 * INNER + tile * LANES)).astype(jnp.float32)
                    lines.append(first_lines(params_ref, phase_ref, kept_refs, where, freq))
                else:
                    lines.append(second_lines(phase_ref, kept_refs, where))
            mixed = radix_four(lines)
            for e in range(RADIX):
                for ri in range(2):
                    at = pl.ds(pl.multiple_of(ri * QUARTER + b, STEP), STEP)
                    where = (e, at, pl.ds(tile * LANES, LANES))
                    store_split(coarse_ref, fine_ref, where, mixed[e][ri])
        return carry

    lax.fori_loop(0, QUARTER // STEP, some_rows, 0)
    for e in range(RADIX):
        mid = triple_dot(matrix_ref, e, coarse_ref[e], fine_ref[e], ((1,), (0,)))
        for tile in range(tiles):
            lanes = slice(tile * LANES, (tile + 1) * LANES)
            cos_part, sin_part = twist_ref[0, e, :, lanes], twist_ref[1, e, :, lanes]
            real, imag = mid[:QUARTER, lanes], mid[QUARTER:, lanes]
            out_ref[tile, 0, pl.ds(e, QUARTER, stride=RADIX), :] = real * cos_part - imag * sin_part
            out_ref[tile, 1, pl.ds(e, QUARTER, stride=RADIX), :] = real * sin_part + imag * cos_part


def inner_kernel(mid_ref, matrix_ref, *refs):
    out_refs, (coarse_ref, fine_ref) = refs[:-2], refs[-2:]
    wide = mid_ref.shape[2]
    shards, _, rows, _ = out_refs[0].shape

    def some_rows(step, carry):
        at = pl.multiple_of(step * STEP, STEP)
        for half in range(0, QUARTER, LANES):
            parts = [
                tuple(mid_ref[(a * QUARTER + half) // LANES, ri, pl.ds(at, STEP), :] for ri in range(2))
                for a in range(RADIX)
            ]
            mixed = radix_four(parts)
            for e in range(RADIX):
                for ri in range(2):
                    where = (e, pl.ds(at, STEP), pl.ds(ri * QUARTER + half, LANES))
                    store_split(coarse_ref, fine_ref, where, mixed[e][ri])
        return carry

    lax.fori_loop(0, wide // STEP, some_rows, 0)
    some = rows // RADIX
    for e in range(RADIX):
        value = triple_dot(matrix_ref, e, coarse_ref[e], fine_ref[e], ((1,), (1,)))
        for f in range(shards):
            for part, out_ref in enumerate(out_refs):
                at = (f * len(out_refs) + part) * some
                for tile in range(wide // LANES):
                    out_ref[f, tile, pl.ds(e, some, stride=RADIX), :] = value[
                        at : at + some, tile * LANES : (tile + 1) * LANES
                    ]


def part_kernel(in_ref, out_ref):
    members, tiles, rows, _ = out_ref.shape
    for tile in range(tiles):
        for start in range(0, rows, SUBLANES):
            columns = [((start + r) * tiles + tile) * LANES for r in range(SUBLANES)]
            turned = jnp.transpose(jnp.stack([in_ref[:, at : at + LANES] for at in columns]), (1, 0, 2))
            for m in range(members):
                out_ref[m, tile, start : start + SUBLANES, :] = turned[m]


def join_kernel(in_ref, *refs):
    join_rows(in_ref, refs[-1].at[0])


def join_rows(in_ref, out_ref):
    _, tiles, rows, _ = in_ref.shape
    for tile in range(tiles):
        for start in range(0, rows, SUBLANES):
            turned = jnp.transpose(in_ref[:, tile, start : start + SUBLANES, :], (1, 0, 2))
            for r in range(SUBLANES):
                at = ((start + r) * tiles + tile) * LANES
                out_ref[:, at : at + LANES] = turned[r]


def pieces_kernel(each, group_ref, in_ref, *out_refs):
    for n, out_ref in enumerate(out_refs):

        @pl.when(pl.program_id(0) // each == n)
        def _(out_ref=out_ref):
            join_rows(in_ref, out_ref)


def near_kernel(base_ref, own_ref, out_ref):
    members, length = own_ref.shape
    tiles = length // LANES - 1
    scale, exponent = tile_params(own_ref[:, tiles * LANES :])
    lane = lax.broadcasted_iota(jnp.int32, (members, LANES), 1)

    def one_tile(tile, carry):
        at = pl.ds(pl.multiple_of(tile * LANES, LANES), LANES)
        freq = (base_ref[0] + tile * LANES + lane).astype(jnp.float32)
        out_ref[0, :, at], out_ref[1, :, at] = left_lines(own_ref[:, at], freq, scale, exponent)
        return carry

    lax.fori_loop(0, tiles + 1, one_tile, 0)


def tile_params(beyond):
    return (jnp.broadcast_to(beyond[:, n : n + 1], beyond.shape) for n in (1, 2))


def mirror_kernel(base_ref, near_ref, far_ref, edge_ref, beyond_ref, out_ref):
    members, length = far_ref.shape
    tiles = length // LANES - 1
    shape = (members, LANES)
    lane = lax.broadcasted_iota(jnp.int32, shape, 1)
    mirror = (LANES - lane) % LANES
    first_group, last_group = base_ref[1] == 0, base_ref[1] == base_ref[2] - 1
    scale, exponent = tile_params(beyond_ref[...])
    half_root = math.sqrt(0.5)

    def tile_of(ref, tile):
        return ref[:, pl.ds(pl.multiple_of(tile * LANES, LANES), LANES)]

    def turned(value):
        return jnp.take_along_axis(value, mirror, axis=1, mode="promise_in_bounds")

    def store(tile, far, keep, weight):
        offset = base_ref[0] + tile * LANES + lane
        far_offset = jnp.where(offset == 0, 0, OUTER * INNER - offset)
        back = left_lines(far, far_offset.astype(jnp.float32), scale, exponent)
        at = pl.ds(pl.multiple_of(tile * LANES, LANES), LANES)
        real, imag = near_ref[0, :, at] + back[0], near_ref[1, :, at] - back[1]
        out_ref[0, :, at] = jnp.where(keep, real * weight, 0.0)
        out_ref[1, :, at] = jnp.where(keep, imag * weight, 0.0)

    def one_tile(tile, last):
        ahead = turned(tile_of(far_ref, tiles - 1 - tile))
        is_edge = (lane == 0) & (tile == 0) & first_group
        store(tile, jnp.where(lane == 0, last, ahead), lane >= 0, jnp.where(is_edge, half_root, 1.0))
        return ahead

    start = jnp.where(first_group, turned(edge_ref[...]), turned(tile_of(far_ref, tiles)))
    last = lax.fori_loop(0, tiles, one_tile, start)
    store(tiles, jnp.where(lane == 0, last, 0.0), (lane == 0) & last_group, half_root)


def limits():
    return pltpu.CompilerParams(vmem_limit_bytes=VMEM_LIMIT)


def part_call(phase):
    members, length = phase.shape
    rows = length // INNER
    tiles = INNER // LANES
    return pl.pallas_call(
        part_kernel,
        grid=(rows // BLOCK_ROWS,),
        in_specs=[pl.BlockSpec((members, BLOCK_ROWS * INNER), lambda g: (0, g))],
        out_specs=pl.BlockSpec((members, tiles, BLOCK_ROWS, LANES), lambda g: (0, 0, g, 0)),
        out_shape=pltpu.HBM((members, tiles, rows, LANES), jnp.float32),
        compiler_params=limits(),
        cost_estimate=pl.CostEstimate(flops=0, bytes_accessed=8 * members * length, transcendentals=0),
    )(pltpu.with_memory_space_constraint(phase, pltpu.HBM))


def join_call(piece, track, within, length, so_far):
    members, tiles, rows, _ = piece.shape
    steps = rows // BLOCK_ROWS
    piece = pltpu.with_memory_space_constraint(piece, pltpu.HBM)
    operands = (piece,) if so_far is None else (piece, so_far)
    return pl.pallas_call(
        join_kernel,
        grid=(steps,),
        in_specs=[
            pl.BlockSpec((members, tiles, BLOCK_ROWS, LANES), lambda g: (0, 0, g, 0)),
            pl.BlockSpec(memory_space=pl.ANY),
        ][: len(operands)],
        out_specs=pl.BlockSpec((1, members, BLOCK_ROWS * INNER), lambda g: (track, 0, within * steps + g)),
        out_shape=jax.ShapeDtypeStruct((2, members, length), jnp.float32),
        input_output_aliases={} if so_far is None else {1: 0},
        compiler_params=limits(),
        cost_estimate=pl.CostEstimate(flops=0, bytes_accessed=8 * members * rows * INNER, transcendentals=0),
    )(*operands)


def pieces_call(my_group, piece, groups):
    members, tiles, rows, _ = piece.shape
    each = rows // BLOCK_ROWS // groups

    def source(g, group_ref):
        slot = (groups - g // each) % groups
        return (0, 0, (slot ^ group_ref[0]) * each + g % each, 0)

    def place(n):
        return lambda g, group_ref: (0, jnp.clip(g - n * each, 0, each - 1))

    return pl.pallas_call(
        functools.partial(pieces_kernel, each),
        grid_spec=pltpu.PrefetchScalarGridSpec(
            num_scalar_prefetch=1,
            grid=(groups * each,),
            in_specs=[pl.BlockSpec((members, tiles, BLOCK_ROWS, LANES), source)],
            out_specs=[pl.BlockSpec((members, BLOCK_ROWS * INNER), place(n)) for n in range(groups)],
        ),
        out_shape=[pltpu.HBM((members, rows // groups * INNER), jnp.float32)] * groups,
        compiler_params=limits(),
        cost_estimate=pl.CostEstimate(flops=0, bytes_accessed=8 * members * rows * INNER, transcendentals=0),
    )(my_group.astype(jnp.int32).reshape(1), pltpu.with_memory_space_constraint(piece, pltpu.HBM))


def outer_call(params, phase, kept, matrices, twists):
    track = 1 if kept else 0
    sources, tiles, rows, _ = phase.shape
    some = OUTER_TILES
    lines = pl.BlockSpec((sources, some, rows, LANES), lambda g: (0, g, 0, 0))
    more = 0 if kept else 3
    return pl.pallas_call(
        functools.partial(outer_kernel, track),
        grid=(tiles // some,),
        in_specs=[pl.BlockSpec(memory_space=pltpu.SMEM)]
        + [lines] * (1 + len(kept))
        + [
            pl.BlockSpec(matrices.shape, lambda g: (0, 0, 0, 0)),
            pl.BlockSpec((2, RADIX, QUARTER, some * LANES), lambda g: (0, 0, 0, g)),
        ],
        out_specs=[pl.BlockSpec((some, 2, OUTER, LANES), lambda g: (g, 0, 0, 0))] + [lines] * more,
        out_shape=[jax.ShapeDtypeStruct((tiles, 2, OUTER, LANES), jnp.float32)]
        + [pltpu.HBM(phase.shape, jnp.float32)] * more,
        scratch_shapes=[pltpu.VMEM((RADIX, 2 * QUARTER, some * LANES), jnp.bfloat16)] * 2,
        compiler_params=limits(),
        cost_estimate=pl.CostEstimate(
            flops=24 * OUTER * QUARTER * INNER, bytes_accessed=32 * OUTER * INNER, transcendentals=0
        ),
    )(params, phase, *kept, matrices, twists)


def inner_call(mid, matrices, shards, parts):
    rows = INNER // shards // parts
    tiles = OUTER // LANES
    return pl.pallas_call(
        inner_kernel,
        grid=(OUTER // WIDE,),
        in_specs=[
            pl.BlockSpec((INNER // LANES, 2, WIDE, LANES), lambda g: (0, 0, g, 0)),
            pl.BlockSpec(matrices.shape, lambda g: (0, 0, 0, 0)),
        ],
        out_specs=[pl.BlockSpec((shards, WIDE // LANES, rows, LANES), lambda g: (0, g, 0, 0))] * parts,
        out_shape=[pltpu.HBM((shards, tiles, rows, LANES), jnp.float32)] * parts,
        scratch_shapes=[pltpu.VMEM((RADIX, WIDE, 2 * QUARTER), jnp.bfloat16)] * 2,
        compiler_params=limits(),
        cost_estimate=pl.CostEstimate(
            flops=12 * OUTER * QUARTER * INNER, bytes_accessed=12 * OUTER * INNER, transcendentals=0
        ),
    )(mid, matrices)


def near_call(base, own):
    members, length = own.shape
    return pl.pallas_call(
        near_kernel,
        in_specs=[pl.BlockSpec(memory_space=pltpu.SMEM), pl.BlockSpec(memory_space=pltpu.VMEM)],
        out_specs=pl.BlockSpec(memory_space=pltpu.VMEM),
        out_shape=jax.ShapeDtypeStruct((2, members, length), jnp.float32),
        compiler_params=limits(),
        cost_estimate=pl.CostEstimate(
            flops=100 * members * length, bytes_accessed=12 * members * length, transcendentals=0
        ),
    )(base, own)


def mirror_call(base, near, far, edge, beyond):
    members, length = far.shape
    return pl.pallas_call(
        mirror_kernel,
        in_specs=[pl.BlockSpec(memory_space=pltpu.SMEM)] + [pl.BlockSpec(memory_space=pltpu.VMEM)] * 4,
        out_specs=pl.BlockSpec(memory_space=pltpu.VMEM),
        out_shape=jax.ShapeDtypeStruct((2, members, length), jnp.float32),
        compiler_params=limits(),
        cost_estimate=pl.CostEstimate(
            flops=100 * members * length, bytes_accessed=20 * members * length, transcendentals=0
        ),
    )(base, near, far, edge, beyond)


def line_params(roughness, waviness, coherence):
    return jnp.stack(
        [jnp.sqrt(2.0 * roughness * (waviness - 1.0) / ANCHOR), -0.5 * waviness, 1.0 / coherence]
    )


def to_group(piece, slot):
    groups = lax.axis_size("mem")
    return lax.ppermute(piece, "mem", [(z, z ^ slot) for z in range(groups)]) if slot else piece


def rows_gram(rows):
    return lax.dot_general(rows, rows, (((1,), (1,)), ((), ())), precision=lax.Precision.HIGH)


def nearest_last(groups):
    return [(groups - n) % groups for n in range(groups)]


def own_and_far(phase, params, my_group):
    groups = lax.axis_size("mem")
    half = phase.shape[1] // 2
    width = half // groups
    lane = lax.broadcasted_iota(jnp.int32, (phase.shape[0], LANES), 1)

    def lines(start):
        return (
            lax.dynamic_slice_in_dim(phase, start, width, 1),
            lax.dynamic_slice_in_dim(phase, start + width, LANES, 1),
        )

    own, far = [], []
    for slot in nearest_last(groups):
        group = my_group ^ slot
        inner, beyond = lines(group * width)
        for n in range(2):
            beyond = jnp.where(lane == n + 1, params[n][:, None], beyond)
        far_inner, far_beyond = lines(half + (groups - 1 - group) * width)
        message = jnp.concatenate(
            [
                jnp.concatenate([inner, beyond], axis=1)[None],
                jnp.concatenate([far_inner, far_beyond], axis=1)[None],
            ]
        )
        message = to_group(message, slot)
        own.append(message[0])
        far.append(message[1])
    return jnp.concatenate(own, axis=0), jnp.concatenate(far, axis=0)


def edge_of(own):
    shards = lax.axis_size("len")
    return lax.ppermute(own[:, :LANES], "len", [(d, (shards - d) % shards) for d in range(shards)])


def across(far):
    shards = lax.axis_size("len")
    return lax.ppermute(far, "len", [(d, shards - 1 - d) for d in range(shards)])


def line_base(width):
    groups = lax.axis_size("mem")
    my_index, my_group = lax.axis_index("len"), lax.axis_index("mem")
    base = (my_index * (2 * groups) + my_group) * width
    return jnp.stack([base, my_group, jnp.full_like(my_group, groups)]).astype(jnp.int32)


def lines_gram(base, near, far, edge, beyond):
    sums = mirror_call(base, near, far, edge, beyond)
    return rows_gram(sums[0]) + rows_gram(sums[1])


def in_order(gram_matrix, members, slots):
    my_group = lax.axis_index("mem")
    row = lax.broadcasted_iota(jnp.int32, gram_matrix.shape, 0)
    column = lax.broadcasted_iota(jnp.int32, gram_matrix.shape, 1)
    to_slot = False
    for n, slot in enumerate(slots):
        to_slot = to_slot | (((row // members) ^ slot == my_group) & (column // members == n))
    to_slot = (to_slot & (row % members == column % members)).astype(jnp.float32)
    return jnp.dot(jnp.dot(to_slot, gram_matrix, precision=highest), to_slot.T, precision=highest)


def summed(value):
    for axis in ("len", "mem"):
        value = jnp.sum(lax.all_gather(value, axis), axis=0)
    return value


def per_device_whole(phase_left, phase_right, roughness, waviness, coherence):
    shards, groups = lax.axis_size("len"), lax.axis_size("mem")
    my_index = lax.axis_index("len")
    members = phase_left.shape[0]

    def swap(piece):
        return lax.all_to_all(piece, "len", split_axis=0, concat_axis=0, tiled=True)

    all_params = line_params(roughness, waviness, coherence)
    params = lax.dynamic_index_in_dim(all_params, my_index, 1, keepdims=False)
    outer_tables = jnp.asarray(outer_matrices())
    inner_tables = jnp.asarray(inner_matrices())
    twists = jnp.asarray(twist_tables())
    local_len = phase_left.shape[1]

    left, right = part_call(phase_left), part_call(phase_right)
    right, my_group = lax.optimization_barrier((right, lax.axis_index("mem")))
    left, right = lax.optimization_barrier((swap(left), right))
    right = swap(right)
    own, far = own_and_far(phase_left, all_params, my_group)
    mid, *kept = outer_call(params, left, (), outer_tables, twists)
    first = list(inner_call(mid, inner_tables, shards, 2))
    right, *first = lax.optimization_barrier((right, *first))
    early = swap(first[0])
    (mid,) = outer_call(params, right, kept, outer_tables, twists)
    (second,) = inner_call(mid, inner_tables, shards, 1)
    early, second = lax.optimization_barrier((early, second))
    base = line_base(own.shape[1] - LANES)
    near = near_call(base, own)
    second, near, far = lax.optimization_barrier((swap(second), near, far))
    pieces = pieces_call(lax.axis_index("mem"), second, groups)
    rows = [to_group(piece, slot) for slot, piece in zip(nearest_last(groups), pieces)]
    _, first[1], edge, far, second = lax.optimization_barrier((pieces, first[1], own, far, second))
    profile = join_call(second, 1, 0, local_len, None)
    line_gram = lines_gram(base, near, across(far), edge_of(edge), own[:, -LANES:])
    profile = join_call(early, 0, 0, local_len, profile)
    profile, first[1] = lax.optimization_barrier((profile, first[1]))
    late = swap(first[1])
    late, line_gram = lax.optimization_barrier((late, line_gram))
    profile = join_call(late, 0, 1, local_len, profile)
    profile, line_gram, rows = lax.optimization_barrier((profile, line_gram, rows))
    gram_matrix = 0.25 * line_gram + (0.5 / (OUTER * INNER)) * rows_gram(jnp.concatenate(rows, axis=0))
    return (profile, upper_of(summed(in_order(gram_matrix, members, nearest_last(groups)))))


def per_device(phase_left, phase_right, roughness, waviness, coherence):
    whole_members = phase_left.shape[0] == lax.axis_size("len") and lax.axis_size("mem") in (2, 4)
    form = per_device_whole if whole_members else per_device_spread
    return form(phase_left, phase_right, roughness, waviness, coherence)


def solution(mesh):
    placed = (P("mem", "len"), P("mem", "len"), P("mem"), P("mem"), P("mem"))
    return jax.shard_map(
        per_device,
        mesh=mesh,
        in_specs=placed,
        out_specs=(P(None, "mem", "len"), P()),
        check_vma=False,
    )
```

```python
import functools
import math

import jax
import jax.numpy as jnp
import numpy as np
from jax import lax
from jax.experimental import pallas as pl
from jax.experimental.pallas import tpu as pltpu
from jax.sharding import PartitionSpec as P

OUTER = 1024
INNER = 1024
ANCHOR = 64
RADIX = 4
QUARTER = 256
LANES = 128
STEP = 16
SUBLANES = 8
WIDE = 256
BLOCK_ROWS = 8
OUTER_TILES = 2
VMEM_LIMIT = 48 * 1024 * 1024
SIN_HALF = (0.49999999785787, -0.02083332246218, 2.604078316692e-4, -1.547581723527e-6, 5.088214043e-9)
COS_HALF = (
    0.99999999977982,
    -0.12499999839235,
    2.604164763023e-3,
    -2.170056380508e-5,
    9.67192778775e-8,
    -2.5440497557e-10,
)


highest = lax.Precision.HIGHEST


def merged(shard, axis, combine):
    everything = lax.all_gather(shard, axis)
    leading = everything[0]

    def step(k, so_far):
        return combine(so_far, everything[k])

    return lax.fori_loop(1, lax.axis_size(axis), step, leading)


def dft_tables(length):
    index = lax.iota(jnp.int32, length)
    product = index[:, None] * index[None, :] % length
    phase_angle = product.astype(jnp.float32) * (2.0 * math.pi / length)
    return (jnp.cos(phase_angle), jnp.sin(phase_angle))


def spectra_of(phase_left, phase_right, roughness, waviness, coherence, freq):
    amplitude = jnp.sqrt(2.0 * roughness * (waviness - 1.0) / ANCHOR)[:, None] * (
        (freq + ANCHOR) / ANCHOR
    ) ** (-0.5 * waviness[:, None])
    freq_ratio = freq / coherence[:, None]
    coherent = 1.0 / (1.0 + freq_ratio * freq_ratio)
    incoherent = freq_ratio * jnp.sqrt(2.0 + freq_ratio * freq_ratio) * coherent
    cos_left = jnp.cos(phase_left)
    sin_left = jnp.sin(phase_left)
    cos_right = jnp.cos(phase_right)
    sin_right = jnp.sin(phase_right)
    real_part = jnp.stack(
        [amplitude * cos_left, amplitude * (coherent * cos_left + incoherent * cos_right)]
    )
    imag_part = jnp.stack(
        [amplitude * sin_left, amplitude * (coherent * sin_left + incoherent * sin_right)]
    )
    return (real_part, imag_part)


def upper_of(gram_matrix):
    return jnp.linalg.cholesky(gram_matrix).T


def combine_factors(upper_a, upper_b):
    gram_matrix = jnp.dot(upper_a.T, upper_a, precision=highest) + jnp.dot(
        upper_b.T, upper_b, precision=highest
    )
    return upper_of(gram_matrix)


def gram_of(snapshot):
    return jnp.einsum("tmr,tnr->mn", snapshot, snapshot, precision=highest)


def per_device_spread(phase_left, phase_right, roughness, waviness, coherence):
    shards = lax.axis_size("len")
    my_index = lax.axis_index("len")
    local_members, local_len = phase_left.shape
    columns = 2 * local_members
    outer_block = OUTER // shards
    inner_block = INNER // shards

    def to_rows(part):
        shaped = part.reshape(2, local_members, inner_block, OUTER)
        return jnp.transpose(shaped, (2, 3, 0, 1)).reshape(
            inner_block, shards, outer_block * columns
        )

    inner_cos, inner_sin = dft_tables(INNER)
    freq = (my_index * local_len + lax.iota(jnp.int32, local_len)).astype(jnp.float32)[None, :]
    real_part, imag_part = spectra_of(phase_left, phase_right, roughness, waviness, coherence, freq)
    pieces = (
        lax.all_to_all(to_rows(real_part), "len", split_axis=1, concat_axis=0, tiled=True),
        lax.all_to_all(to_rows(imag_part), "len", split_axis=1, concat_axis=0, tiled=True),
    )
    real_in = pieces[0].reshape(INNER, -1)
    imag_in = pieces[1].reshape(INNER, -1)
    real_out = jnp.dot(inner_cos, real_in, precision=highest) - jnp.dot(
        inner_sin, imag_in, precision=highest
    )
    imag_out = jnp.dot(inner_cos, imag_in, precision=highest) + jnp.dot(
        inner_sin, real_in, precision=highest
    )
    row_index = lax.iota(jnp.int32, INNER)[:, None]
    outer_index = (my_index * outer_block + lax.iota(jnp.int32, outer_block))[None, :]
    twist = (row_index * outer_index % (OUTER * INNER)).astype(jnp.float32) * (
        2.0 * math.pi / (OUTER * INNER)
    )
    twist_cos = jnp.repeat(jnp.cos(twist), columns, axis=1)
    twist_sin = jnp.repeat(jnp.sin(twist), columns, axis=1)
    rot_real = (real_out * twist_cos - imag_out * twist_sin).reshape(
        shards, inner_block, outer_block * columns
    )
    rot_imag = (real_out * twist_sin + imag_out * twist_cos).reshape(
        shards, inner_block, outer_block * columns
    )
    outer_cos, outer_sin = dft_tables(OUTER)
    outer_cos = outer_cos.reshape(OUTER, shards, outer_block)
    outer_sin = outer_sin.reshape(OUTER, shards, outer_block)
    pieces = (
        lax.all_to_all(rot_real, "len", split_axis=0, concat_axis=0, tiled=True),
        lax.all_to_all(rot_imag, "len", split_axis=0, concat_axis=0, tiled=True),
    )
    item_count = pieces[0].shape[1]
    real_in = pieces[0].reshape(shards, item_count, outer_block, columns)
    imag_in = pieces[1].reshape(shards, item_count, outer_block, columns)
    first = jnp.einsum("jqa,qiac->cij", outer_cos, real_in, precision=highest)
    second = jnp.einsum("jqa,qiac->cij", outer_sin, imag_in, precision=highest)
    profile_block = first - second
    outgoing = jnp.transpose(
        profile_block.reshape(columns, inner_block, shards, outer_block), (2, 0, 1, 3)
    ).reshape(shards, -1)
    arrived = lax.all_to_all(outgoing, "len", split_axis=0, concat_axis=0, tiled=True)
    profile = jnp.transpose(
        arrived.reshape(shards, columns, inner_block, outer_block), (1, 3, 0, 2)
    ).reshape(2, local_members, local_len)
    scale = 1.0 / math.sqrt(2.0 * OUTER * INNER)
    snapshot = profile_block.reshape(2, local_members, inner_block * OUTER) * scale
    gathered = lax.all_gather(snapshot, "mem", axis=1, tiled=True)
    gram_local = gram_of(gathered)
    r_factor = merged(upper_of(gram_local), "len", combine_factors)
    return (profile, r_factor)


def host_cis(product, period):
    angle = product % period * (2.0 * np.pi / period)
    return np.cos(angle), np.sin(angle)


def split_host(table):
    coarse = table.astype(np.float32).astype(jnp.bfloat16)
    fine = (table - coarse.astype(np.float64)).astype(np.float32).astype(jnp.bfloat16)
    return np.stack([coarse, fine])


def outer_matrices():
    c, e, b = np.arange(QUARTER), np.arange(RADIX), np.arange(QUARTER)
    cos_part, sin_part = host_cis((RADIX * c[None, :, None] + e[:, None, None]) * b[None, None, :], OUTER)
    upper = np.concatenate([cos_part, -sin_part], axis=2)
    lower = np.concatenate([sin_part, cos_part], axis=2)
    return split_host(np.concatenate([upper, lower], axis=1))


def inner_matrices():
    c, e, b = np.arange(QUARTER), np.arange(RADIX), np.arange(QUARTER)
    cos_part, sin_part = host_cis((RADIX * c[None, :, None] + e[:, None, None]) * b[None, None, :], INNER)
    return split_host(np.concatenate([cos_part, -sin_part], axis=2))


def twist_tables():
    j1 = RADIX * np.arange(QUARTER)[None, :, None] + np.arange(RADIX)[:, None, None]
    cos_part, sin_part = host_cis(j1 * np.arange(INNER)[None, None, :], OUTER * INNER)
    return np.stack([cos_part, sin_part]).astype(np.float32)


def sin_cos(angle):
    square = angle * angle

    def series(coefficients):
        total = jnp.float32(coefficients[-1])
        for coefficient in coefficients[-2::-1]:
            total = total * square + jnp.float32(coefficient)
        return total

    half_sin = angle * series(SIN_HALF)
    half_cos = series(COS_HALF)
    twice = half_sin + half_sin
    return twice * half_cos, 1.0 - twice * half_sin


def amplitude_of(freq, scale, exponent):
    return scale * jnp.exp2(exponent * jnp.log2((freq + ANCHOR) * (1.0 / ANCHOR)))


def left_lines(left, freq, scale, exponent):
    amplitude = amplitude_of(freq, scale, exponent)
    sin_left, cos_left = sin_cos(left)
    return amplitude * cos_left, amplitude * sin_left


def radix_four(parts):
    (r0, i0), (r1, i1), (r2, i2), (r3, i3) = parts
    even_sum, even_gap = (r0 + r2, i0 + i2), (r0 - r2, i0 - i2)
    odd_sum, odd_gap = (r1 + r3, i1 + i3), (r1 - r3, i1 - i3)
    return (
        (even_sum[0] + odd_sum[0], even_sum[1] + odd_sum[1]),
        (even_gap[0] - odd_gap[1], even_gap[1] + odd_gap[0]),
        (even_sum[0] - odd_sum[0], even_sum[1] - odd_sum[1]),
        (even_gap[0] + odd_gap[1], even_gap[1] - odd_gap[0]),
    )


def store_split(coarse_ref, fine_ref, where, value):
    coarse = value.astype(jnp.bfloat16)
    coarse_ref[where] = coarse
    fine_ref[where] = (value - coarse.astype(jnp.float32)).astype(jnp.bfloat16)


def triple_dot(matrix_ref, e, coarse, fine, dims):
    def product(a, b):
        return lax.dot_general(a, b, (dims, ((), ())), preferred_element_type=jnp.float32)

    return product(matrix_ref[0, e], coarse) + (
        product(matrix_ref[0, e], fine) + product(matrix_ref[1, e], coarse)
    )


def first_lines(params_ref, left_ref, kept_refs, where, freq):
    scale, exponent, inverse_coherence = params_ref[0], params_ref[1], params_ref[2]
    amplitude = amplitude_of(freq, scale, exponent)
    freq_ratio = freq * inverse_coherence
    ratio_square = freq_ratio * freq_ratio
    coherent = 1.0 / (1.0 + ratio_square)
    incoherent = freq_ratio * jnp.sqrt(2.0 + ratio_square) * coherent
    sin_left, cos_left = sin_cos(left_ref[where])
    real, imag = amplitude * cos_left, amplitude * sin_left
    kept_refs[0][where] = coherent * real
    kept_refs[1][where] = coherent * imag
    kept_refs[2][where] = amplitude * incoherent
    return real, imag


def second_lines(right_ref, kept_refs, where):
    sin_right, cos_right = sin_cos(right_ref[where])
    independent = kept_refs[2][where]
    return (
        kept_refs[0][where] + independent * cos_right,
        kept_refs[1][where] + independent * sin_right,
    )


def outer_kernel(track, params_ref, phase_ref, *refs):
    if track == 0:
        matrix_ref, twist_ref, out_ref, *kept_refs, coarse_ref, fine_ref = refs
    else:
        *kept_refs, matrix_ref, twist_ref, out_ref, coarse_ref, fine_ref = refs
    _, tiles, rows, _ = phase_ref.shape
    lane = lax.broadcasted_iota(jnp.int32, (STEP, LANES), 1) + pl.program_id(0) * tiles * LANES
    row = lax.broadcasted_iota(jnp.int32, (STEP, LANES), 0)
    place = row * INNER + lane

    def some_rows(step, carry):
        b = step * STEP
        for tile in range(tiles):
            lines = []
            for a in range(RADIX):
                k1 = a * QUARTER + b
                where = (k1 // rows, tile, pl.ds(pl.multiple_of(k1 % rows, STEP), STEP))
                if track == 0:
                    freq = (place + (k1 * INNER + tile * LANES)).astype(jnp.float32)
                    lines.append(first_lines(params_ref, phase_ref, kept_refs, where, freq))
                else:
                    lines.append(second_lines(phase_ref, kept_refs, where))
            mixed = radix_four(lines)
            for e in range(RADIX):
                for ri in range(2):
                    at = pl.ds(pl.multiple_of(ri * QUARTER + b, STEP), STEP)
                    where = (e, at, pl.ds(tile * LANES, LANES))
                    store_split(coarse_ref, fine_ref, where, mixed[e][ri])
        return carry

    lax.fori_loop(0, QUARTER // STEP, some_rows, 0)
    for e in range(RADIX):
        mid = triple_dot(matrix_ref, e, coarse_ref[e], fine_ref[e], ((1,), (0,)))
        for tile in range(tiles):
            lanes = slice(tile * LANES, (tile + 1) * LANES)
            cos_part, sin_part = twist_ref[0, e, :, lanes], twist_ref[1, e, :, lanes]
            real, imag = mid[:QUARTER, lanes], mid[QUARTER:, lanes]
            out_ref[tile, 0, pl.ds(e, QUARTER, stride=RADIX), :] = real * cos_part - imag * sin_part
            out_ref[tile, 1, pl.ds(e, QUARTER, stride=RADIX), :] = real * sin_part + imag * cos_part


def inner_kernel(mid_ref, matrix_ref, *refs):
    out_refs, (coarse_ref, fine_ref) = refs[:-2], refs[-2:]
    wide = mid_ref.shape[2]
    shards, _, rows, _ = out_refs[0].shape

    def some_rows(step, carry):
        at = pl.multiple_of(step * STEP, STEP)
        for half in range(0, QUARTER, LANES):
            parts = [
                tuple(mid_ref[(a * QUARTER + half) // LANES, ri, pl.ds(at, STEP), :] for ri in range(2))
                for a in range(RADIX)
            ]
            mixed = radix_four(parts)
            for e in range(RADIX):
                for ri in range(2):
                    where = (e, pl.ds(at, STEP), pl.ds(ri * QUARTER + half, LANES))
                    store_split(coarse_ref, fine_ref, where, mixed[e][ri])
        return carry

    lax.fori_loop(0, wide // STEP, some_rows, 0)
    some = rows // RADIX
    for e in range(RADIX):
        value = triple_dot(matrix_ref, e, coarse_ref[e], fine_ref[e], ((1,), (1,)))
        for f in range(shards):
            for part, out_ref in enumerate(out_refs):
                at = (f * len(out_refs) + part) * some
                for tile in range(wide // LANES):
                    out_ref[f, tile, pl.ds(e, some, stride=RADIX), :] = value[
                        at : at + some, tile * LANES : (tile + 1) * LANES
                    ]


def part_kernel(in_ref, out_ref):
    members, tiles, rows, _ = out_ref.shape
    for tile in range(tiles):
        for start in range(0, rows, SUBLANES):
            columns = [((start + r) * tiles + tile) * LANES for r in range(SUBLANES)]
            turned = jnp.transpose(jnp.stack([in_ref[:, at : at + LANES] for at in columns]), (1, 0, 2))
            for m in range(members):
                out_ref[m, tile, start : start + SUBLANES, :] = turned[m]


def join_kernel(in_ref, *refs):
    join_rows(in_ref, refs[-1].at[0])


def join_rows(in_ref, out_ref):
    _, tiles, rows, _ = in_ref.shape
    for tile in range(tiles):
        for start in range(0, rows, SUBLANES):
            turned = jnp.transpose(in_ref[:, tile, start : start + SUBLANES, :], (1, 0, 2))
            for r in range(SUBLANES):
                at = ((start + r) * tiles + tile) * LANES
                out_ref[:, at : at + LANES] = turned[r]


def pieces_kernel(each, group_ref, in_ref, *out_refs):
    for n, out_ref in enumerate(out_refs):

        @pl.when(pl.program_id(0) // each == n)
        def _(out_ref=out_ref):
            join_rows(in_ref, out_ref)


def near_kernel(base_ref, own_ref, out_ref):
    members, length = own_ref.shape
    tiles = length // LANES - 1
    scale, exponent = tile_params(own_ref[:, tiles * LANES :])
    lane = lax.broadcasted_iota(jnp.int32, (members, LANES), 1)

    def one_tile(tile, carry):
        at = pl.ds(pl.multiple_of(tile * LANES, LANES), LANES)
        freq = (base_ref[0] + tile * LANES + lane).astype(jnp.float32)
        out_ref[0, :, at], out_ref[1, :, at] = left_lines(own_ref[:, at], freq, scale, exponent)
        return carry

    lax.fori_loop(0, tiles + 1, one_tile, 0)


def tile_params(beyond):
    return (jnp.broadcast_to(beyond[:, n : n + 1], beyond.shape) for n in (1, 2))


def mirror_kernel(base_ref, near_ref, far_ref, edge_ref, beyond_ref, out_ref):
    members, length = far_ref.shape
    tiles = length // LANES - 1
    shape = (members, LANES)
    lane = lax.broadcasted_iota(jnp.int32, shape, 1)
    mirror = (LANES - lane) % LANES
    first_group, last_group = base_ref[1] == 0, base_ref[1] == base_ref[2] - 1
    scale, exponent = tile_params(beyond_ref[...])
    half_root = math.sqrt(0.5)

    def tile_of(ref, tile):
        return ref[:, pl.ds(pl.multiple_of(tile * LANES, LANES), LANES)]

    def turned(value):
        return jnp.take_along_axis(value, mirror, axis=1, mode="promise_in_bounds")

    def store(tile, far, keep, weight):
        offset = base_ref[0] + tile * LANES + lane
        far_offset = jnp.where(offset == 0, 0, OUTER * INNER - offset)
        back = left_lines(far, far_offset.astype(jnp.float32), scale, exponent)
        at = pl.ds(pl.multiple_of(tile * LANES, LANES), LANES)
        real, imag = near_ref[0, :, at] + back[0], near_ref[1, :, at] - back[1]
        out_ref[0, :, at] = jnp.where(keep, real * weight, 0.0)
        out_ref[1, :, at] = jnp.where(keep, imag * weight, 0.0)

    def one_tile(tile, last):
        ahead = turned(tile_of(far_ref, tiles - 1 - tile))
        is_edge = (lane == 0) & (tile == 0) & first_group
        store(tile, jnp.where(lane == 0, last, ahead), lane >= 0, jnp.where(is_edge, half_root, 1.0))
        return ahead

    start = jnp.where(first_group, turned(edge_ref[...]), turned(tile_of(far_ref, tiles)))
    last = lax.fori_loop(0, tiles, one_tile, start)
    store(tiles, jnp.where(lane == 0, last, 0.0), (lane == 0) & last_group, half_root)


def limits():
    return pltpu.CompilerParams(vmem_limit_bytes=VMEM_LIMIT)


def part_call(phase):
    members, length = phase.shape
    rows = length // INNER
    tiles = INNER // LANES
    return pl.pallas_call(
        part_kernel,
        grid=(rows // BLOCK_ROWS,),
        in_specs=[pl.BlockSpec((members, BLOCK_ROWS * INNER), lambda g: (0, g))],
        out_specs=pl.BlockSpec((members, tiles, BLOCK_ROWS, LANES), lambda g: (0, 0, g, 0)),
        out_shape=pltpu.HBM((members, tiles, rows, LANES), jnp.float32),
        compiler_params=limits(),
        cost_estimate=pl.CostEstimate(flops=0, bytes_accessed=8 * members * length, transcendentals=0),
    )(pltpu.with_memory_space_constraint(phase, pltpu.HBM))


def join_call(piece, track, within, length, so_far):
    members, tiles, rows, _ = piece.shape
    steps = rows // BLOCK_ROWS
    piece = pltpu.with_memory_space_constraint(piece, pltpu.HBM)
    operands = (piece,) if so_far is None else (piece, so_far)
    return pl.pallas_call(
        join_kernel,
        grid=(steps,),
        in_specs=[
            pl.BlockSpec((members, tiles, BLOCK_ROWS, LANES), lambda g: (0, 0, g, 0)),
            pl.BlockSpec(memory_space=pl.ANY),
        ][: len(operands)],
        out_specs=pl.BlockSpec((1, members, BLOCK_ROWS * INNER), lambda g: (track, 0, within * steps + g)),
        out_shape=jax.ShapeDtypeStruct((2, members, length), jnp.float32),
        input_output_aliases={} if so_far is None else {1: 0},
        compiler_params=limits(),
        cost_estimate=pl.CostEstimate(flops=0, bytes_accessed=8 * members * rows * INNER, transcendentals=0),
    )(*operands)


def pieces_call(my_group, piece, groups):
    members, tiles, rows, _ = piece.shape
    each = rows // BLOCK_ROWS // groups

    def source(g, group_ref):
        slot = (groups - g // each) % groups
        return (0, 0, (slot ^ group_ref[0]) * each + g % each, 0)

    def place(n):
        return lambda g, group_ref: (0, jnp.clip(g - n * each, 0, each - 1))

    return pl.pallas_call(
        functools.partial(pieces_kernel, each),
        grid_spec=pltpu.PrefetchScalarGridSpec(
            num_scalar_prefetch=1,
            grid=(groups * each,),
            in_specs=[pl.BlockSpec((members, tiles, BLOCK_ROWS, LANES), source)],
            out_specs=[pl.BlockSpec((members, BLOCK_ROWS * INNER), place(n)) for n in range(groups)],
        ),
        out_shape=[pltpu.HBM((members, rows // groups * INNER), jnp.float32)] * groups,
        compiler_params=limits(),
        cost_estimate=pl.CostEstimate(flops=0, bytes_accessed=8 * members * rows * INNER, transcendentals=0),
    )(my_group.astype(jnp.int32).reshape(1), pltpu.with_memory_space_constraint(piece, pltpu.HBM))


def outer_call(params, phase, kept, matrices, twists):
    track = 1 if kept else 0
    sources, tiles, rows, _ = phase.shape
    some = OUTER_TILES
    lines = pl.BlockSpec((sources, some, rows, LANES), lambda g: (0, g, 0, 0))
    more = 0 if kept else 3
    return pl.pallas_call(
        functools.partial(outer_kernel, track),
        grid=(tiles // some,),
        in_specs=[pl.BlockSpec(memory_space=pltpu.SMEM)]
        + [lines] * (1 + len(kept))
        + [
            pl.BlockSpec(matrices.shape, lambda g: (0, 0, 0, 0)),
            pl.BlockSpec((2, RADIX, QUARTER, some * LANES), lambda g: (0, 0, 0, g)),
        ],
        out_specs=[pl.BlockSpec((some, 2, OUTER, LANES), lambda g: (g, 0, 0, 0))] + [lines] * more,
        out_shape=[jax.ShapeDtypeStruct((tiles, 2, OUTER, LANES), jnp.float32)]
        + [pltpu.HBM(phase.shape, jnp.float32)] * more,
        scratch_shapes=[pltpu.VMEM((RADIX, 2 * QUARTER, some * LANES), jnp.bfloat16)] * 2,
        compiler_params=limits(),
        cost_estimate=pl.CostEstimate(
            flops=24 * OUTER * QUARTER * INNER, bytes_accessed=32 * OUTER * INNER, transcendentals=0
        ),
    )(params, phase, *kept, matrices, twists)


def inner_call(mid, matrices, shards, parts):
    rows = INNER // shards // parts
    tiles = OUTER // LANES
    return pl.pallas_call(
        inner_kernel,
        grid=(OUTER // WIDE,),
        in_specs=[
            pl.BlockSpec((INNER // LANES, 2, WIDE, LANES), lambda g: (0, 0, g, 0)),
            pl.BlockSpec(matrices.shape, lambda g: (0, 0, 0, 0)),
        ],
        out_specs=[pl.BlockSpec((shards, WIDE // LANES, rows, LANES), lambda g: (0, g, 0, 0))] * parts,
        out_shape=[pltpu.HBM((shards, tiles, rows, LANES), jnp.float32)] * parts,
        scratch_shapes=[pltpu.VMEM((RADIX, WIDE, 2 * QUARTER), jnp.bfloat16)] * 2,
        compiler_params=limits(),
        cost_estimate=pl.CostEstimate(
            flops=12 * OUTER * QUARTER * INNER, bytes_accessed=12 * OUTER * INNER, transcendentals=0
        ),
    )(mid, matrices)


def near_call(base, own):
    members, length = own.shape
    return pl.pallas_call(
        near_kernel,
        in_specs=[pl.BlockSpec(memory_space=pltpu.SMEM), pl.BlockSpec(memory_space=pltpu.VMEM)],
        out_specs=pl.BlockSpec(memory_space=pltpu.VMEM),
        out_shape=jax.ShapeDtypeStruct((2, members, length), jnp.float32),
        compiler_params=limits(),
        cost_estimate=pl.CostEstimate(
            flops=100 * members * length, bytes_accessed=12 * members * length, transcendentals=0
        ),
    )(base, own)


def mirror_call(base, near, far, edge, beyond):
    members, length = far.shape
    return pl.pallas_call(
        mirror_kernel,
        in_specs=[pl.BlockSpec(memory_space=pltpu.SMEM)] + [pl.BlockSpec(memory_space=pltpu.VMEM)] * 4,
        out_specs=pl.BlockSpec(memory_space=pltpu.VMEM),
        out_shape=jax.ShapeDtypeStruct((2, members, length), jnp.float32),
        compiler_params=limits(),
        cost_estimate=pl.CostEstimate(
            flops=100 * members * length, bytes_accessed=20 * members * length, transcendentals=0
        ),
    )(base, near, far, edge, beyond)


def line_params(roughness, waviness, coherence):
    return jnp.stack(
        [jnp.sqrt(2.0 * roughness * (waviness - 1.0) / ANCHOR), -0.5 * waviness, 1.0 / coherence]
    )


def to_group(piece, slot):
    groups = lax.axis_size("mem")
    return lax.ppermute(piece, "mem", [(z, z ^ slot) for z in range(groups)]) if slot else piece


def rows_gram(rows):
    return lax.dot_general(rows, rows, (((1,), (1,)), ((), ())), precision=lax.Precision.HIGH)


def nearest_last(groups):
    return [(groups - n) % groups for n in range(groups)]


def own_and_far(phase, params, my_group):
    groups = lax.axis_size("mem")
    half = phase.shape[1] // 2
    width = half // groups
    lane = lax.broadcasted_iota(jnp.int32, (phase.shape[0], LANES), 1)

    def lines(start):
        return (
            lax.dynamic_slice_in_dim(phase, start, width, 1),
            lax.dynamic_slice_in_dim(phase, start + width, LANES, 1),
        )

    own, far = [], []
    for slot in nearest_last(groups):
        group = my_group ^ slot
        inner, beyond = lines(group * width)
        for n in range(2):
            beyond = jnp.where(lane == n + 1, params[n][:, None], beyond)
        far_inner, far_beyond = lines(half + (groups - 1 - group) * width)
        message = jnp.concatenate(
            [
                jnp.concatenate([inner, beyond], axis=1)[None],
                jnp.concatenate([far_inner, far_beyond], axis=1)[None],
            ]
        )
        message = to_group(message, slot)
        own.append(message[0])
        far.append(message[1])
    return jnp.concatenate(own, axis=0), jnp.concatenate(far, axis=0)


def edge_of(own):
    shards = lax.axis_size("len")
    return lax.ppermute(own[:, :LANES], "len", [(d, (shards - d) % shards) for d in range(shards)])


def across(far):
    shards = lax.axis_size("len")
    return lax.ppermute(far, "len", [(d, shards - 1 - d) for d in range(shards)])


def line_base(width):
    groups = lax.axis_size("mem")
    my_index, my_group = lax.axis_index("len"), lax.axis_index("mem")
    base = (my_index * (2 * groups) + my_group) * width
    return jnp.stack([base, my_group, jnp.full_like(my_group, groups)]).astype(jnp.int32)


def lines_gram(base, near, far, edge, beyond):
    sums = mirror_call(base, near, far, edge, beyond)
    return rows_gram(sums[0]) + rows_gram(sums[1])


def in_order(gram_matrix, members, slots):
    my_group = lax.axis_index("mem")
    row = lax.broadcasted_iota(jnp.int32, gram_matrix.shape, 0)
    column = lax.broadcasted_iota(jnp.int32, gram_matrix.shape, 1)
    to_slot = False
    for n, slot in enumerate(slots):
        to_slot = to_slot | (((row // members) ^ slot == my_group) & (column // members == n))
    to_slot = (to_slot & (row % members == column % members)).astype(jnp.float32)
    return jnp.dot(jnp.dot(to_slot, gram_matrix, precision=highest), to_slot.T, precision=highest)


def summed(value):
    for axis in ("len", "mem"):
        value = jnp.sum(lax.all_gather(value, axis), axis=0)
    return value


def per_device_whole(phase_left, phase_right, roughness, waviness, coherence):
    shards, groups = lax.axis_size("len"), lax.axis_size("mem")
    my_index = lax.axis_index("len")
    members = phase_left.shape[0]

    def swap(piece):
        return lax.all_to_all(piece, "len", split_axis=0, concat_axis=0, tiled=True)

    all_params = line_params(roughness, waviness, coherence)
    params = lax.dynamic_index_in_dim(all_params, my_index, 1, keepdims=False)
    outer_tables = jnp.asarray(outer_matrices())
    inner_tables = jnp.asarray(inner_matrices())
    twists = jnp.asarray(twist_tables())
    local_len = phase_left.shape[1]

    left, right = part_call(phase_left), part_call(phase_right)
    right, my_group = lax.optimization_barrier((right, lax.axis_index("mem")))
    left, right = lax.optimization_barrier((swap(left), right))
    right = swap(right)
    own, far = own_and_far(phase_left, all_params, my_group)
    mid, *kept = outer_call(params, left, (), outer_tables, twists)
    first = list(inner_call(mid, inner_tables, shards, 2))
    right, *first = lax.optimization_barrier((right, *first))
    early = swap(first[0])
    (mid,) = outer_call(params, right, kept, outer_tables, twists)
    (second,) = inner_call(mid, inner_tables, shards, 1)
    early, second = lax.optimization_barrier((early, second))
    base = line_base(own.shape[1] - LANES)
    near = near_call(base, own)
    second, near, far = lax.optimization_barrier((swap(second), near, far))
    pieces = pieces_call(lax.axis_index("mem"), second, groups)
    rows = [to_group(piece, slot) for slot, piece in zip(nearest_last(groups), pieces)]
    _, first[1], edge, far, second = lax.optimization_barrier((pieces, first[1], own, far, second))
    profile = join_call(second, 1, 0, local_len, None)
    late = swap(first[1])
    line_gram = lines_gram(base, near, across(far), edge_of(edge), own[:, -LANES:])
    profile = join_call(early, 0, 0, local_len, profile)
    late, line_gram = lax.optimization_barrier((late, line_gram))
    profile = join_call(late, 0, 1, local_len, profile)
    profile, line_gram, rows = lax.optimization_barrier((profile, line_gram, rows))
    gram_matrix = 0.25 * line_gram + (0.5 / (OUTER * INNER)) * rows_gram(jnp.concatenate(rows, axis=0))
    return (profile, upper_of(summed(in_order(gram_matrix, members, nearest_last(groups)))))


def per_device(phase_left, phase_right, roughness, waviness, coherence):
    whole_members = phase_left.shape[0] == lax.axis_size("len") and lax.axis_size("mem") in (2, 4)
    form = per_device_whole if whole_members else per_device_spread
    return form(phase_left, phase_right, roughness, waviness, coherence)


def solution(mesh):
    placed = (P("mem", "len"), P("mem", "len"), P("mem"), P("mem"), P("mem"))
    return jax.shard_map(
        per_device,
        mesh=mesh,
        in_specs=placed,
        out_specs=(P(None, "mem", "len"), P()),
        check_vma=False,
    )
```
